512 devices in a mesh: dp: 64 (over x, z, core), fsdp: 8 (over y).
Axes of the slice: x: 4, y: 8, z: 8, core: 2. Of those that a mesh axis runs over, the one named last changes fastest.
Arguments:
- queries: bfloat16 [8, 8192, 4096], P('fsdp', 'dp'), may hold values from -180 to 180
- key_rows: bfloat16 [8, 8192, 512], P('fsdp', 'dp'), may hold values from -8 to 8
- out_grad: bfloat16 [8, 8192, 4096], P('fsdp', 'dp'), may hold values from -6 to 6
- inputs: bfloat16 [8, 8192, 4096], P('fsdp', 'dp'), may hold values from -6 to 6
- w_value: bfloat16 [4096, 512], P('fsdp'), may hold values from -0.09375 to 0.09375
- doc_pos: int32 [8, 8192], P('fsdp', 'dp'), may hold values from 0 to 384, as said below
Outputs:
- key_grad: bfloat16 [8, 8192, 512], P('fsdp', 'dp')
- weight_grad: bfloat16 [4096, 512], P('fsdp')
The draws below stay inside these ranges and needn't reach their ends.
Inputs may be any that keep to these rules, and one draw needn't show every extreme that they name: `doc_pos`: documents are contiguous runs 0, 1, 2, ... within a sequence, each of at most 385 tokens; every sequence starts a document at its first token, and in every sequence one document has exactly 385 tokens.
All inputs are finite; a program needn't handle non-finite values.
Results may differ from the reference program's by a relative error of at most 0.02.
Values may be sent and summed in bfloat16 or wider, within the bound.
No kernel may reach another device: no remote copies, remote signals or barrier semaphores. Data moves between devices by JAX's collectives and lax.ppermute only.
A program may use at most 64 MiB of HBM per device.

```python
import math
import jax
import jax.numpy as jnp
from jax import lax

D = 4096
KEY_HEADS = 4
GROUP_WIDTH = 8
HEAD_SIZE = 128
SPAN = 3
TOK_DEV = 128
PACKED_SEQUENCES = 8
SEQUENCE_LENGTH = 8192
DOC_MAX = 385
QUERY_COLUMNS = 4096
KW = 512
N_DP = 64


def shared_draw(key):
    key_start_row = jnp.clip(jax.random.normal(jax.random.fold_in(key, 5), (PACKED_SEQUENCES, SEQUENCE_LENGTH, KW), jnp.float32), -6.0, 6.0)
    return key_start_row


def draw_key_rows(key, part):
    key_start_row = shared_draw(key)
    return key_start_row.astype(jnp.bfloat16)


def draw_queries(key, part):
    key = jax.random.fold_in(key, 9)
    query_base = jax.random.normal(jax.random.fold_in(key, 1), (PACKED_SEQUENCES, SEQUENCE_LENGTH, QUERY_COLUMNS), jnp.float32)
    return query_base.astype(jnp.bfloat16)


def draw_doc_pos(key, part):
    key = jax.random.fold_in(key, 11)
    length_key, long_key = jax.random.split(key)
    lengths = jax.random.randint(length_key, (PACKED_SEQUENCES, SEQUENCE_LENGTH), 1, DOC_MAX + 1, dtype=jnp.int32)
    long_doc = jax.random.randint(long_key, (PACKED_SEQUENCES, 1), 0, max(SEQUENCE_LENGTH // (2 * DOC_MAX), 1), dtype=jnp.int32)
    position = jnp.arange(SEQUENCE_LENGTH, dtype=jnp.int32)[None, :]
    lengths = jnp.where(position == long_doc, DOC_MAX, lengths).astype(jnp.int32)
    doc_ends = jnp.cumsum(lengths, axis=1).astype(jnp.int32)
    doc_starts = doc_ends - lengths
    targets = jnp.arange(SEQUENCE_LENGTH, dtype=jnp.int32)
    doc_index = jax.vmap(partial_search)(doc_ends, jnp.broadcast_to(targets, (PACKED_SEQUENCES, SEQUENCE_LENGTH)))
    start_of = jnp.take_along_axis(doc_starts, doc_index.astype(jnp.int32), axis=1)
    return (position - start_of).astype(jnp.int32)


def partial_search(doc_ends, targets):
    return jnp.searchsorted(doc_ends, targets, side='right').astype(jnp.int32)


def level_of(own_key, shape, shards, smallest, top_value):
    factor_of = 1.0
    for dim, shards_of in shards:
        heights = jax.random.uniform(jax.random.fold_in(jax.random.fold_in(own_key, 6), dim), (shards_of,), jnp.float32, smallest / len(shards), top_value / len(shards))
        factor_of = factor_of * jnp.repeat(jnp.exp(heights), shape[dim] // shards_of).reshape((-1,) + (1,) * (len(shape) - 1 - dim))
    return factor_of


def noise(own_key, dims, scale, bound, cuts=(), held_as=jnp.bfloat16):
    values = scale * jax.random.normal(own_key, dims, jnp.float32)
    if cuts:
        values = values * level_of(own_key, dims, cuts, -0.22, 0.18)
    return jnp.clip(values, -bound, bound).astype(held_as)


def setup_inputs(seed: int = 0) -> dict:
    seeds = jax.random.split(jax.random.key(seed), 7)
    queries = draw_queries(jax.random.fold_in(seeds[6], 71), 0)
    key_rows = draw_key_rows(jax.random.fold_in(seeds[6], 71), 0)
    out_grad = noise(seeds[2], (PACKED_SEQUENCES, SEQUENCE_LENGTH, QUERY_COLUMNS), 1.0, 6.0, ((0, 8), (1, 64)))
    inputs = noise(seeds[3], (PACKED_SEQUENCES, SEQUENCE_LENGTH, D), 1.0, 6.0, ((0, 8), (1, 64)))
    w_value = noise(seeds[4], (D, KW), D ** -0.5, 0.09375, ((0, 8),))
    doc_pos = draw_doc_pos(jax.random.fold_in(seeds[6], 71), 0)
    return dict(queries=queries, key_rows=key_rows, out_grad=out_grad, inputs=inputs, w_value=w_value, doc_pos=doc_pos)


masked_value = -1e+30

def attend(query_row_block, key_span_rows, value_span_rows, gradient_rows, position):
    count_of_rows = query_row_block.shape[0]
    span_length = key_span_rows.shape[0]
    score_scale = 1.0 / math.sqrt(HEAD_SIZE)
    offset = (SPAN * count_of_rows + jnp.arange(count_of_rows, dtype=jnp.int32))[:, None] - jnp.arange(span_length, dtype=jnp.int32)[None, :]
    allowed = (offset >= 0) & (offset <= position[:, None])
    query_head_matrix = query_row_block.reshape(count_of_rows, KEY_HEADS, GROUP_WIDTH, HEAD_SIZE).transpose(1, 2, 0, 3)
    gradient_heads = gradient_rows.reshape(count_of_rows, KEY_HEADS, GROUP_WIDTH, HEAD_SIZE).transpose(1, 2, 0, 3)
    key_head_matrix = key_span_rows.reshape(span_length, KEY_HEADS, HEAD_SIZE).transpose(1, 0, 2)
    value_head_matrix = value_span_rows.reshape(span_length, KEY_HEADS, HEAD_SIZE).transpose(1, 0, 2)

    def one_head(operands):
        query_head, grad_head, key_head, value_head = operands
        query_wide = query_head.astype(jnp.float32)
        grad_wide = grad_head.astype(jnp.float32)
        value_wide = value_head.astype(jnp.float32)
        scores = jnp.einsum('gtd,wd->gtw', query_wide, key_head.astype(jnp.float32)) * score_scale
        scores = jnp.where(allowed[None], scores, masked_value)
        row_max = lax.optimization_barrier(jnp.max(scores, axis=-1, keepdims=True))
        exp_scores = jnp.exp(scores - row_max)
        attn_weights = exp_scores / lax.optimization_barrier(jnp.sum(exp_scores, axis=-1, keepdims=True))
        weights_low = lax.optimization_barrier(attn_weights.astype(jnp.bfloat16)).astype(jnp.float32)
        output = jnp.einsum('gtw,wd->gtd', weights_low, value_wide)
        row_delta = lax.optimization_barrier(jnp.sum(grad_wide * output, axis=-1, keepdims=True))
        prob_grad = jnp.einsum('gtd,wd->gtw', grad_wide, value_wide)
        score_grad = attn_weights * (prob_grad - row_delta)
        score_low = lax.optimization_barrier(score_grad.astype(jnp.bfloat16)).astype(jnp.float32)
        value_portion = jnp.einsum('gtw,gtd->wd', weights_low, grad_wide)
        key_portion = jnp.einsum('gtw,gtd->wd', score_low, query_wide) * score_scale
        return (key_portion, value_portion)
    key_portion, value_portion = lax.map(one_head, (query_head_matrix, gradient_heads, key_head_matrix, value_head_matrix))
    key_portion = key_portion.transpose(1, 0, 2).reshape(span_length, KEY_HEADS * HEAD_SIZE)
    value_portion = value_portion.transpose(1, 0, 2).reshape(span_length, KEY_HEADS * HEAD_SIZE)
    return (key_portion, value_portion)

def reference(queries, key_rows, out_grad, inputs, w_value, doc_pos):
    values = jnp.dot(inputs.reshape(PACKED_SEQUENCES * SEQUENCE_LENGTH, D), w_value, preferred_element_type=jnp.float32)
    values = values.astype(jnp.bfloat16).reshape(PACKED_SEQUENCES, SEQUENCE_LENGTH, KW)
    front_pad = SPAN * TOK_DEV
    span_length = (SPAN + 1) * TOK_DEV

    def one_sequence(operands):
        query_seq, key_seq, grad_seq, value_seq, position_seq = operands
        key_padded = jnp.concatenate([jnp.zeros((front_pad, KW), jnp.bfloat16), key_seq], axis=0)
        value_padded = jnp.concatenate([jnp.zeros((front_pad, KW), jnp.bfloat16), value_seq], axis=0)

        def block_step(accums, block_index):
            key_accum, value_accum = accums
            row_start = (block_index * TOK_DEV).astype(jnp.int32)
            query_block = lax.dynamic_slice_in_dim(query_seq, row_start, TOK_DEV, 0)
            grad_block = lax.dynamic_slice_in_dim(grad_seq, row_start, TOK_DEV, 0)
            position_block = lax.dynamic_slice_in_dim(position_seq, row_start, TOK_DEV, 0)
            key_span_rows = lax.dynamic_slice_in_dim(key_padded, row_start, span_length, 0)
            value_span_rows = lax.dynamic_slice_in_dim(value_padded, row_start, span_length, 0)
            key_portion, value_portion = attend(query_block, key_span_rows, value_span_rows, grad_block, position_block)
            key_accum = lax.dynamic_update_slice_in_dim(key_accum, lax.dynamic_slice_in_dim(key_accum, row_start, span_length, 0) + key_portion, row_start, 0)
            value_accum = lax.dynamic_update_slice_in_dim(value_accum, lax.dynamic_slice_in_dim(value_accum, row_start, span_length, 0) + value_portion, row_start, 0)
            return ((key_accum, value_accum), None)
        empty = jnp.zeros((front_pad + SEQUENCE_LENGTH, KW), jnp.float32)
        (key_accum, value_accum), _ = lax.scan(block_step, (empty, empty), jnp.arange(N_DP, dtype=jnp.int32))
        return (key_accum[front_pad:], value_accum[front_pad:])
    key_total, value_total = lax.map(one_sequence, (queries, key_rows, out_grad, values, doc_pos))
    key_grad = key_total.astype(jnp.bfloat16)
    value_low = value_total.astype(jnp.bfloat16)
    input_blocks = inputs.reshape(PACKED_SEQUENCES * N_DP, TOK_DEV, D)
    value_blocks = value_low.reshape(PACKED_SEQUENCES * N_DP, TOK_DEV, KW)

    def add_block(running, operands):
        input_block, value_block = operands
        product = jnp.dot(input_block.T, value_block, preferred_element_type=jnp.float32)
        rounded = lax.optimization_barrier(product.astype(jnp.bfloat16))
        return (running + rounded.astype(jnp.float32), None)
    total_grad, _ = lax.scan(add_block, jnp.zeros((D, KW), jnp.float32), (input_blocks, value_blocks))
    weight_grad = (total_grad * (1.0 / math.sqrt(PACKED_SEQUENCES * SEQUENCE_LENGTH))).astype(jnp.bfloat16)
    return (key_grad, weight_grad)
```

```python
import math

import jax
import jax.numpy as jnp
from jax import lax
from jax.experimental import pallas as pl
from jax.experimental.pallas import tpu as pltpu
from jax.sharding import PartitionSpec as P

KEY_HEADS = 4
GROUP_WIDTH = 8
HEAD_SIZE = 128
SPAN = 3
BLOCK = 128
PAIR = 2 * HEAD_SIZE
GROUP_COLUMNS = GROUP_WIDTH * HEAD_SIZE
SPAN_ROWS = (SPAN + 1) * BLOCK

masked_value = -1e30
NT = (((1,), (1,)), ((), ()))


def shift(block, distance):
    devices = range(lax.axis_size("dp"))
    route = [(i, i + distance) for i in devices if i + distance in devices]
    return lax.ppermute(block, "dp", route)


def stacked(ref, pair):
    first = ref[:, pair * PAIR : pair * PAIR + HEAD_SIZE]
    second = ref[:, pair * PAIR + HEAD_SIZE : (pair + 1) * PAIR]
    return jnp.concatenate([first, second], axis=0)


def weights_kernel(
    position_ref, query_ref, grad_ref, k0_ref, k1_ref, k2_ref, k3_ref, weights_ref, v0_ref, v1_ref, v2_ref, v3_ref
):
    keys_down = lax.broadcasted_iota(jnp.int32, (SPAN_ROWS, BLOCK), 0)
    queries_across = lax.broadcasted_iota(jnp.int32, (SPAN_ROWS, BLOCK), 1)
    offset = SPAN * BLOCK + queries_across - keys_down
    allowed = (offset >= 0) & (offset <= position_ref[...])
    mask = jnp.where(allowed, 0.0, masked_value).astype(jnp.bfloat16)
    keys = jnp.concatenate([k0_ref[...], k1_ref[...], k2_ref[...], k3_ref[...]], axis=0)
    keys = jnp.concatenate([keys, mask], axis=1)
    unit = (
        lax.broadcasted_iota(jnp.int32, (PAIR, BLOCK), 0) % BLOCK
        == lax.broadcasted_iota(jnp.int32, (PAIR, BLOCK), 1)
    )
    unit = jnp.where(unit, 1.0, 0.0).astype(jnp.bfloat16)
    score_scale = 1.0 / math.sqrt(HEAD_SIZE)
    total = jnp.zeros((SPAN_ROWS, HEAD_SIZE), jnp.float32)
    for pair in range(GROUP_WIDTH // 2):
        heads = jnp.concatenate([stacked(query_ref, pair), unit], axis=1)
        scores = lax.dot_general(keys, heads, NT, preferred_element_type=jnp.float32)
        top = jnp.max(scores, axis=0, keepdims=True)
        weights = jnp.exp((scores - top) * score_scale)
        weights = weights * (1.0 / jnp.sum(weights, axis=0, keepdims=True))
        low = weights.astype(jnp.bfloat16)
        weights_ref[0, :, pair * PAIR : (pair + 1) * PAIR] = low
        total += jnp.dot(low, stacked(grad_ref, pair), preferred_element_type=jnp.float32)
    for block, out_ref in enumerate((v0_ref, v1_ref, v2_ref, v3_ref)):
        out_ref[...] = total[block * BLOCK : (block + 1) * BLOCK].astype(out_ref.dtype)


def scores_kernel(
    weights_ref, query_ref, grad_ref, v0_ref, v1_ref, v2_ref, v3_ref, k0_ref, k1_ref, k2_ref, k3_ref
):
    values = jnp.concatenate([v0_ref[...], v1_ref[...], v2_ref[...], v3_ref[...]], axis=0)
    total = jnp.zeros((SPAN_ROWS, HEAD_SIZE), jnp.float32)
    for pair in range(GROUP_WIDTH // 2):
        prob_grad = lax.dot_general(
            values, stacked(grad_ref, pair), NT, preferred_element_type=jnp.float32
        )
        weights = weights_ref[0, :, pair * PAIR : (pair + 1) * PAIR].astype(jnp.float32)
        row_delta = jnp.sum(weights * prob_grad, axis=0, keepdims=True)
        low = (weights * (prob_grad - row_delta)).astype(jnp.bfloat16)
        total += jnp.dot(low, stacked(query_ref, pair), preferred_element_type=jnp.float32)
    total = total * (1.0 / math.sqrt(HEAD_SIZE))
    for block, out_ref in enumerate((k0_ref, k1_ref, k2_ref, k3_ref)):
        out_ref[...] = total[block * BLOCK : (block + 1) * BLOCK].astype(out_ref.dtype)


wide = pl.BlockSpec((BLOCK, GROUP_COLUMNS), lambda g: (0, g))
narrow = pl.BlockSpec((BLOCK, HEAD_SIZE), lambda g: (0, g))
held = pl.BlockSpec((1, SPAN_ROWS, GROUP_COLUMNS), lambda g: (g, 0, 0))
gradients = [
    jax.ShapeDtypeStruct((BLOCK, KEY_HEADS * HEAD_SIZE), kind)
    for kind in (jnp.bfloat16, jnp.bfloat16, jnp.bfloat16, jnp.float32)
]
KERNEL_FLOPS = 2 * 2 * SPAN_ROWS * BLOCK * KEY_HEADS * GROUP_COLUMNS
params = pltpu.CompilerParams(vmem_limit_bytes=40 * 1024 * 1024)


def attention_weights(position, queries, grads, keys):
    return pl.pallas_call(
        weights_kernel,
        grid=(KEY_HEADS,),
        in_specs=[pl.BlockSpec((1, BLOCK), lambda g: (0, 0)), wide, wide] + [narrow] * 4,
        out_specs=[held] + [narrow] * 4,
        out_shape=[jax.ShapeDtypeStruct((KEY_HEADS, SPAN_ROWS, GROUP_COLUMNS), jnp.bfloat16)]
        + gradients,
        compiler_params=params,
        cost_estimate=pl.CostEstimate(
            flops=2 * KERNEL_FLOPS, bytes_accessed=8 << 20, transcendentals=SPAN_ROWS * BLOCK * 32
        ),
        name="attention_weights",
    )(position, queries, grads, *keys)


def key_gradient(weights, queries, grads, values):
    return pl.pallas_call(
        scores_kernel,
        grid=(KEY_HEADS,),
        in_specs=[held, wide, wide] + [narrow] * 4,
        out_specs=[narrow] * 4,
        out_shape=gradients,
        compiler_params=params,
        cost_estimate=pl.CostEstimate(
            flops=2 * KERNEL_FLOPS, bytes_accessed=8 << 20, transcendentals=0
        ),
        name="key_gradient",
    )(weights, queries, grads, *values)


def span_of(block):
    return [shift(block, 3), shift(block, 2), shift(block, 1), block]


def owed(parts):
    total = parts[SPAN]
    for distance in (1, 2, 3):
        total = total + shift(parts[SPAN - distance], -distance).astype(jnp.float32)
    return total.astype(jnp.bfloat16)


def sum_over_dp(partial):
    size = lax.axis_size("dp")
    rows, columns = partial.shape
    each = rows // size
    pieces = lax.all_to_all(partial, "dp", 0, 0, tiled=True).reshape(size, each, columns)
    return jnp.sum(pieces.astype(jnp.float32), axis=0)


def per_device(queries, key_rows, out_grad, inputs, w_value, doc_pos):
    queries, keys, grads, rows = queries[0], key_rows[0], out_grad[0], inputs[0]
    key_span = span_of(keys)
    w_whole = lax.all_gather(w_value, "fsdp", axis=0, tiled=True)
    rows_here = lax.all_to_all(rows, "fsdp", 1, 0, tiled=True)
    weights, *value_parts = attention_weights(doc_pos, queries, grads, key_span)
    value_grad = owed(value_parts)
    fsdp_size = lax.axis_size("fsdp")
    copies = jnp.broadcast_to(value_grad[None], (fsdp_size,) + value_grad.shape)
    value_grads = lax.all_to_all(copies, "fsdp", 0, 0, tiled=True).reshape(-1, value_grad.shape[1])

    values = jnp.dot(rows, w_whole, preferred_element_type=jnp.float32).astype(jnp.bfloat16)
    key_parts = key_gradient(weights, queries, grads, span_of(values))
    key_grad = owed(key_parts)

    product = lax.dot_general(
        rows_here, value_grads, (((0,), (0,)), ((), ())), preferred_element_type=jnp.float32
    )
    piece = sum_over_dp(product.astype(jnp.bfloat16))
    dp_size = lax.axis_size("dp")
    token_total = fsdp_size * dp_size * BLOCK
    piece = (piece * (1.0 / math.sqrt(token_total))).astype(jnp.bfloat16)
    copies = jnp.broadcast_to(piece[None], (dp_size,) + piece.shape).reshape(-1, piece.shape[1])
    weight_grad = lax.all_to_all(copies, "dp", 0, 0, tiled=True)
    return (key_grad[None], weight_grad)


def solution(mesh):
    return jax.shard_map(
        per_device,
        mesh=mesh,
        in_specs=(
            P("fsdp", "dp", None),
            P("fsdp", "dp", None),
            P("fsdp", "dp", None),
            P("fsdp", "dp", None),
            P("fsdp", None),
            P("fsdp", "dp"),
        ),
        out_specs=(P("fsdp", "dp", None), P("fsdp", None)),
        check_vma=False,
    )
```

```python
import math

import jax
import jax.numpy as jnp
from jax import lax
from jax.experimental import pallas as pl
from jax.experimental.pallas import tpu as pltpu
from jax.sharding import Mesh, PartitionSpec as P

KEY_HEADS = 4
GROUP_WIDTH = 8
HEAD_SIZE = 128
SPAN = 3
BLOCK = 128
PAIR = 2 * HEAD_SIZE
GROUP_COLUMNS = GROUP_WIDTH * HEAD_SIZE
SPAN_ROWS = (SPAN + 1) * BLOCK

DP = ("x", "z", "c")
masked_value = -1e30
NT = (((1,), (1,)), ((), ()))


def shift(block, distance):
    devices = range(lax.axis_size(DP))
    route = [(i, i + distance) for i in devices if i + distance in devices]
    return lax.ppermute(block, DP, route)


def stacked(ref, pair):
    first = ref[:, pair * PAIR : pair * PAIR + HEAD_SIZE]
    second = ref[:, pair * PAIR + HEAD_SIZE : (pair + 1) * PAIR]
    return jnp.concatenate([first, second], axis=0)


def weights_kernel(
    position_ref, query_ref, grad_ref, k0_ref, k1_ref, k2_ref, k3_ref, weights_ref, v0_ref, v1_ref, v2_ref, v3_ref
):
    keys_down = lax.broadcasted_iota(jnp.int32, (SPAN_ROWS, BLOCK), 0)
    queries_across = lax.broadcasted_iota(jnp.int32, (SPAN_ROWS, BLOCK), 1)
    offset = SPAN * BLOCK + queries_across - keys_down
    allowed = (offset >= 0) & (offset <= position_ref[...])
    mask = jnp.where(allowed, 0.0, masked_value).astype(jnp.bfloat16)
    keys = jnp.concatenate([k0_ref[...], k1_ref[...], k2_ref[...], k3_ref[...]], axis=0)
    keys = jnp.concatenate([keys, mask], axis=1)
    unit = (
        lax.broadcasted_iota(jnp.int32, (PAIR, BLOCK), 0) % BLOCK
        == lax.broadcasted_iota(jnp.int32, (PAIR, BLOCK), 1)
    )
    unit = jnp.where(unit, 1.0, 0.0).astype(jnp.bfloat16)
    score_scale = 1.0 / math.sqrt(HEAD_SIZE)
    total = jnp.zeros((SPAN_ROWS, HEAD_SIZE), jnp.float32)
    for pair in range(GROUP_WIDTH // 2):
        heads = jnp.concatenate([stacked(query_ref, pair), unit], axis=1)
        scores = lax.dot_general(keys, heads, NT, preferred_element_type=jnp.float32)
        top = jnp.max(scores, axis=0, keepdims=True)
        weights = jnp.exp((scores - top) * score_scale)
        weights = weights * (1.0 / jnp.sum(weights, axis=0, keepdims=True))
        low = weights.astype(jnp.bfloat16)
        weights_ref[0, :, pair * PAIR : (pair + 1) * PAIR] = low
        total += jnp.dot(low, stacked(grad_ref, pair), preferred_element_type=jnp.float32)
    for block, out_ref in enumerate((v0_ref, v1_ref, v2_ref, v3_ref)):
        out_ref[...] = total[block * BLOCK : (block + 1) * BLOCK].astype(out_ref.dtype)


def scores_kernel(
    weights_ref, query_ref, grad_ref, v0_ref, v1_ref, v2_ref, v3_ref, k0_ref, k1_ref, k2_ref, k3_ref
):
    values = jnp.concatenate([v0_ref[...], v1_ref[...], v2_ref[...], v3_ref[...]], axis=0)
    total = jnp.zeros((SPAN_ROWS, HEAD_SIZE), jnp.float32)
    for pair in range(GROUP_WIDTH // 2):
        prob_grad = lax.dot_general(
            values, stacked(grad_ref, pair), NT, preferred_element_type=jnp.float32
        )
        weights = weights_ref[0, :, pair * PAIR : (pair + 1) * PAIR].astype(jnp.float32)
        row_delta = jnp.sum(weights * prob_grad, axis=0, keepdims=True)
        low = (weights * (prob_grad - row_delta)).astype(jnp.bfloat16)
        total += jnp.dot(low, stacked(query_ref, pair), preferred_element_type=jnp.float32)
    total = total * (1.0 / math.sqrt(HEAD_SIZE))
    for block, out_ref in enumerate((k0_ref, k1_ref, k2_ref, k3_ref)):
        out_ref[...] = total[block * BLOCK : (block + 1) * BLOCK].astype(out_ref.dtype)


wide = pl.BlockSpec((BLOCK, GROUP_COLUMNS), lambda g: (0, g))
narrow = pl.BlockSpec((BLOCK, HEAD_SIZE), lambda g: (0, g))
held = pl.BlockSpec((1, SPAN_ROWS, GROUP_COLUMNS), lambda g: (g, 0, 0))
gradients = [
    jax.ShapeDtypeStruct((BLOCK, KEY_HEADS * HEAD_SIZE), kind)
    for kind in (jnp.bfloat16, jnp.bfloat16, jnp.bfloat16, jnp.float32)
]
KERNEL_FLOPS = 2 * 2 * SPAN_ROWS * BLOCK * KEY_HEADS * GROUP_COLUMNS
params = pltpu.CompilerParams(vmem_limit_bytes=40 * 1024 * 1024)


def attention_weights(position, queries, grads, keys):
    return pl.pallas_call(
        weights_kernel,
        grid=(KEY_HEADS,),
        in_specs=[pl.BlockSpec((1, BLOCK), lambda g: (0, 0)), wide, wide] + [narrow] * 4,
        out_specs=[held] + [narrow] * 4,
        out_shape=[jax.ShapeDtypeStruct((KEY_HEADS, SPAN_ROWS, GROUP_COLUMNS), jnp.bfloat16)]
        + gradients,
        compiler_params=params,
        cost_estimate=pl.CostEstimate(
            flops=2 * KERNEL_FLOPS, bytes_accessed=8 << 20, transcendentals=SPAN_ROWS * BLOCK * 32
        ),
        name="attention_weights",
    )(position, queries, grads, *keys)


def key_gradient(weights, queries, grads, values):
    return pl.pallas_call(
        scores_kernel,
        grid=(KEY_HEADS,),
        in_specs=[held, wide, wide] + [narrow] * 4,
        out_specs=[narrow] * 4,
        out_shape=gradients,
        compiler_params=params,
        cost_estimate=pl.CostEstimate(
            flops=2 * KERNEL_FLOPS, bytes_accessed=8 << 20, transcendentals=0
        ),
        name="key_gradient",
    )(weights, queries, grads, *values)


def span_of(block):
    return [shift(block, 3), shift(block, 2), shift(block, 1), block]


def owed(parts):
    total = parts[SPAN]
    for distance in (1, 2, 3):
        total = total + shift(parts[SPAN - distance], -distance).astype(jnp.float32)
    return total.astype(jnp.bfloat16)


def exchange_rows(rows):
    columns = rows.shape[1]
    quarter = columns // 4
    copies = [rows[:, x * quarter : (x + 1) * quarter] for x in range(4) for c in range(2)]
    copies = jnp.concatenate(copies, axis=0)
    return lax.all_to_all(copies, ("x", "c"), 0, 0, tiled=True)


def exchange_value_grad(value_grad):
    half = value_grad.shape[1] // 2
    copies = jnp.concatenate([value_grad[:, :half], value_grad[:, half:]] * 4, axis=0)
    return lax.all_to_all(copies, ("x", "c"), 0, 0, tiled=True)


def to_plane(piece):
    route = []
    for x in range(4):
        for z in range(8):
            for c in range(2):
                for y in range(8):
                    source = ((x * 8 + z) * 2 + c) * 8 + y
                    target = (((y % 4) * 8 + z) * 2 + c) * 8 + 2 * x + y // 4
                    route.append((source, target))
    return lax.ppermute(piece, ("x", "z", "c", "y"), route)


def whole_shard(piece):
    rows, columns = piece.shape
    copies = jnp.broadcast_to(piece[None], (32, rows, columns)).reshape(32 * rows, columns)
    half = lax.all_to_all(copies, ("x", "z"), 0, 0, tiled=True)
    other = lax.ppermute(half, "c", [(0, 1), (1, 0)])
    first = lax.axis_index("c") == 0
    return jnp.concatenate(
        [jnp.where(first, half, other), jnp.where(first, other, half)], axis=1
    )


def per_device(queries, key_rows, out_grad, inputs, w_value, doc_pos):
    queries, keys, grads, rows = queries[0], key_rows[0], out_grad[0], inputs[0]
    key_span = span_of(keys)
    w_whole = lax.all_gather(w_value, "y", axis=0, tiled=True)
    rows_here = exchange_rows(rows)
    weights, *value_parts = attention_weights(doc_pos, queries, grads, key_span)
    value_grads = exchange_value_grad(owed(value_parts))
    product = lax.dot_general(
        rows_here, value_grads, (((0,), (0,)), ((), ())), preferred_element_type=jnp.float32
    ).astype(jnp.bfloat16)

    w_whole, product = lax.optimization_barrier((w_whole, product))
    pieces = lax.all_to_all(product, ("y", "z"), 0, 0, tiled=True)
    values = jnp.dot(rows, w_whole, preferred_element_type=jnp.float32).astype(jnp.bfloat16)
    key_parts = key_gradient(weights, queries, grads, span_of(values))
    pieces, key_parts = lax.optimization_barrier((pieces, key_parts))

    key_grad = owed(key_parts)
    pieces = pieces.reshape(64, -1, pieces.shape[1]).astype(jnp.float32)
    token_total = lax.axis_size(("x", "z", "c", "y")) * BLOCK
    piece = (jnp.sum(pieces, axis=0) * (1.0 / math.sqrt(token_total))).astype(jnp.bfloat16)
    weight_grad = whole_shard(to_plane(piece))
    return (key_grad[None], weight_grad)


def solution(mesh):
    mesh = Mesh(mesh.devices.reshape(4, 8, 2, 8), ("x", "z", "c", "y"))
    tokens = P("y", DP, None)
    return jax.shard_map(
        per_device,
        mesh=mesh,
        in_specs=(tokens, tokens, tokens, tokens, P("y", None), P("y", DP)),
        out_specs=(tokens, P("y", None)),
        check_vma=False,
    )
```

```python
import math

import jax
import jax.numpy as jnp
from jax import lax
from jax.experimental import pallas as pl
from jax.experimental.pallas import tpu as pltpu
from jax.sharding import Mesh, PartitionSpec as P

KEY_HEADS = 4
GROUP_WIDTH = 8
HEAD_SIZE = 128
SPAN = 3
BLOCK = 128
PAIR = 2 * HEAD_SIZE
GROUP_COLUMNS = GROUP_WIDTH * HEAD_SIZE
SPAN_ROWS = (SPAN + 1) * BLOCK

DP = ("x", "z", "c")
masked_value = -1e30
NT = (((1,), (1,)), ((), ()))


def shift(block, distance):
    devices = range(lax.axis_size(DP))
    route = [(i, i + distance) for i in devices if i + distance in devices]
    return lax.ppermute(block, DP, route)


def stacked(ref, pair):
    first = ref[:, pair * PAIR : pair * PAIR + HEAD_SIZE]
    second = ref[:, pair * PAIR + HEAD_SIZE : (pair + 1) * PAIR]
    return jnp.concatenate([first, second], axis=0)


def weights_kernel(
    position_ref, query_ref, grad_ref, k0_ref, k1_ref, k2_ref, k3_ref, weights_ref, v0_ref, v1_ref, v2_ref, v3_ref
):
    keys_down = lax.broadcasted_iota(jnp.int32, (SPAN_ROWS, BLOCK), 0)
    queries_across = lax.broadcasted_iota(jnp.int32, (SPAN_ROWS, BLOCK), 1)
    offset = SPAN * BLOCK + queries_across - keys_down
    allowed = (offset >= 0) & (offset <= position_ref[...])
    mask = jnp.where(allowed, 0.0, masked_value).astype(jnp.bfloat16)
    keys = jnp.concatenate([k0_ref[...], k1_ref[...], k2_ref[...], k3_ref[...]], axis=0)
    keys = jnp.concatenate([keys, mask], axis=1)
    unit = (
        lax.broadcasted_iota(jnp.int32, (PAIR, BLOCK), 0) % BLOCK
        == lax.broadcasted_iota(jnp.int32, (PAIR, BLOCK), 1)
    )
    unit = jnp.where(unit, 1.0, 0.0).astype(jnp.bfloat16)
    score_scale = 1.0 / math.sqrt(HEAD_SIZE)
    total = jnp.zeros((SPAN_ROWS, HEAD_SIZE), jnp.float32)
    for pair in range(GROUP_WIDTH // 2):
        heads = jnp.concatenate([stacked(query_ref, pair), unit], axis=1)
        scores = lax.dot_general(keys, heads, NT, preferred_element_type=jnp.float32)
        top = jnp.max(scores, axis=0, keepdims=True)
        weights = jnp.exp((scores - top) * score_scale)
        weights = weights * (1.0 / jnp.sum(weights, axis=0, keepdims=True))
        low = weights.astype(jnp.bfloat16)
        weights_ref[0, :, pair * PAIR : (pair + 1) * PAIR] = low
        total += jnp.dot(low, stacked(grad_ref, pair), preferred_element_type=jnp.float32)
    for block, out_ref in enumerate((v0_ref, v1_ref, v2_ref, v3_ref)):
        out_ref[...] = total[block * BLOCK : (block + 1) * BLOCK].astype(out_ref.dtype)


def scores_kernel(
    weights_ref, query_ref, grad_ref, v0_ref, v1_ref, v2_ref, v3_ref, k0_ref, k1_ref, k2_ref, k3_ref
):
    values = jnp.concatenate([v0_ref[...], v1_ref[...], v2_ref[...], v3_ref[...]], axis=0)
    total = jnp.zeros((SPAN_ROWS, HEAD_SIZE), jnp.float32)
    for pair in range(GROUP_WIDTH // 2):
        prob_grad = lax.dot_general(
            values, stacked(grad_ref, pair), NT, preferred_element_type=jnp.float32
        )
        weights = weights_ref[0, :, pair * PAIR : (pair + 1) * PAIR].astype(jnp.float32)
        row_delta = jnp.sum(weights * prob_grad, axis=0, keepdims=True)
        low = (weights * (prob_grad - row_delta)).astype(jnp.bfloat16)
        total += jnp.dot(low, stacked(query_ref, pair), preferred_element_type=jnp.float32)
    total = total * (1.0 / math.sqrt(HEAD_SIZE))
    for block, out_ref in enumerate((k0_ref, k1_ref, k2_ref, k3_ref)):
        out_ref[...] = total[block * BLOCK : (block + 1) * BLOCK].astype(out_ref.dtype)


wide = pl.BlockSpec((BLOCK, GROUP_COLUMNS), lambda g: (0, g))
narrow = pl.BlockSpec((BLOCK, HEAD_SIZE), lambda g: (0, g))
held = pl.BlockSpec((1, SPAN_ROWS, GROUP_COLUMNS), lambda g: (g, 0, 0))
gradients = [
    jax.ShapeDtypeStruct((BLOCK, KEY_HEADS * HEAD_SIZE), kind)
    for kind in (jnp.bfloat16, jnp.bfloat16, jnp.bfloat16, jnp.float32)
]
KERNEL_FLOPS = 2 * 2 * SPAN_ROWS * BLOCK * KEY_HEADS * GROUP_COLUMNS
params = pltpu.CompilerParams(vmem_limit_bytes=40 * 1024 * 1024)


def attention_weights(position, queries, grads, keys):
    return pl.pallas_call(
        weights_kernel,
        grid=(KEY_HEADS,),
        in_specs=[pl.BlockSpec((1, BLOCK), lambda g: (0, 0)), wide, wide] + [narrow] * 4,
        out_specs=[held] + [narrow] * 4,
        out_shape=[jax.ShapeDtypeStruct((KEY_HEADS, SPAN_ROWS, GROUP_COLUMNS), jnp.bfloat16)]
        + gradients,
        compiler_params=params,
        cost_estimate=pl.CostEstimate(
            flops=2 * KERNEL_FLOPS, bytes_accessed=8 << 20, transcendentals=SPAN_ROWS * BLOCK * 32
        ),
        name="attention_weights",
    )(position, queries, grads, *keys)


def key_gradient(weights, queries, grads, values):
    return pl.pallas_call(
        scores_kernel,
        grid=(KEY_HEADS,),
        in_specs=[held, wide, wide] + [narrow] * 4,
        out_specs=[narrow] * 4,
        out_shape=gradients,
        compiler_params=params,
        cost_estimate=pl.CostEstimate(
            flops=2 * KERNEL_FLOPS, bytes_accessed=8 << 20, transcendentals=0
        ),
        name="key_gradient",
    )(weights, queries, grads, *values)


def span_of(block):
    return [shift(block, 3), shift(block, 2), shift(block, 1), block]


def owed(parts):
    total = parts[SPAN]
    for distance in (1, 2, 3):
        total = total + shift(parts[SPAN - distance], -distance).astype(jnp.float32)
    return total.astype(jnp.bfloat16)


OTHER_CORE = [(0, 1), (1, 0)]
QUARTER = 1024
HALF = 256


def quarters_kernel(rows_ref, out_ref):
    out_ref[...] = rows_ref[...]


def partial_values_kernel(core_ref, near_ref, far_ref, weight_ref, out_ref):
    block = pl.program_id(0)
    for rows_ref, core in ((near_ref, core_ref[0]), (far_ref, 1 - core_ref[0])):
        values = jnp.dot(rows_ref[...], weight_ref[...], preferred_element_type=jnp.float32)
        out_ref[pl.ds(pl.multiple_of((2 * block + core) * BLOCK, BLOCK), BLOCK), :] = values.astype(
            jnp.bfloat16
        )


def pack_kernel(own_ref, one_ref, two_ref, three_ref, values_ref, out_ref):
    total = own_ref[...] + one_ref[...].astype(jnp.float32)
    total = total + two_ref[...].astype(jnp.float32) + three_ref[...].astype(jnp.float32)
    low = total.astype(jnp.bfloat16)
    for device in range(8):
        core = device % 2
        rows = slice(device * BLOCK, (device + 1) * BLOCK)
        out_ref[rows, :HALF] = low[:, core * HALF : (core + 1) * HALF]
        out_ref[rows, HALF:] = values_ref[rows, :]


def product_kernel(core_ref, near_ref, far_ref, grads_ref, out_ref):
    total = None
    for rows_ref, core in ((near_ref, core_ref[0]), (far_ref, 1 - core_ref[0])):
        grads = [
            grads_ref[pl.ds(pl.multiple_of((2 * x + core) * BLOCK, BLOCK), BLOCK), :HALF]
            for x in range(4)
        ]
        part = lax.dot_general(
            rows_ref[...],
            jnp.concatenate(grads, axis=0),
            (((0,), (0,)), ((), ())),
            preferred_element_type=jnp.float32,
        )
        total = part if total is None else total + part
    out_ref[...] = total.astype(jnp.bfloat16)


def exchange_rows(rows):
    quarters = pl.pallas_call(
        quarters_kernel,
        grid=(4,),
        in_specs=[pl.BlockSpec((BLOCK, QUARTER), lambda x: (0, x))],
        out_specs=pl.BlockSpec((BLOCK, QUARTER), lambda x: (x, 0)),
        out_shape=jax.ShapeDtypeStruct((4 * BLOCK, QUARTER), jnp.bfloat16),
        name="quarters",
    )(rows)
    near = lax.all_to_all(quarters, "x", 0, 0, tiled=True)
    return near, lax.ppermute(near, "c", OTHER_CORE)


def exchange_projection(w_value):
    route = [(target, source) for source, target in plane_route()]
    start = (lax.axis_index("x") * BLOCK, lax.axis_index("c") * HALF)
    piece = lax.dynamic_slice(w_value, start, (BLOCK, HALF))
    piece = lax.ppermute(piece, ("x", "z", "c", "y"), route)
    copies = jnp.broadcast_to(piece[None], (8, BLOCK, HALF)).reshape(8 * BLOCK, HALF)
    return lax.all_to_all(copies, "y", 0, 0, tiled=True)


def partial_values(core, near, far, weight):
    rows = pl.BlockSpec((BLOCK, QUARTER), lambda x, core: (x, 0))
    return pl.pallas_call(
        partial_values_kernel,
        grid_spec=pltpu.PrefetchScalarGridSpec(
            num_scalar_prefetch=1,
            grid=(4,),
            in_specs=[rows, rows, pl.BlockSpec((QUARTER, HALF), lambda x, core: (0, 0))],
            out_specs=pl.BlockSpec((8 * BLOCK, HALF), lambda x, core: (0, 0)),
        ),
        out_shape=jax.ShapeDtypeStruct((8 * BLOCK, HALF), jnp.bfloat16),
        name="partial_values",
    )(core, near, far, weight)


def exchange_packed(value_parts, values):
    received = [shift(value_parts[SPAN - distance], -distance) for distance in (1, 2, 3)]
    packed = pl.pallas_call(
        pack_kernel,
        out_shape=jax.ShapeDtypeStruct((8 * BLOCK, 2 * HALF), jnp.bfloat16),
        name="pack",
    )(value_parts[SPAN], *received, values)
    return lax.all_to_all(packed, ("x", "c"), 0, 0, tiled=True)


def group_product(core, near, far, packed):
    rows = pl.BlockSpec((4 * BLOCK, HALF), lambda part, core: (0, part))
    return pl.pallas_call(
        product_kernel,
        grid_spec=pltpu.PrefetchScalarGridSpec(
            num_scalar_prefetch=1,
            grid=(QUARTER // HALF,),
            in_specs=[rows, rows, pl.BlockSpec((8 * BLOCK, 2 * HALF), lambda part, core: (0, 0))],
            out_specs=pl.BlockSpec((HALF, HALF), lambda part, core: (part, 0)),
        ),
        out_shape=jax.ShapeDtypeStruct((QUARTER, HALF), jnp.bfloat16),
        name="group_product",
    )(core, near, far, packed)


def plane_route():
    route = []
    for x in range(4):
        for z in range(8):
            for c in range(2):
                for y in range(8):
                    source = ((x * 8 + z) * 2 + c) * 8 + y
                    target = (((y % 4) * 8 + z) * 2 + c) * 8 + 2 * x + y // 4
                    route.append((source, target))
    return route


def whole_shard(piece):
    rows, columns = piece.shape
    copies = jnp.broadcast_to(piece[None], (32, rows, columns)).reshape(32 * rows, columns)
    half = lax.all_to_all(copies, ("x", "z"), 0, 0, tiled=True)
    other = lax.ppermute(half, "c", OTHER_CORE)
    first = lax.axis_index("c") == 0
    return jnp.concatenate(
        [jnp.where(first, half, other), jnp.where(first, other, half)], axis=1
    )


def per_device(queries, key_rows, out_grad, inputs, w_value, doc_pos):
    queries, keys, grads, rows = queries[0], key_rows[0], out_grad[0], inputs[0]
    core = lax.axis_index("c").astype(jnp.int32).reshape(1)
    key_span = span_of(keys)
    near, far = exchange_rows(rows)
    weight = exchange_projection(w_value)
    values = partial_values(core, near, far, weight)
    weights, *value_parts = attention_weights(doc_pos, queries, grads, key_span)
    packed = exchange_packed(value_parts, values)
    product = group_product(core, near, far, packed)
    pieces = lax.all_to_all(product, ("y", "z"), 0, 0, tiled=True)

    parts = packed.reshape(4, 2, BLOCK, 2 * HALF)[..., HALF:].astype(jnp.float32)
    values = jnp.sum(parts, axis=0).astype(jnp.bfloat16)
    values = jnp.concatenate([values[0], values[1]], axis=1)
    value_span = span_of(values)
    pieces, value_span = lax.optimization_barrier((pieces, value_span))
    key_parts = key_gradient(weights, queries, grads, value_span)
    key_grad = owed(key_parts)

    pieces = pieces.reshape(64, -1, HALF).astype(jnp.float32)
    token_total = lax.axis_size(("x", "z", "c", "y")) * BLOCK
    piece = (jnp.sum(pieces, axis=0) * (1.0 / math.sqrt(token_total))).astype(jnp.bfloat16)
    weight_grad = whole_shard(lax.ppermute(piece, ("x", "z", "c", "y"), plane_route()))
    return (key_grad[None], weight_grad)


def solution(mesh):
    mesh = Mesh(mesh.devices.reshape(4, 8, 2, 8), ("x", "z", "c", "y"))
    tokens = P("y", DP, None)
    return jax.shard_map(
        per_device,
        mesh=mesh,
        in_specs=(tokens, tokens, tokens, tokens, P("y", None), P("y", DP)),
        out_specs=(tokens, P("y", None)),
        check_vma=False,
    )
```

```python
import math

import jax
import jax.numpy as jnp
from jax import lax
from jax.experimental import pallas as pl
from jax.experimental.pallas import tpu as pltpu
from jax.sharding import Mesh, PartitionSpec as P

KEY_HEADS = 4
GROUP_WIDTH = 8
HEAD_SIZE = 128
SPAN = 3
BLOCK = 128
PAIR = 2 * HEAD_SIZE
GROUP_COLUMNS = GROUP_WIDTH * HEAD_SIZE
SPAN_ROWS = (SPAN + 1) * BLOCK

DP = ("x", "z", "c")
masked_value = -1e30
NT = (((1,), (1,)), ((), ()))


def shift(block, distance):
    devices = range(lax.axis_size(DP))
    route = [(i, i + distance) for i in devices if i + distance in devices]
    return lax.ppermute(block, DP, route)


def stacked(ref, pair):
    first = ref[:, pair * PAIR : pair * PAIR + HEAD_SIZE]
    second = ref[:, pair * PAIR + HEAD_SIZE : (pair + 1) * PAIR]
    return jnp.concatenate([first, second], axis=0)


def weights_kernel(
    position_ref, query_ref, grad_ref, k0_ref, k1_ref, k2_ref, k3_ref, weights_ref, v0_ref, v1_ref, v2_ref, v3_ref
):
    keys_down = lax.broadcasted_iota(jnp.int32, (SPAN_ROWS, BLOCK), 0)
    queries_across = lax.broadcasted_iota(jnp.int32, (SPAN_ROWS, BLOCK), 1)
    offset = SPAN * BLOCK + queries_across - keys_down
    allowed = (offset >= 0) & (offset <= position_ref[...])
    mask = jnp.where(allowed, 0.0, masked_value).astype(jnp.bfloat16)
    keys = jnp.concatenate([k0_ref[...], k1_ref[...], k2_ref[...], k3_ref[...]], axis=0)
    keys = jnp.concatenate([keys, mask], axis=1)
    unit = (
        lax.broadcasted_iota(jnp.int32, (PAIR, BLOCK), 0) % BLOCK
        == lax.broadcasted_iota(jnp.int32, (PAIR, BLOCK), 1)
    )
    unit = jnp.where(unit, 1.0, 0.0).astype(jnp.bfloat16)
    score_scale = 1.0 / math.sqrt(HEAD_SIZE)
    total = jnp.zeros((SPAN_ROWS, HEAD_SIZE), jnp.float32)
    for pair in range(GROUP_WIDTH // 2):
        heads = jnp.concatenate([stacked(query_ref, pair), unit], axis=1)
        scores = lax.dot_general(keys, heads, NT, preferred_element_type=jnp.float32)
        top = jnp.max(scores, axis=0, keepdims=True)
        weights = jnp.exp((scores - top) * score_scale)
        weights = weights * (1.0 / jnp.sum(weights, axis=0, keepdims=True))
        low = weights.astype(jnp.bfloat16)
        weights_ref[0, :, pair * PAIR : (pair + 1) * PAIR] = low
        total += jnp.dot(low, stacked(grad_ref, pair), preferred_element_type=jnp.float32)
    for block, out_ref in enumerate((v0_ref, v1_ref, v2_ref, v3_ref)):
        out_ref[...] = total[block * BLOCK : (block + 1) * BLOCK].astype(out_ref.dtype)


def scores_kernel(
    weights_ref, query_ref, grad_ref, v0_ref, v1_ref, v2_ref, v3_ref, k0_ref, k1_ref, k2_ref, k3_ref
):
    values = jnp.concatenate([v0_ref[...], v1_ref[...], v2_ref[...], v3_ref[...]], axis=0)
    total = jnp.zeros((SPAN_ROWS, HEAD_SIZE), jnp.float32)
    for pair in range(GROUP_WIDTH // 2):
        prob_grad = lax.dot_general(
            values, stacked(grad_ref, pair), NT, preferred_element_type=jnp.float32
        )
        weights = weights_ref[0, :, pair * PAIR : (pair + 1) * PAIR].astype(jnp.float32)
        row_delta = jnp.sum(weights * prob_grad, axis=0, keepdims=True)
        low = (weights * (prob_grad - row_delta)).astype(jnp.bfloat16)
        total += jnp.dot(low, stacked(query_ref, pair), preferred_element_type=jnp.float32)
    total = total * (1.0 / math.sqrt(HEAD_SIZE))
    for block, out_ref in enumerate((k0_ref, k1_ref, k2_ref, k3_ref)):
        out_ref[...] = total[block * BLOCK : (block + 1) * BLOCK].astype(out_ref.dtype)


wide = pl.BlockSpec((BLOCK, GROUP_COLUMNS), lambda g: (0, g))
narrow = pl.BlockSpec((BLOCK, HEAD_SIZE), lambda g: (0, g))
held = pl.BlockSpec((1, SPAN_ROWS, GROUP_COLUMNS), lambda g: (g, 0, 0))
gradients = [
    jax.ShapeDtypeStruct((BLOCK, KEY_HEADS * HEAD_SIZE), kind)
    for kind in (jnp.bfloat16, jnp.bfloat16, jnp.bfloat16, jnp.float32)
]
KERNEL_FLOPS = 2 * 2 * SPAN_ROWS * BLOCK * KEY_HEADS * GROUP_COLUMNS
params = pltpu.CompilerParams(vmem_limit_bytes=16 * 1024 * 1024)


def attention_weights(position, queries, grads, keys):
    return pl.pallas_call(
        weights_kernel,
        grid=(KEY_HEADS,),
        in_specs=[pl.BlockSpec((1, BLOCK), lambda g: (0, 0)), wide, wide] + [narrow] * 4,
        out_specs=[held] + [narrow] * 4,
        out_shape=[jax.ShapeDtypeStruct((KEY_HEADS, SPAN_ROWS, GROUP_COLUMNS), jnp.bfloat16)]
        + gradients,
        compiler_params=params,
        cost_estimate=pl.CostEstimate(
            flops=2 * KERNEL_FLOPS, bytes_accessed=8 << 20, transcendentals=SPAN_ROWS * BLOCK * 32
        ),
        name="attention_weights",
    )(position, queries, grads, *keys)


def key_gradient(weights, queries, grads, values):
    return pl.pallas_call(
        scores_kernel,
        grid=(KEY_HEADS,),
        in_specs=[held, wide, wide] + [narrow] * 4,
        out_specs=[narrow] * 4,
        out_shape=gradients,
        compiler_params=params,
        cost_estimate=pl.CostEstimate(
            flops=2 * KERNEL_FLOPS, bytes_accessed=8 << 20, transcendentals=0
        ),
        name="key_gradient",
    )(weights, queries, grads, *values)


def span_of(block):
    return [shift(block, 3), shift(block, 2), shift(block, 1), block]


def owed(parts):
    total = parts[SPAN]
    for distance in (1, 2, 3):
        total = total + shift(parts[SPAN - distance], -distance).astype(jnp.float32)
    return total.astype(jnp.bfloat16)


OTHER_CORE = [(0, 1), (1, 0)]
QUARTER = 1024
HALF = 256


def quarters_kernel(rows_ref, out_ref, sems):
    copies = [
        pltpu.make_async_copy(
            rows_ref.at[:, pl.ds(x * QUARTER, QUARTER)],
            out_ref.at[pl.ds(x * BLOCK, BLOCK), :],
            sems.at[x],
        )
        for x in range(4)
    ]
    for copy in copies:
        copy.start()
    for copy in copies:
        copy.wait()


def partial_values_kernel(core_ref, near_ref, far_ref, weight_ref, out_ref):
    for rows_ref, core in ((near_ref, core_ref[0]), (far_ref, 1 - core_ref[0])):
        values = jnp.dot(rows_ref[...], weight_ref[...], preferred_element_type=jnp.float32)
        values = values.astype(jnp.bfloat16)
        for x in range(4):
            rows = pl.ds(pl.multiple_of((2 * x + core) * BLOCK, BLOCK), BLOCK)
            out_ref[rows, :] = values[x * BLOCK : (x + 1) * BLOCK]


def pack_kernel(own_ref, one_ref, two_ref, three_ref, values_ref, out_ref):
    total = own_ref[...] + one_ref[...].astype(jnp.float32)
    total = total + two_ref[...].astype(jnp.float32) + three_ref[...].astype(jnp.float32)
    low = total.astype(jnp.bfloat16)
    for device in range(8):
        core = device % 2
        rows = slice(device * BLOCK, (device + 1) * BLOCK)
        out_ref[rows, :HALF] = low[:, core * HALF : (core + 1) * HALF]
        out_ref[rows, HALF:] = values_ref[rows, :]


def product_kernel(core_ref, near_ref, far_ref, grads_ref, out_ref):
    total = None
    for rows_ref, core in ((near_ref, core_ref[0]), (far_ref, 1 - core_ref[0])):
        grads = [
            grads_ref[pl.ds(pl.multiple_of((2 * x + core) * BLOCK, BLOCK), BLOCK), :HALF]
            for x in range(4)
        ]
        part = lax.dot_general(
            jnp.concatenate(grads, axis=0),
            rows_ref[...],
            (((0,), (0,)), ((), ())),
            preferred_element_type=jnp.float32,
        )
        total = part if total is None else total + part
    out_ref[...] = total.T.astype(jnp.bfloat16)


def exchange_rows(rows):
    quarters = pl.pallas_call(
        quarters_kernel,
        in_specs=[pl.BlockSpec(memory_space=pl.ANY)],
        out_specs=pl.BlockSpec(memory_space=pl.ANY),
        out_shape=jax.ShapeDtypeStruct((4 * BLOCK, QUARTER), jnp.bfloat16),
        scratch_shapes=[pltpu.SemaphoreType.DMA((4,))],
        compiler_params=params,
        name="quarters",
    )(rows)
    return lax.all_to_all(quarters, "x", 0, 0, tiled=True)


def projection_piece(w_value):
    route = [(target, source) for source, target in plane_route()]
    start = (lax.axis_index("x") * BLOCK, lax.axis_index("c") * HALF)
    piece = lax.dynamic_slice(w_value, start, (BLOCK, HALF))
    return lax.ppermute(piece, ("x", "z", "c", "y"), route)


def projection_part(piece):
    copies = jnp.broadcast_to(piece[None], (8, BLOCK, HALF)).reshape(8 * BLOCK, HALF)
    return lax.all_to_all(copies, "y", 0, 0, tiled=True)


in_smem = pl.BlockSpec(memory_space=pltpu.SMEM)
in_vmem = pl.BlockSpec(memory_space=pltpu.VMEM)


def partial_values(core, near, far, weight):
    return pl.pallas_call(
        partial_values_kernel,
        in_specs=[in_smem, in_vmem, in_vmem, in_vmem],
        out_specs=in_vmem,
        out_shape=jax.ShapeDtypeStruct((8 * BLOCK, HALF), jnp.bfloat16),
        compiler_params=params,
        name="partial_values",
    )(core, near, far, weight)


def exchange_packed(value_parts, values):
    received = [shift(value_parts[SPAN - distance], -distance) for distance in (1, 2, 3)]
    packed = pl.pallas_call(
        pack_kernel,
        out_shape=jax.ShapeDtypeStruct((8 * BLOCK, 2 * HALF), jnp.bfloat16),
        compiler_params=params,
        name="pack",
    )(value_parts[SPAN], *received, values)
    return lax.all_to_all(packed, ("x", "c"), 0, 0, tiled=True)


def group_product(core, near, far, packed):
    rows = pl.BlockSpec((4 * BLOCK, HALF), lambda part: (0, part))
    return pl.pallas_call(
        product_kernel,
        grid=(QUARTER // HALF,),
        in_specs=[in_smem, rows, rows, pl.BlockSpec((8 * BLOCK, 2 * HALF), lambda part: (0, 0))],
        out_specs=pl.BlockSpec((HALF, HALF), lambda part: (part, 0)),
        out_shape=jax.ShapeDtypeStruct((QUARTER, HALF), jnp.bfloat16),
        compiler_params=params,
        name="group_product",
    )(core, near, far, packed)


def plane_route():
    route = []
    for x in range(4):
        for z in range(8):
            for c in range(2):
                for y in range(8):
                    source = ((x * 8 + z) * 2 + c) * 8 + y
                    target = (((y % 4) * 8 + z) * 2 + c) * 8 + 2 * x + y // 4
                    route.append((source, target))
    return route


def whole_shard(piece):
    rows, columns = piece.shape
    copies = jnp.broadcast_to(piece[None], (32, rows, columns)).reshape(32 * rows, columns)
    half = lax.all_to_all(copies, ("x", "z"), 0, 0, tiled=True)
    other = lax.ppermute(half, "c", OTHER_CORE)
    first = lax.axis_index("c") == 0
    return jnp.concatenate(
        [jnp.where(first, half, other), jnp.where(first, other, half)], axis=1
    )


def per_device(queries, key_rows, out_grad, inputs, w_value, doc_pos):
    queries, keys, grads, rows = queries[0], key_rows[0], out_grad[0], inputs[0]
    core = lax.axis_index("c").astype(jnp.int32).reshape(1)
    key_span = span_of(keys)
    near = exchange_rows(rows)
    weight = projection_piece(w_value)
    weights, *value_parts = attention_weights(doc_pos, queries, grads, key_span)
    near, weight, value_parts = lax.optimization_barrier((near, weight, value_parts))

    far = lax.ppermute(near, "c", OTHER_CORE)
    values = partial_values(core, near, far, projection_part(weight))
    packed = exchange_packed(value_parts, values)
    product = group_product(core, near, far, packed)
    pieces = lax.all_to_all(product, ("y", "z"), 0, 0, tiled=True)

    parts = packed.reshape(4, 2, BLOCK, 2 * HALF)[..., HALF:].astype(jnp.float32)
    values = jnp.sum(parts, axis=0).astype(jnp.bfloat16)
    values = jnp.concatenate([values[0], values[1]], axis=1)
    value_span = span_of(values)
    pieces, value_span = lax.optimization_barrier((pieces, value_span))
    key_parts = key_gradient(weights, queries, grads, value_span)

    pieces = pieces.reshape(64, -1, HALF).astype(jnp.float32)
    token_total = lax.axis_size(("x", "z", "c", "y")) * BLOCK
    piece = (jnp.sum(pieces, axis=0) * (1.0 / math.sqrt(token_total))).astype(jnp.bfloat16)
    piece = lax.ppermute(piece, ("x", "z", "c", "y"), plane_route())
    piece, key_parts = lax.optimization_barrier((piece, key_parts))
    weight_grad = whole_shard(piece)
    key_grad = owed(key_parts)
    return (key_grad[None], weight_grad)


def solution(mesh):
    mesh = Mesh(mesh.devices.reshape(4, 8, 2, 8), ("x", "z", "c", "y"))
    tokens = P("y", DP, None)
    return jax.shard_map(
        per_device,
        mesh=mesh,
        in_specs=(tokens, tokens, tokens, tokens, P("y", None), P("y", DP)),
        out_specs=(tokens, P("y", None)),
        check_vma=False,
    )
```

```python
import math

import jax
import jax.numpy as jnp
from jax import lax
from jax.experimental import pallas as pl
from jax.experimental.pallas import tpu as pltpu
from jax.sharding import Mesh, PartitionSpec as P

KEY_HEADS = 4
GROUP_WIDTH = 8
HEAD_SIZE = 128
SPAN = 3
BLOCK = 128
PAIR = 2 * HEAD_SIZE
GROUP_COLUMNS = GROUP_WIDTH * HEAD_SIZE
SPAN_ROWS = (SPAN + 1) * BLOCK

DP = ("x", "z", "c")
OTHER_CORE = [(0, 1), (1, 0)]
QUARTER = 1024
HALF = 256
masked_value = -1e30
NT = (((1,), (1,)), ((), ()))


def shift(block, distance, parities=(0, 1)):
    devices = range(lax.axis_size(DP))
    route = [(i, i + distance) for i in devices if i + distance in devices and i % 2 in parities]
    return lax.ppermute(block, DP, route)


def swap(block):
    return lax.ppermute(block, "c", OTHER_CORE)


def from_earlier(block):
    two = shift(block, 2)
    three = shift(block, 3, (1,))
    one = shift(block, 1, (0,))
    return one, two, three, swap(two)


def to_earlier(parts, even):
    third, second, first, _ = parts
    from_three = shift(third, -3, (0,))
    across = swap(first)
    across_third = shift(third, -1, (1,))
    joined = second.astype(jnp.float32) + jnp.where(even, across_third, across).astype(jnp.float32)
    from_two = shift(joined.astype(jnp.bfloat16), -2)
    return from_two, across, from_three


def span_rows(core_ref, own_ref, one_ref, two_ref, three_ref, swapped_ref):
    even = core_ref[0] == 0
    third = jnp.where(even, three_ref[...], swapped_ref[...])
    first = jnp.where(even, swapped_ref[...], one_ref[...])
    return jnp.concatenate([third, two_ref[...], first, own_ref[...]], axis=0)


def stacked(ref, pair):
    first = ref[:, pair * PAIR : pair * PAIR + HEAD_SIZE]
    second = ref[:, pair * PAIR + HEAD_SIZE : (pair + 1) * PAIR]
    return jnp.concatenate([first, second], axis=0)


def weights_kernel(core_ref, position_ref, query_ref, grad_ref, *refs):
    keys_down = lax.broadcasted_iota(jnp.int32, (SPAN_ROWS, BLOCK), 0)
    queries_across = lax.broadcasted_iota(jnp.int32, (SPAN_ROWS, BLOCK), 1)
    offset = SPAN * BLOCK + queries_across - keys_down
    allowed = (offset >= 0) & (offset <= position_ref[...])
    mask = jnp.where(allowed, 0.0, masked_value).astype(jnp.bfloat16)
    key_refs, weights_ref, out_refs = refs[:5], refs[5], refs[6:]
    keys = jnp.concatenate([span_rows(core_ref, *key_refs), mask], axis=1)
    unit = (
        lax.broadcasted_iota(jnp.int32, (PAIR, BLOCK), 0) % BLOCK
        == lax.broadcasted_iota(jnp.int32, (PAIR, BLOCK), 1)
    )
    unit = jnp.where(unit, 1.0, 0.0).astype(jnp.bfloat16)
    score_scale = 1.0 / math.sqrt(HEAD_SIZE)
    total = jnp.zeros((SPAN_ROWS, HEAD_SIZE), jnp.float32)
    for pair in range(GROUP_WIDTH // 2):
        heads = jnp.concatenate([stacked(query_ref, pair), unit], axis=1)
        scores = lax.dot_general(keys, heads, NT, preferred_element_type=jnp.float32)
        top = jnp.max(scores, axis=0, keepdims=True)
        weights = jnp.exp((scores - top) * score_scale)
        weights = weights * (1.0 / jnp.sum(weights, axis=0, keepdims=True))
        low = weights.astype(jnp.bfloat16)
        weights_ref[0, :, pair * PAIR : (pair + 1) * PAIR] = low
        total += jnp.dot(low, stacked(grad_ref, pair), preferred_element_type=jnp.float32)
    for block, out_ref in enumerate(out_refs):
        out_ref[...] = total[block * BLOCK : (block + 1) * BLOCK].astype(out_ref.dtype)


def scores_kernel(core_ref, weights_ref, query_ref, grad_ref, *refs):
    value_refs, out_refs = refs[:5], refs[5:]
    values = span_rows(core_ref, *value_refs)
    total = jnp.zeros((SPAN_ROWS, HEAD_SIZE), jnp.float32)
    for pair in range(GROUP_WIDTH // 2):
        prob_grad = lax.dot_general(
            values, stacked(grad_ref, pair), NT, preferred_element_type=jnp.float32
        )
        weights = weights_ref[0, :, pair * PAIR : (pair + 1) * PAIR].astype(jnp.float32)
        row_delta = jnp.sum(weights * prob_grad, axis=0, keepdims=True)
        low = (weights * (prob_grad - row_delta)).astype(jnp.bfloat16)
        total += jnp.dot(low, stacked(query_ref, pair), preferred_element_type=jnp.float32)
    total = total * (1.0 / math.sqrt(HEAD_SIZE))
    for block, out_ref in enumerate(out_refs):
        out_ref[...] = total[block * BLOCK : (block + 1) * BLOCK].astype(out_ref.dtype)


in_smem = pl.BlockSpec(memory_space=pltpu.SMEM)
in_vmem = pl.BlockSpec(memory_space=pltpu.VMEM)
wide = pl.BlockSpec((BLOCK, GROUP_COLUMNS), lambda g: (0, g))
narrow = pl.BlockSpec((BLOCK, HEAD_SIZE), lambda g: (0, g))
held = pl.BlockSpec((1, SPAN_ROWS, GROUP_COLUMNS), lambda g: (g, 0, 0))
gradients = [
    jax.ShapeDtypeStruct((BLOCK, KEY_HEADS * HEAD_SIZE), kind)
    for kind in (jnp.bfloat16, jnp.bfloat16, jnp.bfloat16, jnp.float32)
]
KERNEL_FLOPS = 2 * 2 * SPAN_ROWS * BLOCK * KEY_HEADS * GROUP_COLUMNS
params = pltpu.CompilerParams(vmem_limit_bytes=16 * 1024 * 1024)


def in_hbm(array):
    return pltpu.with_memory_space_constraint(array, pltpu.HBM)


def attention_weights(core, position, queries, grads, keys):
    return pl.pallas_call(
        weights_kernel,
        grid=(KEY_HEADS,),
        in_specs=[in_smem, pl.BlockSpec((1, BLOCK), lambda g: (0, 0)), wide, wide] + [narrow] * 5,
        out_specs=[held] + [narrow] * 4,
        out_shape=[pltpu.HBM((KEY_HEADS, SPAN_ROWS, GROUP_COLUMNS), jnp.bfloat16)] + gradients,
        compiler_params=params,
        cost_estimate=pl.CostEstimate(
            flops=2 * KERNEL_FLOPS, bytes_accessed=8 << 20, transcendentals=SPAN_ROWS * BLOCK * 32
        ),
        name="attention_weights",
    )(core, position, in_hbm(queries), in_hbm(grads), *keys)


def key_gradient(core, weights, queries, grads, values):
    return pl.pallas_call(
        scores_kernel,
        grid=(KEY_HEADS,),
        in_specs=[in_smem, held, wide, wide] + [narrow] * 5,
        out_specs=[narrow] * 4,
        out_shape=gradients,
        compiler_params=params,
        cost_estimate=pl.CostEstimate(
            flops=2 * KERNEL_FLOPS, bytes_accessed=8 << 20, transcendentals=0
        ),
        name="key_gradient",
    )(core, in_hbm(weights), in_hbm(queries), in_hbm(grads), *values)


def quarters_kernel(rows_ref, out_ref, sems):
    copies = [
        pltpu.make_async_copy(
            rows_ref.at[:, pl.ds(x * QUARTER, QUARTER)],
            out_ref.at[pl.ds(x * BLOCK, BLOCK), :],
            sems.at[x],
        )
        for x in range(4)
    ]
    for copy in copies:
        copy.start()
    for copy in copies:
        copy.wait()


def partial_values_kernel(core_ref, near_ref, far_ref, weight_ref, out_ref):
    for rows_ref, core in ((near_ref, core_ref[0]), (far_ref, 1 - core_ref[0])):
        values = jnp.dot(rows_ref[...], weight_ref[...], preferred_element_type=jnp.float32)
        values = values.astype(jnp.bfloat16)
        for x in range(4):
            rows = pl.ds(pl.multiple_of((2 * x + core) * BLOCK, BLOCK), BLOCK)
            out_ref[rows, :] = values[x * BLOCK : (x + 1) * BLOCK]


def pack_kernel(core_ref, own_ref, two_ref, across_ref, three_ref, values_ref, out_ref):
    last = jnp.where(core_ref[0] == 0, across_ref[...], three_ref[...])
    total = own_ref[...] + two_ref[...].astype(jnp.float32) + last.astype(jnp.float32)
    low = total.astype(jnp.bfloat16)
    for device in range(8):
        core = device % 2
        rows = slice(device * BLOCK, (device + 1) * BLOCK)
        out_ref[rows, :HALF] = low[:, core * HALF : (core + 1) * HALF]
        out_ref[rows, HALF:] = values_ref[rows, :]


def product_kernel(core_ref, near_ref, far_ref, grads_ref, out_ref):
    total = None
    for rows_ref, core in ((near_ref, core_ref[0]), (far_ref, 1 - core_ref[0])):
        grads = [
            grads_ref[pl.ds(pl.multiple_of((2 * x + core) * BLOCK, BLOCK), BLOCK), :HALF]
            for x in range(4)
        ]
        part = lax.dot_general(
            jnp.concatenate(grads, axis=0),
            rows_ref[...],
            (((0,), (0,)), ((), ())),
            preferred_element_type=jnp.float32,
        )
        total = part if total is None else total + part
    out_ref[...] = total.T.astype(jnp.bfloat16)


def exchange_rows(rows):
    quarters = pl.pallas_call(
        quarters_kernel,
        in_specs=[pl.BlockSpec(memory_space=pl.ANY)],
        out_specs=pl.BlockSpec(memory_space=pl.ANY),
        out_shape=jax.ShapeDtypeStruct((4 * BLOCK, QUARTER), jnp.bfloat16),
        scratch_shapes=[pltpu.SemaphoreType.DMA((4,))],
        compiler_params=params,
        name="quarters",
    )(in_hbm(rows))
    return lax.all_to_all(quarters, "x", 0, 0, tiled=True)


def projection_piece(w_value):
    route = [(target, source) for source, target in plane_route()]
    start = (lax.axis_index("x") * BLOCK, lax.axis_index("c") * HALF)
    piece = lax.dynamic_slice(w_value, start, (BLOCK, HALF))
    return lax.ppermute(piece, ("x", "z", "c", "y"), route)


def projection_part(piece):
    copies = jnp.broadcast_to(piece[None], (8, BLOCK, HALF)).reshape(8 * BLOCK, HALF)
    return lax.all_to_all(copies, "y", 0, 0, tiled=True)


def partial_values(core, near, far, weight):
    return pl.pallas_call(
        partial_values_kernel,
        in_specs=[in_smem, in_vmem, in_vmem, in_vmem],
        out_specs=in_vmem,
        out_shape=jax.ShapeDtypeStruct((8 * BLOCK, HALF), jnp.bfloat16),
        compiler_params=params,
        name="partial_values",
    )(core, near, far, weight)


def exchange_packed(core, own, received, values):
    packed = pl.pallas_call(
        pack_kernel,
        in_specs=[in_smem] + [in_vmem] * 5,
        out_specs=in_vmem,
        out_shape=jax.ShapeDtypeStruct((8 * BLOCK, 2 * HALF), jnp.bfloat16),
        compiler_params=params,
        name="pack",
    )(core, own, *received, values)
    return lax.all_to_all(packed, ("x", "c"), 0, 0, tiled=True)


def group_product(core, near, far, packed):
    rows = pl.BlockSpec((4 * BLOCK, HALF), lambda part: (0, part))
    return pl.pallas_call(
        product_kernel,
        grid=(QUARTER // HALF,),
        in_specs=[in_smem, rows, rows, pl.BlockSpec((8 * BLOCK, 2 * HALF), lambda part: (0, 0))],
        out_specs=pl.BlockSpec((HALF, HALF), lambda part: (part, 0)),
        out_shape=jax.ShapeDtypeStruct((QUARTER, HALF), jnp.bfloat16),
        compiler_params=params,
        name="group_product",
    )(core, near, far, packed)


def plane_route():
    route = []
    for x in range(4):
        for z in range(8):
            for c in range(2):
                for y in range(8):
                    source = ((x * 8 + z) * 2 + c) * 8 + y
                    target = (((y % 4) * 8 + z) * 2 + c) * 8 + 2 * x + y // 4
                    route.append((source, target))
    return route


def whole_shard(piece):
    rows, columns = piece.shape
    copies = jnp.broadcast_to(piece[None], (32, rows, columns)).reshape(32 * rows, columns)
    half = lax.all_to_all(copies, ("x", "z"), 0, 0, tiled=True)
    other = swap(half)
    first = lax.axis_index("c") == 0
    return jnp.concatenate(
        [jnp.where(first, half, other), jnp.where(first, other, half)], axis=1
    )


def per_device(queries, key_rows, out_grad, inputs, w_value, doc_pos):
    queries, keys, grads, rows = queries[0], key_rows[0], out_grad[0], inputs[0]
    core = lax.axis_index("c").astype(jnp.int32).reshape(1)
    even = core[0] == 0
    key_blocks = from_earlier(keys)
    near = exchange_rows(rows)
    weight = projection_piece(w_value)
    weights, *value_parts = attention_weights(core, doc_pos, queries, grads, (keys,) + key_blocks)
    near, weight, value_parts = lax.optimization_barrier((near, weight, value_parts))

    received = to_earlier(value_parts, even)
    far = swap(near)
    values = partial_values(core, near, far, projection_part(weight))
    packed = exchange_packed(core, value_parts[SPAN], received, values)
    product = group_product(core, near, far, packed)
    pieces = lax.all_to_all(product, ("y", "z"), 0, 0, tiled=True)

    parts = packed.reshape(4, 2, BLOCK, 2 * HALF)[..., HALF:].astype(jnp.float32)
    values = jnp.sum(parts, axis=0).astype(jnp.bfloat16)
    values = jnp.concatenate([values[0], values[1]], axis=1)
    value_blocks = from_earlier(values)
    pieces, value_blocks = lax.optimization_barrier((pieces, value_blocks))
    key_parts = key_gradient(core, weights, queries, grads, (values,) + value_blocks)

    pieces = pieces.reshape(64, -1, HALF).astype(jnp.float32)
    token_total = lax.axis_size(("x", "z", "c", "y")) * BLOCK
    piece = (jnp.sum(pieces, axis=0) * (1.0 / math.sqrt(token_total))).astype(jnp.bfloat16)
    piece = lax.ppermute(piece, ("x", "z", "c", "y"), plane_route())
    piece, key_parts = lax.optimization_barrier((piece, key_parts))
    weight_grad = whole_shard(piece)
    two, across, three = to_earlier(key_parts, even)
    key_grad = key_parts[SPAN] + two.astype(jnp.float32)
    key_grad = key_grad + jnp.where(even, across, three).astype(jnp.float32)
    return (key_grad.astype(jnp.bfloat16)[None], weight_grad)


def solution(mesh):
    mesh = Mesh(mesh.devices.reshape(4, 8, 2, 8), ("x", "z", "c", "y"))
    tokens = P("y", DP, None)
    return jax.shard_map(
        per_device,
        mesh=mesh,
        in_specs=(tokens, tokens, tokens, tokens, P("y", None), P("y", DP)),
        out_specs=(tokens, P("y", None)),
        check_vma=False,
    )
```

```python
import math

import jax
import jax.numpy as jnp
from jax import lax
from jax.experimental import pallas as pl
from jax.experimental.pallas import tpu as pltpu
from jax.sharding import Mesh, PartitionSpec as P

GROUP_WIDTH = 8
HEAD_SIZE = 128
SPAN = 3
BLOCK = 128
PAIR = 2 * HEAD_SIZE
GROUP_COLUMNS = GROUP_WIDTH * HEAD_SIZE
SPAN_ROWS = (SPAN + 1) * BLOCK
HEADS = 2
QUARTER = 1024
HALF = 256

DP = ("x", "z", "c")
ALL = ("x", "z", "c", "y")
OTHER_CORE = [(0, 1), (1, 0)]
masked_value = -1e30
NT = (((1,), (1,)), ((), ()))
TN = (((0,), (0,)), ((), ()))


def shift(block, chips):
    devices = range(lax.axis_size(DP))
    route = [(i, i + 2 * chips) for i in devices if i + 2 * chips in devices]
    return lax.ppermute(block, DP, route)


def swap(block):
    return lax.ppermute(block, "c", OTHER_CORE)


def plane_route():
    route = []
    for x in range(4):
        for z in range(8):
            for c in range(2):
                for y in range(8):
                    source = ((x * 8 + z) * 2 + c) * 8 + y
                    target = (((y % 4) * 8 + z) * 2 + c) * 8 + 2 * x + y // 4
                    route.append((source, target))
    return route


def in_hbm(array):
    return pltpu.with_memory_space_constraint(array, pltpu.HBM)


def span_blocks(chip_blocks):
    return shift(chip_blocks[BLOCK:], 2), shift(chip_blocks, 1), chip_blocks


def stacked(ref, pair):
    first = ref[:, pair * PAIR : pair * PAIR + HEAD_SIZE]
    second = ref[:, pair * PAIR + HEAD_SIZE : (pair + 1) * PAIR]
    return jnp.concatenate([first, second], axis=0)


def rows_at(block, count):
    return pl.ds(pl.multiple_of(block * BLOCK, BLOCK), count * BLOCK)


def store_gradients(total, out_refs):
    start = 0
    for out_ref in out_refs:
        rows = out_ref.shape[0]
        out_ref[...] = total[start : start + rows, :].astype(out_ref.dtype)
        start += rows


def weights_kernel(
    core_ref, own_position, other_position, own_query, other_query, own_grad, other_grad, *refs
):
    key_refs, weights_ref, out_refs, span_ref, total_ref = refs[:3], refs[3], refs[4:7], refs[7], refs[8]
    start = 0
    for key_ref in key_refs:
        span_ref[start : start + key_ref.shape[0], :] = key_ref[...]
        start += key_ref.shape[0]
    total_ref[...] = jnp.zeros_like(total_ref)
    keys_down = lax.broadcasted_iota(jnp.int32, (SPAN_ROWS, BLOCK), 0)
    queries_across = lax.broadcasted_iota(jnp.int32, (SPAN_ROWS, BLOCK), 1)
    offset = SPAN * BLOCK + queries_across - keys_down
    unit = (
        lax.broadcasted_iota(jnp.int32, (PAIR, BLOCK), 0) % BLOCK
        == lax.broadcasted_iota(jnp.int32, (PAIR, BLOCK), 1)
    )
    unit = jnp.where(unit, 1.0, 0.0).astype(jnp.bfloat16)
    score_scale = 1.0 / math.sqrt(HEAD_SIZE)
    sides = (
        (core_ref[0], own_position, own_query, own_grad),
        (1 - core_ref[0], other_position, other_query, other_grad),
    )
    for side, (block, position_ref, query_ref, grad_ref) in enumerate(sides):
        allowed = (offset >= 0) & (offset <= position_ref[...])
        mask = jnp.where(allowed, 0.0, masked_value).astype(jnp.bfloat16)
        keys = jnp.concatenate([span_ref[rows_at(block, SPAN + 1), :], mask], axis=1)
        total = jnp.zeros((SPAN_ROWS, HEAD_SIZE), jnp.float32)
        for pair in range(GROUP_WIDTH // 2):
            heads = jnp.concatenate([stacked(query_ref, pair), unit], axis=1)
            scores = lax.dot_general(keys, heads, NT, preferred_element_type=jnp.float32)
            top = jnp.max(scores, axis=0, keepdims=True)
            weights = jnp.exp((scores - top) * score_scale)
            weights = weights * (1.0 / jnp.sum(weights, axis=0, keepdims=True))
            low = weights.astype(jnp.bfloat16)
            weights_ref[0, side, :, pair * PAIR : (pair + 1) * PAIR] = low
            total += jnp.dot(low, stacked(grad_ref, pair), preferred_element_type=jnp.float32)
        total_ref[rows_at(block, SPAN + 1), :] += total
    store_gradients(total_ref[...], out_refs)


def scores_kernel(core_ref, weights_ref, own_query, other_query, own_grad, other_grad, *refs):
    value_refs, out_refs, span_ref, total_ref = refs[:3], refs[3:6], refs[6], refs[7]
    start = 0
    for value_ref in value_refs:
        span_ref[start : start + value_ref.shape[0], :] = value_ref[...]
        start += value_ref.shape[0]
    total_ref[...] = jnp.zeros_like(total_ref)
    sides = ((core_ref[0], own_query, own_grad), (1 - core_ref[0], other_query, other_grad))
    for side, (block, query_ref, grad_ref) in enumerate(sides):
        values = span_ref[rows_at(block, SPAN + 1), :]
        total = jnp.zeros((SPAN_ROWS, HEAD_SIZE), jnp.float32)
        for pair in range(GROUP_WIDTH // 2):
            prob_grad = lax.dot_general(
                values, stacked(grad_ref, pair), NT, preferred_element_type=jnp.float32
            )
            weights = weights_ref[0, side, :, pair * PAIR : (pair + 1) * PAIR].astype(jnp.float32)
            row_delta = jnp.sum(weights * prob_grad, axis=0, keepdims=True)
            low = (weights * (prob_grad - row_delta)).astype(jnp.bfloat16)
            total += jnp.dot(low, stacked(query_ref, pair), preferred_element_type=jnp.float32)
        total_ref[rows_at(block, SPAN + 1), :] += total
    store_gradients(total_ref[...] * (1.0 / math.sqrt(HEAD_SIZE)), out_refs)


in_smem = pl.BlockSpec(memory_space=pltpu.SMEM)
in_vmem = pl.BlockSpec(memory_space=pltpu.VMEM)
wide = pl.BlockSpec((BLOCK, GROUP_COLUMNS), lambda g, core: (0, HEADS * core[0] + g))
held = pl.BlockSpec((1, 2, SPAN_ROWS, GROUP_COLUMNS), lambda g, core: (g, 0, 0, 0))
position_spec = pl.BlockSpec((1, BLOCK), lambda g, core: (0, 0))
span_specs = [
    pl.BlockSpec((rows, HEAD_SIZE), lambda g, core: (0, g)) for rows in (BLOCK, 2 * BLOCK, 2 * BLOCK)
]
gradients = [
    jax.ShapeDtypeStruct((rows, HALF), kind)
    for rows, kind in (
        (BLOCK, jnp.bfloat16),
        (2 * BLOCK, jnp.bfloat16),
        (2 * BLOCK, jnp.float32),
    )
]
span_scratch = [
    pltpu.VMEM((SPAN_ROWS + BLOCK, HEAD_SIZE), jnp.bfloat16),
    pltpu.VMEM((SPAN_ROWS + BLOCK, HEAD_SIZE), jnp.float32),
]
KERNEL_FLOPS = 2 * 2 * SPAN_ROWS * BLOCK * HEADS * 2 * GROUP_COLUMNS
params = pltpu.CompilerParams(vmem_limit_bytes=20 * 1024 * 1024)


def attention_weights(core, positions, queries, grads, keys):
    return pl.pallas_call(
        weights_kernel,
        grid_spec=pltpu.PrefetchScalarGridSpec(
            num_scalar_prefetch=1,
            grid=(HEADS,),
            in_specs=[position_spec] * 2 + [wide] * 4 + span_specs,
            out_specs=[held] + span_specs,
            scratch_shapes=span_scratch,
        ),
        out_shape=[pltpu.HBM((HEADS, 2, SPAN_ROWS, GROUP_COLUMNS), jnp.bfloat16)] + gradients,
        compiler_params=params,
        cost_estimate=pl.CostEstimate(
            flops=2 * KERNEL_FLOPS, bytes_accessed=8 << 20, transcendentals=SPAN_ROWS * BLOCK * 32
        ),
        name="attention_weights",
    )(core, *positions, *queries, *grads, *keys)


def key_gradient(core, weights, queries, grads, values):
    return pl.pallas_call(
        scores_kernel,
        grid_spec=pltpu.PrefetchScalarGridSpec(
            num_scalar_prefetch=1,
            grid=(HEADS,),
            in_specs=[held] + [wide] * 4 + span_specs,
            out_specs=span_specs,
            scratch_shapes=span_scratch,
        ),
        out_shape=gradients,
        compiler_params=params,
        cost_estimate=pl.CostEstimate(
            flops=2 * KERNEL_FLOPS, bytes_accessed=8 << 20, transcendentals=0
        ),
        name="key_gradient",
    )(core, in_hbm(weights), *queries, *grads, *values)


def quarters_kernel(rows_ref, out_ref, sems):
    copies = [
        pltpu.make_async_copy(
            rows_ref.at[:, pl.ds(x * QUARTER, QUARTER)],
            out_ref.at[pl.ds(x * BLOCK, BLOCK), :],
            sems.at[x],
        )
        for x in range(4)
    ]
    for copy in copies:
        copy.start()
    for copy in copies:
        copy.wait()


def join_kernel(core_ref, own_ref, other_ref, out_ref):
    core = core_ref[0]
    for ref, block in ((own_ref, core), (other_ref, 1 - core)):
        half = jnp.where(core == 0, ref[:, :HALF], ref[:, HALF:])
        out_ref[rows_at(block, 1), :] = half


def partial_values_kernel(core_ref, near_ref, far_ref, weight_ref, out_ref):
    for rows_ref, core in ((near_ref, core_ref[0]), (far_ref, 1 - core_ref[0])):
        values = jnp.dot(rows_ref[...], weight_ref[...], preferred_element_type=jnp.float32)
        values = values.astype(jnp.bfloat16)
        for x in range(4):
            out_ref[rows_at(2 * x + core, 1), :] = values[x * BLOCK : (x + 1) * BLOCK]


def pack_kernel(two_ref, one_ref, own_ref, values_ref, out_ref):
    total = own_ref[...] + one_ref[...].astype(jnp.float32)
    last = total[BLOCK:] + two_ref[...].astype(jnp.float32)
    low = jnp.concatenate([total[:BLOCK], last], axis=0).astype(jnp.bfloat16)
    for x in range(4):
        rows = slice(x * 2 * BLOCK, (x + 1) * 2 * BLOCK)
        out_ref[rows, :HALF] = low
        out_ref[rows, HALF:] = values_ref[rows, :]


def product_kernel(core_ref, near_ref, far_ref, grads_ref, out_ref):
    total = None
    for rows_ref, core in ((near_ref, core_ref[0]), (far_ref, 1 - core_ref[0])):
        grads = [grads_ref[rows_at(2 * x + core, 1), :HALF] for x in range(4)]
        part = lax.dot_general(
            jnp.concatenate(grads, axis=0), rows_ref[...], TN, preferred_element_type=jnp.float32
        )
        total = part if total is None else total + part
    out_ref[...] = total.T.astype(jnp.bfloat16)


def column_quarters(rows):
    return pl.pallas_call(
        quarters_kernel,
        in_specs=[pl.BlockSpec(memory_space=pl.ANY)],
        out_specs=pl.BlockSpec(memory_space=pl.ANY),
        out_shape=jax.ShapeDtypeStruct((4 * BLOCK, QUARTER), jnp.bfloat16),
        scratch_shapes=[pltpu.SemaphoreType.DMA((4,))],
        compiler_params=params,
        name="quarters",
    )(rows)


def join_halves(core, own, other):
    return pl.pallas_call(
        join_kernel,
        in_specs=[in_smem, in_vmem, in_vmem],
        out_specs=in_vmem,
        out_shape=jax.ShapeDtypeStruct((2 * BLOCK, HALF), jnp.bfloat16),
        compiler_params=params,
        name="join_halves",
    )(core, own, other)


def projection_piece(w_value):
    route = [(target, source) for source, target in plane_route()]
    start = (lax.axis_index("x") * BLOCK, lax.axis_index("c") * HALF)
    return lax.ppermute(lax.dynamic_slice(w_value, start, (BLOCK, HALF)), ALL, route)


def projection_part(piece):
    copies = jnp.broadcast_to(piece[None], (8, BLOCK, HALF)).reshape(8 * BLOCK, HALF)
    return lax.all_to_all(copies, "y", 0, 0, tiled=True)


def partial_values(core, near, far, weight):
    return pl.pallas_call(
        partial_values_kernel,
        in_specs=[in_smem, in_vmem, in_vmem, in_vmem],
        out_specs=in_vmem,
        out_shape=jax.ShapeDtypeStruct((8 * BLOCK, HALF), jnp.bfloat16),
        compiler_params=params,
        name="partial_values",
    )(core, near, far, weight)


def exchange_packed(two, one, own, values):
    packed = pl.pallas_call(
        pack_kernel,
        in_specs=[in_vmem] * 4,
        out_specs=in_vmem,
        out_shape=jax.ShapeDtypeStruct((8 * BLOCK, 2 * HALF), jnp.bfloat16),
        compiler_params=params,
        name="pack",
    )(two, one, own, values)
    return lax.all_to_all(packed, "x", 0, 0, tiled=True)


def group_product(core, near, far, packed):
    rows = pl.BlockSpec((4 * BLOCK, HALF), lambda part: (0, part))
    return pl.pallas_call(
        product_kernel,
        grid=(QUARTER // HALF,),
        in_specs=[in_smem, rows, rows, pl.BlockSpec((8 * BLOCK, 2 * HALF), lambda part: (0, 0))],
        out_specs=pl.BlockSpec((HALF, HALF), lambda part: (part, 0)),
        out_shape=jax.ShapeDtypeStruct((QUARTER, HALF), jnp.bfloat16),
        compiler_params=params,
        name="group_product",
    )(core, near, far, packed)


def whole_shard(piece, even):
    rows, columns = piece.shape
    copies = jnp.broadcast_to(piece[None], (32, rows, columns)).reshape(32 * rows, columns)
    half = lax.all_to_all(copies, ("x", "z"), 0, 0, tiled=True)
    return both_halves(half, swap(half), even)


def both_halves(half, other, even):
    return jnp.concatenate([jnp.where(even, half, other), jnp.where(even, other, half)], axis=1)


def per_device(queries, key_rows, out_grad, inputs, w_value, doc_pos):
    queries, keys, grads, rows = queries[0], key_rows[0], out_grad[0], inputs[0]
    core = lax.axis_index("c").astype(jnp.int32).reshape(1)
    even = core[0] == 0
    weight = projection_piece(w_value)
    other_keys = swap(keys)
    near = lax.all_to_all(column_quarters(rows), "x", 0, 0, tiled=True)
    both_queries = (in_hbm(queries), swap(queries))
    both_grads = (in_hbm(grads), swap(grads))
    positions = (doc_pos, swap(doc_pos))
    other_keys, weight = lax.optimization_barrier((other_keys, weight))
    key_span = span_blocks(join_halves(core, keys, other_keys))
    weights, *value_parts = attention_weights(core, positions, both_queries, both_grads, key_span)
    near, weight, value_parts = lax.optimization_barrier((near, weight, value_parts))

    two, one, own = value_parts
    two, one = shift(two, -2), shift(one, -1)
    far = swap(near)
    values = partial_values(core, near, far, projection_part(weight))
    packed = exchange_packed(two, one, own, values)
    product = group_product(core, near, far, packed)
    pieces = lax.all_to_all(product, ("y", "z"), 0, 0, tiled=True)

    parts = packed.reshape(4, 2 * BLOCK, 2 * HALF)[:, :, HALF:].astype(jnp.float32)
    value_span = span_blocks(jnp.sum(parts, axis=0).astype(jnp.bfloat16))
    pieces, value_span = lax.optimization_barrier((pieces, value_span))
    key_parts = key_gradient(core, weights, both_queries, both_grads, value_span)

    pieces = pieces.reshape(64, -1, HALF).astype(jnp.float32)
    token_total = lax.axis_size(ALL) * BLOCK
    piece = (jnp.sum(pieces, axis=0) * (1.0 / math.sqrt(token_total))).astype(jnp.bfloat16)
    piece = lax.ppermute(piece, ALL, plane_route())
    piece, key_parts = lax.optimization_barrier((piece, key_parts))
    weight_grad = whole_shard(piece, even)

    two, one, own = key_parts
    two, one = shift(two, -2).astype(jnp.float32), shift(one, -1).astype(jnp.float32)
    first = (own[:BLOCK] + one[:BLOCK]).astype(jnp.bfloat16)
    second = (own[BLOCK:] + one[BLOCK:] + two).astype(jnp.bfloat16)
    received = swap(jnp.where(even, second, first))
    key_grad = both_halves(jnp.where(even, first, second), received, even)
    return (key_grad[None], weight_grad)


def solution(mesh):
    mesh = Mesh(mesh.devices.reshape(4, 8, 2, 8), ("x", "z", "c", "y"))
    tokens = P("y", DP, None)
    return jax.shard_map(
        per_device,
        mesh=mesh,
        in_specs=(tokens, tokens, tokens, tokens, P("y", None), P("y", DP)),
        out_specs=(tokens, P("y", None)),
        check_vma=False,
    )
```

```python
import math

import jax
import jax.numpy as jnp
from jax import lax
from jax.experimental import pallas as pl
from jax.experimental.pallas import tpu as pltpu
from jax.sharding import Mesh, PartitionSpec as P

GROUP_WIDTH = 8
HEAD_SIZE = 128
SPAN = 3
BLOCK = 128
PAIR = 2 * HEAD_SIZE
GROUP_COLUMNS = GROUP_WIDTH * HEAD_SIZE
SPAN_ROWS = (SPAN + 1) * BLOCK
HEADS = 2
QUARTER = 1024
HALF = 256

DP = ("x", "z", "c")
ALL = ("x", "z", "c", "y")
OTHER_CORE = [(0, 1), (1, 0)]
masked_value = -1e30
NT = (((1,), (1,)), ((), ()))
TN = (((0,), (0,)), ((), ()))


def shift(block, chips):
    devices = range(lax.axis_size(DP))
    route = [(i, i + 2 * chips) for i in devices if i + 2 * chips in devices]
    return lax.ppermute(block, DP, route)


def swap(block):
    return lax.ppermute(block, "c", OTHER_CORE)


def plane_route():
    route = []
    for x in range(4):
        for z in range(8):
            for c in range(2):
                for y in range(8):
                    source = ((x * 8 + z) * 2 + c) * 8 + y
                    target = (((y % 4) * 8 + z) * 2 + c) * 8 + 2 * x + y // 4
                    route.append((source, target))
    return route


def in_hbm(array):
    return pltpu.with_memory_space_constraint(array, pltpu.HBM)


def span_blocks(chip_blocks):
    return shift(chip_blocks[BLOCK:], 2), shift(chip_blocks, 1), chip_blocks


def stacked(ref, pair):
    first = ref[:, pair * PAIR : pair * PAIR + HEAD_SIZE]
    second = ref[:, pair * PAIR + HEAD_SIZE : (pair + 1) * PAIR]
    return jnp.concatenate([first, second], axis=0)


def rows_at(block, count):
    return pl.ds(pl.multiple_of(block * BLOCK, BLOCK), count * BLOCK)


def store_gradients(total, out_refs):
    start = 0
    for out_ref in out_refs:
        rows = out_ref.shape[0]
        out_ref[...] = total[start : start + rows, :].astype(out_ref.dtype)
        start += rows


def weights_kernel(
    core_ref, own_position, other_position, own_query, other_query, own_grad, other_grad, *refs
):
    key_refs, weights_ref, out_refs, span_ref, total_ref = refs[:3], refs[3], refs[4:7], refs[7], refs[8]
    start = 0
    for key_ref in key_refs:
        span_ref[start : start + key_ref.shape[0], :] = key_ref[...]
        start += key_ref.shape[0]
    total_ref[...] = jnp.zeros_like(total_ref)
    keys_down = lax.broadcasted_iota(jnp.int32, (SPAN_ROWS, BLOCK), 0)
    queries_across = lax.broadcasted_iota(jnp.int32, (SPAN_ROWS, BLOCK), 1)
    offset = SPAN * BLOCK + queries_across - keys_down
    unit = (
        lax.broadcasted_iota(jnp.int32, (PAIR, BLOCK), 0) % BLOCK
        == lax.broadcasted_iota(jnp.int32, (PAIR, BLOCK), 1)
    )
    unit = jnp.where(unit, 1.0, 0.0).astype(jnp.bfloat16)
    score_scale = 1.0 / math.sqrt(HEAD_SIZE)
    sides = (
        (core_ref[0], own_position, own_query, own_grad),
        (1 - core_ref[0], other_position, other_query, other_grad),
    )
    for side, (block, position_ref, query_ref, grad_ref) in enumerate(sides):
        allowed = (offset >= 0) & (offset <= position_ref[...])
        mask = jnp.where(allowed, 0.0, masked_value).astype(jnp.bfloat16)
        keys = jnp.concatenate([span_ref[rows_at(block, SPAN + 1), :], mask], axis=1)
        total = jnp.zeros((SPAN_ROWS, HEAD_SIZE), jnp.float32)
        for pair in range(GROUP_WIDTH // 2):
            heads = jnp.concatenate([stacked(query_ref, pair), unit], axis=1)
            scores = lax.dot_general(keys, heads, NT, preferred_element_type=jnp.float32)
            top = jnp.max(scores, axis=0, keepdims=True)
            weights = jnp.exp((scores - top) * score_scale)
            weights = weights * (1.0 / jnp.sum(weights, axis=0, keepdims=True))
            low = weights.astype(jnp.bfloat16)
            weights_ref[0, side, :, pair * PAIR : (pair + 1) * PAIR] = low
            total += jnp.dot(low, stacked(grad_ref, pair), preferred_element_type=jnp.float32)
        total_ref[rows_at(block, SPAN + 1), :] += total
    store_gradients(total_ref[...], out_refs)


def scores_kernel(core_ref, weights_ref, own_query, other_query, own_grad, other_grad, *refs):
    value_refs, out_refs, span_ref, total_ref = refs[:3], refs[3:6], refs[6], refs[7]
    start = 0
    for value_ref in value_refs:
        span_ref[start : start + value_ref.shape[0], :] = value_ref[...]
        start += value_ref.shape[0]
    total_ref[...] = jnp.zeros_like(total_ref)
    sides = ((core_ref[0], own_query, own_grad), (1 - core_ref[0], other_query, other_grad))
    for side, (block, query_ref, grad_ref) in enumerate(sides):
        values = span_ref[rows_at(block, SPAN + 1), :]
        total = jnp.zeros((SPAN_ROWS, HEAD_SIZE), jnp.float32)
        for pair in range(GROUP_WIDTH // 2):
            prob_grad = lax.dot_general(
                values, stacked(grad_ref, pair), NT, preferred_element_type=jnp.float32
            )
            weights = weights_ref[0, side, :, pair * PAIR : (pair + 1) * PAIR].astype(jnp.float32)
            row_delta = jnp.sum(weights * prob_grad, axis=0, keepdims=True)
            low = (weights * (prob_grad - row_delta)).astype(jnp.bfloat16)
            total += jnp.dot(low, stacked(query_ref, pair), preferred_element_type=jnp.float32)
        total_ref[rows_at(block, SPAN + 1), :] += total
    store_gradients(total_ref[...] * (1.0 / math.sqrt(HEAD_SIZE)), out_refs)


in_smem = pl.BlockSpec(memory_space=pltpu.SMEM)
in_vmem = pl.BlockSpec(memory_space=pltpu.VMEM)
wide = pl.BlockSpec((BLOCK, GROUP_COLUMNS), lambda g, core: (0, HEADS * core[0] + g))
held = pl.BlockSpec((1, 2, SPAN_ROWS, GROUP_COLUMNS), lambda g, core: (g, 0, 0, 0))
position_spec = pl.BlockSpec((1, BLOCK), lambda g, core: (0, 0))
span_specs = [
    pl.BlockSpec((rows, HEAD_SIZE), lambda g, core: (0, g)) for rows in (BLOCK, 2 * BLOCK, 2 * BLOCK)
]
gradients = [
    jax.ShapeDtypeStruct((rows, HALF), kind)
    for rows, kind in (
        (BLOCK, jnp.bfloat16),
        (2 * BLOCK, jnp.bfloat16),
        (2 * BLOCK, jnp.float32),
    )
]
span_scratch = [
    pltpu.VMEM((SPAN_ROWS + BLOCK, HEAD_SIZE), jnp.bfloat16),
    pltpu.VMEM((SPAN_ROWS + BLOCK, HEAD_SIZE), jnp.float32),
]
KERNEL_FLOPS = 2 * 2 * SPAN_ROWS * BLOCK * HEADS * 2 * GROUP_COLUMNS
params = pltpu.CompilerParams(vmem_limit_bytes=20 * 1024 * 1024)


def attention_weights(core, positions, queries, grads, keys):
    return pl.pallas_call(
        weights_kernel,
        grid_spec=pltpu.PrefetchScalarGridSpec(
            num_scalar_prefetch=1,
            grid=(HEADS,),
            in_specs=[position_spec] * 2 + [wide] * 4 + span_specs,
            out_specs=[held] + span_specs,
            scratch_shapes=span_scratch,
        ),
        out_shape=[pltpu.HBM((HEADS, 2, SPAN_ROWS, GROUP_COLUMNS), jnp.bfloat16)] + gradients,
        compiler_params=params,
        cost_estimate=pl.CostEstimate(
            flops=2 * KERNEL_FLOPS, bytes_accessed=8 << 20, transcendentals=SPAN_ROWS * BLOCK * 32
        ),
        name="attention_weights",
    )(core, *positions, *queries, *grads, *keys)


def key_gradient(core, weights, queries, grads, values):
    return pl.pallas_call(
        scores_kernel,
        grid_spec=pltpu.PrefetchScalarGridSpec(
            num_scalar_prefetch=1,
            grid=(HEADS,),
            in_specs=[held] + [wide] * 4 + span_specs,
            out_specs=span_specs,
            scratch_shapes=span_scratch,
        ),
        out_shape=gradients,
        compiler_params=params,
        cost_estimate=pl.CostEstimate(
            flops=2 * KERNEL_FLOPS, bytes_accessed=8 << 20, transcendentals=0
        ),
        name="key_gradient",
    )(core, in_hbm(weights), *queries, *grads, *values)


def quarters_kernel(rows_ref, out_ref, sems):
    copies = [
        pltpu.make_async_copy(
            rows_ref.at[:, pl.ds(x * QUARTER, QUARTER)],
            out_ref.at[pl.ds(x * BLOCK, BLOCK), :],
            sems.at[x],
        )
        for x in range(4)
    ]
    for copy in copies:
        copy.start()
    for copy in copies:
        copy.wait()


def join_kernel(core_ref, own_ref, other_ref, out_ref):
    core = core_ref[0]
    for ref, block in ((own_ref, core), (other_ref, 1 - core)):
        half = jnp.where(core == 0, ref[:, :HALF], ref[:, HALF:])
        out_ref[rows_at(block, 1), :] = half


def partial_values_kernel(core_ref, near_ref, far_ref, weight_ref, out_ref):
    for rows_ref, core in ((near_ref, core_ref[0]), (far_ref, 1 - core_ref[0])):
        values = jnp.dot(rows_ref[...], weight_ref[...], preferred_element_type=jnp.float32)
        values = values.astype(jnp.bfloat16)
        for x in range(4):
            out_ref[rows_at(2 * x + core, 1), :] = values[x * BLOCK : (x + 1) * BLOCK]


def pack_kernel(two_ref, one_ref, own_ref, values_ref, out_ref):
    total = own_ref[...] + one_ref[...].astype(jnp.float32)
    last = total[BLOCK:] + two_ref[...].astype(jnp.float32)
    low = jnp.concatenate([total[:BLOCK], last], axis=0).astype(jnp.bfloat16)
    for x in range(4):
        rows = slice(x * 2 * BLOCK, (x + 1) * 2 * BLOCK)
        out_ref[rows, :HALF] = low
        out_ref[rows, HALF:] = values_ref[rows, :]


def product_kernel(core_ref, near_ref, far_ref, grads_ref, out_ref):
    total = None
    for rows_ref, core in ((near_ref, core_ref[0]), (far_ref, 1 - core_ref[0])):
        grads = [grads_ref[rows_at(2 * x + core, 1), :HALF] for x in range(4)]
        part = lax.dot_general(
            jnp.concatenate(grads, axis=0), rows_ref[...], TN, preferred_element_type=jnp.float32
        )
        total = part if total is None else total + part
    out_ref[...] = total.T.astype(jnp.bfloat16)


def column_quarters(rows):
    return pl.pallas_call(
        quarters_kernel,
        in_specs=[pl.BlockSpec(memory_space=pl.ANY)],
        out_specs=pl.BlockSpec(memory_space=pl.ANY),
        out_shape=jax.ShapeDtypeStruct((4 * BLOCK, QUARTER), jnp.bfloat16),
        scratch_shapes=[pltpu.SemaphoreType.DMA((4,))],
        compiler_params=params,
        name="quarters",
    )(rows)


def join_halves(core, own, other):
    return pl.pallas_call(
        join_kernel,
        in_specs=[in_smem, in_vmem, in_vmem],
        out_specs=in_vmem,
        out_shape=jax.ShapeDtypeStruct((2 * BLOCK, HALF), jnp.bfloat16),
        compiler_params=params,
        name="join_halves",
    )(core, own, other)


def projection_piece(w_value):
    route = [(target, source) for source, target in plane_route()]
    start = (lax.axis_index("x") * BLOCK, lax.axis_index("c") * HALF)
    return lax.ppermute(lax.dynamic_slice(w_value, start, (BLOCK, HALF)), ALL, route)


def projection_part(piece):
    copies = jnp.broadcast_to(piece[None], (8, BLOCK, HALF)).reshape(8 * BLOCK, HALF)
    return lax.all_to_all(copies, "y", 0, 0, tiled=True)


def partial_values(core, near, far, weight):
    return pl.pallas_call(
        partial_values_kernel,
        in_specs=[in_smem, in_vmem, in_vmem, in_vmem],
        out_specs=in_vmem,
        out_shape=jax.ShapeDtypeStruct((8 * BLOCK, HALF), jnp.bfloat16),
        compiler_params=params,
        name="partial_values",
    )(core, near, far, weight)


def exchange_packed(two, one, own, values):
    packed = pl.pallas_call(
        pack_kernel,
        in_specs=[in_vmem] * 4,
        out_specs=in_vmem,
        out_shape=jax.ShapeDtypeStruct((8 * BLOCK, 2 * HALF), jnp.bfloat16),
        compiler_params=params,
        name="pack",
    )(two, one, own, values)
    return lax.all_to_all(packed, "x", 0, 0, tiled=True)


def group_product(core, near, far, packed):
    rows = pl.BlockSpec((4 * BLOCK, HALF), lambda part: (0, part))
    return pl.pallas_call(
        product_kernel,
        grid=(QUARTER // HALF,),
        in_specs=[in_smem, rows, rows, pl.BlockSpec((8 * BLOCK, 2 * HALF), lambda part: (0, 0))],
        out_specs=pl.BlockSpec((HALF, HALF), lambda part: (part, 0)),
        out_shape=jax.ShapeDtypeStruct((QUARTER, HALF), jnp.bfloat16),
        compiler_params=params,
        name="group_product",
    )(core, near, far, packed)


def whole_shard(piece, even):
    rows, columns = piece.shape
    copies = jnp.broadcast_to(piece[None], (32, rows, columns)).reshape(32 * rows, columns)
    half = lax.all_to_all(copies, ("x", "z"), 0, 0, tiled=True)
    return both_halves(half, swap(half), even)


def both_halves(half, other, even):
    return jnp.concatenate([jnp.where(even, half, other), jnp.where(even, other, half)], axis=1)


def per_device(queries, key_rows, out_grad, inputs, w_value, doc_pos):
    queries, keys, grads, rows = queries[0], key_rows[0], out_grad[0], inputs[0]
    core = lax.axis_index("c").astype(jnp.int32).reshape(1)
    even = core[0] == 0
    weight = projection_piece(w_value)
    other_keys = swap(keys)
    others = (swap(queries), swap(grads), swap(doc_pos))
    quarters = column_quarters(rows)
    key_span = span_blocks(join_halves(core, keys, other_keys))
    weight, quarters, key_span, others = lax.optimization_barrier(
        (projection_part(weight), quarters, key_span, others)
    )
    near = lax.all_to_all(quarters, "x", 0, 0, tiled=True)
    both_queries, both_grads = (in_hbm(queries), others[0]), (in_hbm(grads), others[1])
    positions = (doc_pos, others[2])
    weights, *value_parts = attention_weights(core, positions, both_queries, both_grads, key_span)

    two, one, own = value_parts
    two, one = shift(two, -2), shift(one, -1)
    near, own = lax.optimization_barrier((near, own))
    far = swap(near)
    values = partial_values(core, near, far, weight)
    packed = exchange_packed(two, one, own, values)
    product = group_product(core, near, far, packed)
    parts = packed.reshape(4, 2 * BLOCK, 2 * HALF)[:, :, HALF:].astype(jnp.float32)
    value_span = span_blocks(jnp.sum(parts, axis=0).astype(jnp.bfloat16))
    product, value_span = lax.optimization_barrier((product, value_span))
    pieces = lax.all_to_all(product, ("y", "z"), 0, 0, tiled=True)
    key_parts = key_gradient(core, weights, both_queries, both_grads, value_span)
    pieces, key_parts = lax.optimization_barrier((pieces, key_parts))

    pieces = pieces.reshape(64, -1, HALF).astype(jnp.float32)
    token_total = lax.axis_size(ALL) * BLOCK
    piece = (jnp.sum(pieces, axis=0) * (1.0 / math.sqrt(token_total))).astype(jnp.bfloat16)
    piece = lax.ppermute(piece, ALL, plane_route())
    two, one, own = key_parts
    two, one = shift(two, -2), shift(one, -1)
    piece, two, one = lax.optimization_barrier((piece, two, one))
    weight_grad = whole_shard(piece, even)

    two, one = two.astype(jnp.float32), one.astype(jnp.float32)
    first = (own[:BLOCK] + one[:BLOCK]).astype(jnp.bfloat16)
    second = (own[BLOCK:] + one[BLOCK:] + two).astype(jnp.bfloat16)
    received = swap(jnp.where(even, second, first))
    key_grad = both_halves(jnp.where(even, first, second), received, even)
    return (key_grad[None], weight_grad)


def solution(mesh):
    mesh = Mesh(mesh.devices.reshape(4, 8, 2, 8), ("x", "z", "c", "y"))
    tokens = P("y", DP, None)
    return jax.shard_map(
        per_device,
        mesh=mesh,
        in_specs=(tokens, tokens, tokens, tokens, P("y", None), P("y", DP)),
        out_specs=(tokens, P("y", None)),
        check_vma=False,
    )
```

```python
import math

import jax
import jax.numpy as jnp
from jax import lax
from jax.experimental import pallas as pl
from jax.experimental.pallas import tpu as pltpu
from jax.sharding import Mesh, PartitionSpec as P

GROUP_WIDTH = 8
HEAD_SIZE = 128
SPAN = 3
BLOCK = 128
PAIR = 2 * HEAD_SIZE
GROUP_COLUMNS = GROUP_WIDTH * HEAD_SIZE
SPAN_ROWS = (SPAN + 1) * BLOCK
HEADS = 2
QUARTER = 1024
HALF = 256

DP = ("x", "z", "c")
ALL = ("x", "z", "c", "y")
OTHER_CORE = [(0, 1), (1, 0)]
masked_value = -1e30
NT = (((1,), (1,)), ((), ()))
TN = (((0,), (0,)), ((), ()))


def shift(block, chips):
    devices = range(lax.axis_size(DP))
    route = [(i, i + 2 * chips) for i in devices if i + 2 * chips in devices]
    return lax.ppermute(block, DP, route)


def swap(block):
    return lax.ppermute(block, "c", OTHER_CORE)


def plane_route():
    route = []
    for x in range(4):
        for z in range(8):
            for c in range(2):
                for y in range(8):
                    source = ((x * 8 + z) * 2 + c) * 8 + y
                    target = (((y % 4) * 8 + z) * 2 + c) * 8 + 2 * x + y // 4
                    route.append((source, target))
    return route


def in_hbm(array):
    return pltpu.with_memory_space_constraint(array, pltpu.HBM)


def span_blocks(chip_blocks):
    return shift(chip_blocks[BLOCK:], 2), shift(chip_blocks, 1), chip_blocks


def stacked(ref, pair):
    first = ref[:, pair * PAIR : pair * PAIR + HEAD_SIZE]
    second = ref[:, pair * PAIR + HEAD_SIZE : (pair + 1) * PAIR]
    return jnp.concatenate([first, second], axis=0)


def rows_at(block, count):
    return pl.ds(pl.multiple_of(block * BLOCK, BLOCK), count * BLOCK)


def store_gradients(total, out_refs):
    start = 0
    for out_ref in out_refs:
        rows = out_ref.shape[0]
        out_ref[...] = total[start : start + rows, :].astype(out_ref.dtype)
        start += rows


def weights_kernel(
    core_ref, own_position, other_position, own_query, other_query, own_grad, other_grad, *refs
):
    key_refs, weights_ref, out_refs, span_ref, total_ref = refs[:3], refs[3], refs[4:7], refs[7], refs[8]
    start = 0
    for key_ref in key_refs:
        span_ref[start : start + key_ref.shape[0], :] = key_ref[...]
        start += key_ref.shape[0]
    total_ref[...] = jnp.zeros_like(total_ref)
    keys_down = lax.broadcasted_iota(jnp.int32, (SPAN_ROWS, BLOCK), 0)
    queries_across = lax.broadcasted_iota(jnp.int32, (SPAN_ROWS, BLOCK), 1)
    offset = SPAN * BLOCK + queries_across - keys_down
    unit = (
        lax.broadcasted_iota(jnp.int32, (PAIR, BLOCK), 0) % BLOCK
        == lax.broadcasted_iota(jnp.int32, (PAIR, BLOCK), 1)
    )
    unit = jnp.where(unit, 1.0, 0.0).astype(jnp.bfloat16)
    score_scale = 1.0 / math.sqrt(HEAD_SIZE)
    sides = (
        (core_ref[0], own_position, own_query, own_grad),
        (1 - core_ref[0], other_position, other_query, other_grad),
    )
    for side, (block, position_ref, query_ref, grad_ref) in enumerate(sides):
        allowed = (offset >= 0) & (offset <= position_ref[...])
        mask = jnp.where(allowed, 0.0, masked_value).astype(jnp.bfloat16)
        keys = jnp.concatenate([span_ref[rows_at(block, SPAN + 1), :], mask], axis=1)
        total = jnp.zeros((SPAN_ROWS, HEAD_SIZE), jnp.float32)
        for pair in range(GROUP_WIDTH // 2):
            heads = jnp.concatenate([stacked(query_ref, pair), unit], axis=1)
            scores = lax.dot_general(keys, heads, NT, preferred_element_type=jnp.float32)
            top = jnp.max(scores, axis=0, keepdims=True)
            weights = jnp.exp((scores - top) * score_scale)
            weights = weights * (1.0 / jnp.sum(weights, axis=0, keepdims=True))
            low = weights.astype(jnp.bfloat16)
            weights_ref[0, side, :, pair * PAIR : (pair + 1) * PAIR] = low
            total += jnp.dot(low, stacked(grad_ref, pair), preferred_element_type=jnp.float32)
        total_ref[rows_at(block, SPAN + 1), :] += total
    store_gradients(total_ref[...], out_refs)


def scores_kernel(core_ref, weights_ref, own_query, other_query, own_grad, other_grad, *refs):
    value_refs, out_refs, span_ref, total_ref = refs[:3], refs[3:6], refs[6], refs[7]
    start = 0
    for value_ref in value_refs:
        span_ref[start : start + value_ref.shape[0], :] = value_ref[...]
        start += value_ref.shape[0]
    total_ref[...] = jnp.zeros_like(total_ref)
    sides = ((core_ref[0], own_query, own_grad), (1 - core_ref[0], other_query, other_grad))
    for side, (block, query_ref, grad_ref) in enumerate(sides):
        values = span_ref[rows_at(block, SPAN + 1), :]
        total = jnp.zeros((SPAN_ROWS, HEAD_SIZE), jnp.float32)
        for pair in range(GROUP_WIDTH // 2):
            prob_grad = lax.dot_general(
                values, stacked(grad_ref, pair), NT, preferred_element_type=jnp.float32
            )
            weights = weights_ref[0, side, :, pair * PAIR : (pair + 1) * PAIR].astype(jnp.float32)
            row_delta = jnp.sum(weights * prob_grad, axis=0, keepdims=True)
            low = (weights * (prob_grad - row_delta)).astype(jnp.bfloat16)
            total += jnp.dot(low, stacked(query_ref, pair), preferred_element_type=jnp.float32)
        total_ref[rows_at(block, SPAN + 1), :] += total
    store_gradients(total_ref[...] * (1.0 / math.sqrt(HEAD_SIZE)), out_refs)


in_smem = pl.BlockSpec(memory_space=pltpu.SMEM)
in_vmem = pl.BlockSpec(memory_space=pltpu.VMEM)
wide = pl.BlockSpec((BLOCK, GROUP_COLUMNS), lambda g, core: (0, HEADS * core[0] + g))
held = pl.BlockSpec((1, 2, SPAN_ROWS, GROUP_COLUMNS), lambda g, core: (g, 0, 0, 0))
position_spec = pl.BlockSpec((1, BLOCK), lambda g, core: (0, 0))
span_specs = [
    pl.BlockSpec((rows, HEAD_SIZE), lambda g, core: (0, g)) for rows in (BLOCK, 2 * BLOCK, 2 * BLOCK)
]
gradients = [
    jax.ShapeDtypeStruct((rows, HALF), kind)
    for rows, kind in (
        (BLOCK, jnp.bfloat16),
        (2 * BLOCK, jnp.bfloat16),
        (2 * BLOCK, jnp.float32),
    )
]
span_scratch = [
    pltpu.VMEM((SPAN_ROWS + BLOCK, HEAD_SIZE), jnp.bfloat16),
    pltpu.VMEM((SPAN_ROWS + BLOCK, HEAD_SIZE), jnp.float32),
]
KERNEL_FLOPS = 2 * 2 * SPAN_ROWS * BLOCK * HEADS * 2 * GROUP_COLUMNS
params = pltpu.CompilerParams(vmem_limit_bytes=20 * 1024 * 1024)


def attention_weights(core, positions, queries, grads, keys):
    return pl.pallas_call(
        weights_kernel,
        grid_spec=pltpu.PrefetchScalarGridSpec(
            num_scalar_prefetch=1,
            grid=(HEADS,),
            in_specs=[position_spec] * 2 + [wide] * 4 + span_specs,
            out_specs=[held] + span_specs,
            scratch_shapes=span_scratch,
        ),
        out_shape=[pltpu.HBM((HEADS, 2, SPAN_ROWS, GROUP_COLUMNS), jnp.bfloat16)] + gradients,
        compiler_params=params,
        cost_estimate=pl.CostEstimate(
            flops=2 * KERNEL_FLOPS, bytes_accessed=8 << 20, transcendentals=SPAN_ROWS * BLOCK * 32
        ),
        name="attention_weights",
    )(core, *positions, *queries, *grads, *keys)


def key_gradient(core, weights, queries, grads, values):
    return pl.pallas_call(
        scores_kernel,
        grid_spec=pltpu.PrefetchScalarGridSpec(
            num_scalar_prefetch=1,
            grid=(HEADS,),
            in_specs=[held] + [wide] * 4 + span_specs,
            out_specs=span_specs,
            scratch_shapes=span_scratch,
        ),
        out_shape=gradients,
        compiler_params=params,
        cost_estimate=pl.CostEstimate(
            flops=2 * KERNEL_FLOPS, bytes_accessed=8 << 20, transcendentals=0
        ),
        name="key_gradient",
    )(core, in_hbm(weights), *queries, *grads, *values)


def quarters_kernel(rows_ref, out_ref, sems):
    copies = [
        pltpu.make_async_copy(
            rows_ref.at[:, pl.ds(x * QUARTER, QUARTER)],
            out_ref.at[pl.ds(x * BLOCK, BLOCK), :],
            sems.at[x],
        )
        for x in range(4)
    ]
    for copy in copies:
        copy.start()
    for copy in copies:
        copy.wait()


def join_kernel(core_ref, own_ref, other_ref, out_ref):
    core = core_ref[0]
    for ref, block in ((own_ref, core), (other_ref, 1 - core)):
        half = jnp.where(core == 0, ref[:, :HALF], ref[:, HALF:])
        out_ref[rows_at(block, 1), :] = half


def pack_kernel(two_ref, one_ref, own_ref, out_ref):
    total = own_ref[...] + one_ref[...].astype(jnp.float32)
    last = total[BLOCK:] + two_ref[...].astype(jnp.float32)
    low = jnp.concatenate([total[:BLOCK], last], axis=0).astype(jnp.bfloat16)
    for x in range(4):
        out_ref[x * 2 * BLOCK : (x + 1) * 2 * BLOCK, :] = low


def product_kernel(core_ref, near_ref, far_ref, grads_ref, out_ref):
    total = None
    for rows_ref, core in ((near_ref, core_ref[0]), (far_ref, 1 - core_ref[0])):
        grads = [grads_ref[rows_at(2 * x + core, 1), :] for x in range(4)]
        part = lax.dot_general(
            jnp.concatenate(grads, axis=0), rows_ref[...], TN, preferred_element_type=jnp.float32
        )
        total = part if total is None else total + part
    out_ref[...] = total.T.astype(jnp.bfloat16)


def column_quarters(rows):
    return pl.pallas_call(
        quarters_kernel,
        in_specs=[pl.BlockSpec(memory_space=pl.ANY)],
        out_specs=pl.BlockSpec(memory_space=pl.ANY),
        out_shape=jax.ShapeDtypeStruct((4 * BLOCK, QUARTER), jnp.bfloat16),
        scratch_shapes=[pltpu.SemaphoreType.DMA((4,))],
        compiler_params=params,
        name="quarters",
    )(rows)


def join_halves(core, own, other):
    return pl.pallas_call(
        join_kernel,
        in_specs=[in_smem, in_vmem, in_vmem],
        out_specs=in_vmem,
        out_shape=jax.ShapeDtypeStruct((2 * BLOCK, HALF), jnp.bfloat16),
        compiler_params=params,
        name="join_halves",
    )(core, own, other)


def exchange_value_grad(two, one, own):
    packed = pl.pallas_call(
        pack_kernel,
        in_specs=[in_vmem] * 3,
        out_specs=in_vmem,
        out_shape=jax.ShapeDtypeStruct((8 * BLOCK, HALF), jnp.bfloat16),
        compiler_params=params,
        name="pack",
    )(two, one, own)
    return lax.all_to_all(packed, "x", 0, 0, tiled=True)


def group_product(core, near, far, value_grads):
    rows = pl.BlockSpec((4 * BLOCK, HALF), lambda part: (0, part))
    return pl.pallas_call(
        product_kernel,
        grid=(QUARTER // HALF,),
        in_specs=[in_smem, rows, rows, pl.BlockSpec((8 * BLOCK, HALF), lambda part: (0, 0))],
        out_specs=pl.BlockSpec((HALF, HALF), lambda part: (part, 0)),
        out_shape=jax.ShapeDtypeStruct((QUARTER, HALF), jnp.bfloat16),
        compiler_params=params,
        name="group_product",
    )(core, near, far, value_grads)


def whole_shard(piece, even):
    rows, columns = piece.shape
    copies = jnp.broadcast_to(piece[None], (32, rows, columns)).reshape(32 * rows, columns)
    half = lax.all_to_all(copies, ("x", "z"), 0, 0, tiled=True)
    return both_halves(half, swap(half), even)


def both_halves(half, other, even):
    return jnp.concatenate([jnp.where(even, half, other), jnp.where(even, other, half)], axis=1)


def per_device(queries, key_rows, out_grad, inputs, w_value, doc_pos):
    queries, keys, grads, rows = queries[0], key_rows[0], out_grad[0], inputs[0]
    core = lax.axis_index("c").astype(jnp.int32).reshape(1)
    even = core[0] == 0
    whole_weight = lax.all_gather(w_value, "y", axis=0, tiled=True)
    key_span = span_blocks(join_halves(core, keys, swap(keys)))
    others = (swap(queries), swap(grads), swap(doc_pos))
    quarters, key_span, others = lax.optimization_barrier((column_quarters(rows), key_span, others))
    near = lax.all_to_all(quarters, "x", 0, 0, tiled=True)
    both_queries, both_grads = (in_hbm(queries), others[0]), (in_hbm(grads), others[1])
    positions = (doc_pos, others[2])
    weights, *value_parts = attention_weights(core, positions, both_queries, both_grads, key_span)

    two, one, own = value_parts
    two, one = shift(two, -2), shift(one, -1)
    near, two, one = lax.optimization_barrier((near, two, one))
    far = swap(near)
    product = group_product(core, near, far, exchange_value_grad(two, one, own))
    rows, product = lax.optimization_barrier((rows, product))
    pieces = lax.all_to_all(product, ("y", "z"), 0, 0, tiled=True)

    values = jnp.dot(rows, whole_weight, preferred_element_type=jnp.float32).astype(jnp.bfloat16)
    value_span = span_blocks(join_halves(core, values, swap(values)))
    pieces, value_span = lax.optimization_barrier((pieces, value_span))
    key_parts = key_gradient(core, weights, both_queries, both_grads, value_span)

    pieces = pieces.reshape(64, -1, HALF).astype(jnp.float32)
    token_total = lax.axis_size(ALL) * BLOCK
    piece = (jnp.sum(pieces, axis=0) * (1.0 / math.sqrt(token_total))).astype(jnp.bfloat16)
    piece = lax.ppermute(piece, ALL, plane_route())
    piece, key_parts = lax.optimization_barrier((piece, key_parts))
    weight_grad = whole_shard(piece, even)

    two, one, own = key_parts
    two, one = shift(two, -2).astype(jnp.float32), shift(one, -1).astype(jnp.float32)
    first = (own[:BLOCK] + one[:BLOCK]).astype(jnp.bfloat16)
    second = (own[BLOCK:] + one[BLOCK:] + two).astype(jnp.bfloat16)
    received = swap(jnp.where(even, second, first))
    key_grad = both_halves(jnp.where(even, first, second), received, even)
    return (key_grad[None], weight_grad)


def solution(mesh):
    mesh = Mesh(mesh.devices.reshape(4, 8, 2, 8), ("x", "z", "c", "y"))
    tokens = P("y", DP, None)
    return jax.shard_map(
        per_device,
        mesh=mesh,
        in_specs=(tokens, tokens, tokens, tokens, P("y", None), P("y", DP)),
        out_specs=(tokens, P("y", None)),
        check_vma=False,
    )
```

```python
import math

import jax
import jax.numpy as jnp
from jax import lax
from jax.experimental import pallas as pl
from jax.experimental.pallas import tpu as pltpu
from jax.sharding import Mesh, PartitionSpec as P

KEY_HEADS = 4
GROUP_WIDTH = 8
HEAD_SIZE = 128
SPAN = 3
BLOCK = 128
PAIR = 2 * HEAD_SIZE
GROUP_COLUMNS = GROUP_WIDTH * HEAD_SIZE
SPAN_ROWS = (SPAN + 1) * BLOCK

DP = ("x", "z", "c")
OTHER_CORE = [(0, 1), (1, 0)]
QUARTER = 1024
HALF = 256
masked_value = -1e30
NT = (((1,), (1,)), ((), ()))


def shift(block, distance, parities=(0, 1)):
    devices = range(lax.axis_size(DP))
    route = [(i, i + distance) for i in devices if i + distance in devices and i % 2 in parities]
    return lax.ppermute(block, DP, route)


def swap(block):
    return lax.ppermute(block, "c", OTHER_CORE)


def from_earlier(block):
    two = shift(block, 2)
    three = shift(block, 3, (1,))
    one = shift(block, 1, (0,))
    return one, two, three, swap(two)


def to_earlier(parts, even):
    third, second, first, _ = parts
    from_three = shift(third, -3, (0,))
    across = swap(first)
    across_third = shift(third, -1, (1,))
    joined = second.astype(jnp.float32) + jnp.where(even, across_third, across).astype(jnp.float32)
    from_two = shift(joined.astype(jnp.bfloat16), -2)
    return from_two, across, from_three


def span_rows(core_ref, own_ref, one_ref, two_ref, three_ref, swapped_ref):
    even = core_ref[0] == 0
    third = jnp.where(even, three_ref[...], swapped_ref[...])
    first = jnp.where(even, swapped_ref[...], one_ref[...])
    return jnp.concatenate([third, two_ref[...], first, own_ref[...]], axis=0)


def stacked(ref, pair):
    first = ref[:, pair * PAIR : pair * PAIR + HEAD_SIZE]
    second = ref[:, pair * PAIR + HEAD_SIZE : (pair + 1) * PAIR]
    return jnp.concatenate([first, second], axis=0)


def weights_kernel(core_ref, position_ref, query_ref, grad_ref, *refs):
    keys_down = lax.broadcasted_iota(jnp.int32, (SPAN_ROWS, BLOCK), 0)
    queries_across = lax.broadcasted_iota(jnp.int32, (SPAN_ROWS, BLOCK), 1)
    offset = SPAN * BLOCK + queries_across - keys_down
    allowed = (offset >= 0) & (offset <= position_ref[...])
    mask = jnp.where(allowed, 0.0, masked_value).astype(jnp.bfloat16)
    key_refs, weights_ref, out_refs = refs[:5], refs[5], refs[6:]
    keys = jnp.concatenate([span_rows(core_ref, *key_refs), mask], axis=1)
    unit = (
        lax.broadcasted_iota(jnp.int32, (PAIR, BLOCK), 0) % BLOCK
        == lax.broadcasted_iota(jnp.int32, (PAIR, BLOCK), 1)
    )
    unit = jnp.where(unit, 1.0, 0.0).astype(jnp.bfloat16)
    score_scale = 1.0 / math.sqrt(HEAD_SIZE)
    total = jnp.zeros((SPAN_ROWS, HEAD_SIZE), jnp.float32)
    for pair in range(GROUP_WIDTH // 2):
        heads = jnp.concatenate([stacked(query_ref, pair), unit], axis=1)
        scores = lax.dot_general(keys, heads, NT, preferred_element_type=jnp.float32)
        top = jnp.max(scores, axis=0, keepdims=True)
        weights = jnp.exp((scores - top) * score_scale)
        weights = weights * (1.0 / jnp.sum(weights, axis=0, keepdims=True))
        low = weights.astype(jnp.bfloat16)
        weights_ref[0, :, pair * PAIR : (pair + 1) * PAIR] = low
        total += jnp.dot(low, stacked(grad_ref, pair), preferred_element_type=jnp.float32)
    for block, out_ref in enumerate(out_refs):
        out_ref[...] = total[block * BLOCK : (block + 1) * BLOCK].astype(out_ref.dtype)


def scores_kernel(core_ref, weights_ref, query_ref, grad_ref, *refs):
    value_refs, out_refs = refs[:5], refs[5:]
    values = span_rows(core_ref, *value_refs)
    total = jnp.zeros((SPAN_ROWS, HEAD_SIZE), jnp.float32)
    for pair in range(GROUP_WIDTH // 2):
        prob_grad = lax.dot_general(
            values, stacked(grad_ref, pair), NT, preferred_element_type=jnp.float32
        )
        weights = weights_ref[0, :, pair * PAIR : (pair + 1) * PAIR].astype(jnp.float32)
        row_delta = jnp.sum(weights * prob_grad, axis=0, keepdims=True)
        low = (weights * (prob_grad - row_delta)).astype(jnp.bfloat16)
        total += jnp.dot(low, stacked(query_ref, pair), preferred_element_type=jnp.float32)
    total = total * (1.0 / math.sqrt(HEAD_SIZE))
    for block, out_ref in enumerate(out_refs):
        out_ref[...] = total[block * BLOCK : (block + 1) * BLOCK].astype(out_ref.dtype)


in_smem = pl.BlockSpec(memory_space=pltpu.SMEM)
in_vmem = pl.BlockSpec(memory_space=pltpu.VMEM)
wide = pl.BlockSpec((BLOCK, GROUP_COLUMNS), lambda g: (0, g))
narrow = pl.BlockSpec((BLOCK, HEAD_SIZE), lambda g: (0, g))
held = pl.BlockSpec((1, SPAN_ROWS, GROUP_COLUMNS), lambda g: (g, 0, 0))
gradients = [
    jax.ShapeDtypeStruct((BLOCK, KEY_HEADS * HEAD_SIZE), kind)
    for kind in (jnp.bfloat16, jnp.bfloat16, jnp.bfloat16, jnp.float32)
]
KERNEL_FLOPS = 2 * 2 * SPAN_ROWS * BLOCK * KEY_HEADS * GROUP_COLUMNS
params = pltpu.CompilerParams(vmem_limit_bytes=16 * 1024 * 1024)


def in_hbm(array):
    return pltpu.with_memory_space_constraint(array, pltpu.HBM)


def attention_weights(core, position, queries, grads, keys):
    return pl.pallas_call(
        weights_kernel,
        grid=(KEY_HEADS,),
        in_specs=[in_smem, pl.BlockSpec((1, BLOCK), lambda g: (0, 0)), wide, wide] + [narrow] * 5,
        out_specs=[held] + [narrow] * 4,
        out_shape=[pltpu.HBM((KEY_HEADS, SPAN_ROWS, GROUP_COLUMNS), jnp.bfloat16)] + gradients,
        compiler_params=params,
        cost_estimate=pl.CostEstimate(
            flops=2 * KERNEL_FLOPS, bytes_accessed=8 << 20, transcendentals=SPAN_ROWS * BLOCK * 32
        ),
        name="attention_weights",
    )(core, position, in_hbm(queries), in_hbm(grads), *keys)


def key_gradient(core, weights, queries, grads, values):
    return pl.pallas_call(
        scores_kernel,
        grid=(KEY_HEADS,),
        in_specs=[in_smem, held, wide, wide] + [narrow] * 5,
        out_specs=[narrow] * 4,
        out_shape=gradients,
        compiler_params=params,
        cost_estimate=pl.CostEstimate(
            flops=2 * KERNEL_FLOPS, bytes_accessed=8 << 20, transcendentals=0
        ),
        name="key_gradient",
    )(core, in_hbm(weights), in_hbm(queries), in_hbm(grads), *values)


def quarters_kernel(rows_ref, out_ref, sems):
    copies = [
        pltpu.make_async_copy(
            rows_ref.at[:, pl.ds(x * QUARTER, QUARTER)],
            out_ref.at[pl.ds(x * BLOCK, BLOCK), :],
            sems.at[x],
        )
        for x in range(4)
    ]
    for copy in copies:
        copy.start()
    for copy in copies:
        copy.wait()


def pack_kernel(core_ref, own_ref, two_ref, across_ref, three_ref, out_ref):
    last = jnp.where(core_ref[0] == 0, across_ref[...], three_ref[...])
    total = own_ref[...] + two_ref[...].astype(jnp.float32) + last.astype(jnp.float32)
    low = total.astype(jnp.bfloat16)
    for device in range(8):
        core = device % 2
        rows = slice(device * BLOCK, (device + 1) * BLOCK)
        out_ref[rows, :] = low[:, core * HALF : (core + 1) * HALF]


def product_kernel(core_ref, near_ref, far_ref, grads_ref, out_ref):
    total = None
    for rows_ref, core in ((near_ref, core_ref[0]), (far_ref, 1 - core_ref[0])):
        grads = [
            grads_ref[pl.ds(pl.multiple_of((2 * x + core) * BLOCK, BLOCK), BLOCK), :]
            for x in range(4)
        ]
        part = lax.dot_general(
            jnp.concatenate(grads, axis=0),
            rows_ref[...],
            (((0,), (0,)), ((), ())),
            preferred_element_type=jnp.float32,
        )
        total = part if total is None else total + part
    out_ref[...] = total.T.astype(jnp.bfloat16)


def exchange_rows(rows):
    quarters = pl.pallas_call(
        quarters_kernel,
        in_specs=[pl.BlockSpec(memory_space=pl.ANY)],
        out_specs=pl.BlockSpec(memory_space=pl.ANY),
        out_shape=jax.ShapeDtypeStruct((4 * BLOCK, QUARTER), jnp.bfloat16),
        scratch_shapes=[pltpu.SemaphoreType.DMA((4,))],
        compiler_params=params,
        name="quarters",
    )(rows)
    return lax.all_to_all(quarters, "x", 0, 0, tiled=True)


def exchange_value_grad(core, own, received):
    packed = pl.pallas_call(
        pack_kernel,
        in_specs=[in_smem] + [in_vmem] * 4,
        out_specs=in_vmem,
        out_shape=jax.ShapeDtypeStruct((8 * BLOCK, HALF), jnp.bfloat16),
        compiler_params=params,
        name="pack",
    )(core, own, *received)
    return lax.all_to_all(packed, ("x", "c"), 0, 0, tiled=True)


def group_product(core, near, far, value_grads):
    rows = pl.BlockSpec((4 * BLOCK, HALF), lambda part: (0, part))
    return pl.pallas_call(
        product_kernel,
        grid=(QUARTER // HALF,),
        in_specs=[in_smem, rows, rows, pl.BlockSpec((8 * BLOCK, HALF), lambda part: (0, 0))],
        out_specs=pl.BlockSpec((HALF, HALF), lambda part: (part, 0)),
        out_shape=jax.ShapeDtypeStruct((QUARTER, HALF), jnp.bfloat16),
        compiler_params=params,
        name="group_product",
    )(core, near, far, value_grads)


def plane_route():
    route = []
    for x in range(4):
        for z in range(8):
            for c in range(2):
                for y in range(8):
                    source = ((x * 8 + z) * 2 + c) * 8 + y
                    target = (((y % 4) * 8 + z) * 2 + c) * 8 + 2 * x + y // 4
                    route.append((source, target))
    return route


def whole_shard(piece):
    rows, columns = piece.shape
    copies = jnp.broadcast_to(piece[None], (32, rows, columns)).reshape(32 * rows, columns)
    half = lax.all_to_all(copies, ("x", "z"), 0, 0, tiled=True)
    other = swap(half)
    first = lax.axis_index("c") == 0
    return jnp.concatenate(
        [jnp.where(first, half, other), jnp.where(first, other, half)], axis=1
    )


def per_device(queries, key_rows, out_grad, inputs, w_value, doc_pos):
    queries, keys, grads, rows = queries[0], key_rows[0], out_grad[0], inputs[0]
    core = lax.axis_index("c").astype(jnp.int32).reshape(1)
    even = core[0] == 0
    whole_weight = lax.all_gather(w_value, "y", axis=0, tiled=True)
    key_blocks = from_earlier(keys)
    near = exchange_rows(rows)
    weights, *value_parts = attention_weights(core, doc_pos, queries, grads, (keys,) + key_blocks)
    received = to_earlier(value_parts, even)
    near, received = lax.optimization_barrier((near, received))

    far = swap(near)
    value_grads = exchange_value_grad(core, value_parts[SPAN], received)
    values = jnp.dot(rows, whole_weight, preferred_element_type=jnp.float32).astype(jnp.bfloat16)
    value_blocks = from_earlier(values)
    value_grads, value_blocks = lax.optimization_barrier((value_grads, value_blocks))
    product = group_product(core, near, far, value_grads)
    pieces = lax.all_to_all(product, ("y", "z"), 0, 0, tiled=True)
    key_parts = key_gradient(core, weights, queries, grads, (values,) + value_blocks)
    two, across, three = to_earlier(key_parts, even)
    pieces, two, across, three = lax.optimization_barrier((pieces, two, across, three))

    pieces = pieces.reshape(64, -1, HALF).astype(jnp.float32)
    token_total = lax.axis_size(("x", "z", "c", "y")) * BLOCK
    piece = (jnp.sum(pieces, axis=0) * (1.0 / math.sqrt(token_total))).astype(jnp.bfloat16)
    piece = lax.ppermute(piece, ("x", "z", "c", "y"), plane_route())
    weight_grad = whole_shard(piece)
    key_grad = key_parts[SPAN] + two.astype(jnp.float32)
    key_grad = key_grad + jnp.where(even, across, three).astype(jnp.float32)
    return (key_grad.astype(jnp.bfloat16)[None], weight_grad)


def solution(mesh):
    mesh = Mesh(mesh.devices.reshape(4, 8, 2, 8), ("x", "z", "c", "y"))
    tokens = P("y", DP, None)
    return jax.shard_map(
        per_device,
        mesh=mesh,
        in_specs=(tokens, tokens, tokens, tokens, P("y", None), P("y", DP)),
        out_specs=(tokens, P("y", None)),
        check_vma=False,
    )
```

```python
import math

import jax
import jax.numpy as jnp
from jax import lax
from jax.experimental import pallas as pl
from jax.experimental.pallas import tpu as pltpu
from jax.sharding import Mesh, PartitionSpec as P

KEY_HEADS = 4
GROUP_WIDTH = 8
HEAD_SIZE = 128
SPAN = 3
BLOCK = 128
PAIR = 2 * HEAD_SIZE
GROUP_COLUMNS = GROUP_WIDTH * HEAD_SIZE
SPAN_ROWS = (SPAN + 1) * BLOCK

DP = ("x", "z", "c")
OTHER_CORE = [(0, 1), (1, 0)]
QUARTER = 1024
SHARD = 512
HALF = 256
masked_value = -1e30
NT = (((1,), (1,)), ((), ()))


def shift(block, distance, parities=(0, 1)):
    devices = range(lax.axis_size(DP))
    route = [(i, i + distance) for i in devices if i + distance in devices and i % 2 in parities]
    return lax.ppermute(block, DP, route)


def swap(block):
    return lax.ppermute(block, "c", OTHER_CORE)


def from_earlier(block):
    two = shift(block, 2)
    three = shift(block, 3, (1,))
    one = shift(block, 1, (0,))
    return one, two, three, swap(two)


def to_earlier(parts, even):
    third, second, first, _ = parts
    from_three = shift(third, -3, (0,))
    across = swap(first)
    across_third = shift(third, -1, (1,))
    joined = second.astype(jnp.float32) + jnp.where(even, across_third, across).astype(jnp.float32)
    from_two = shift(joined.astype(jnp.bfloat16), -2)
    return from_two, across, from_three


def span_rows(core_ref, own_ref, one_ref, two_ref, three_ref, swapped_ref):
    even = core_ref[0] == 0
    third = jnp.where(even, three_ref[...], swapped_ref[...])
    first = jnp.where(even, swapped_ref[...], one_ref[...])
    return jnp.concatenate([third, two_ref[...], first, own_ref[...]], axis=0)


def stacked(ref, pair):
    first = ref[:, pair * PAIR : pair * PAIR + HEAD_SIZE]
    second = ref[:, pair * PAIR + HEAD_SIZE : (pair + 1) * PAIR]
    return jnp.concatenate([first, second], axis=0)


def weights_kernel(core_ref, position_ref, query_ref, grad_ref, *refs):
    keys_down = lax.broadcasted_iota(jnp.int32, (SPAN_ROWS, BLOCK), 0)
    queries_across = lax.broadcasted_iota(jnp.int32, (SPAN_ROWS, BLOCK), 1)
    offset = SPAN * BLOCK + queries_across - keys_down
    allowed = (offset >= 0) & (offset <= position_ref[...])
    mask = jnp.where(allowed, 0.0, masked_value).astype(jnp.bfloat16)
    key_refs, weights_ref, out_refs = refs[:5], refs[5], refs[6:]
    keys = jnp.concatenate([span_rows(core_ref, *key_refs), mask], axis=1)
    unit = (
        lax.broadcasted_iota(jnp.int32, (PAIR, BLOCK), 0) % BLOCK
        == lax.broadcasted_iota(jnp.int32, (PAIR, BLOCK), 1)
    )
    unit = jnp.where(unit, 1.0, 0.0).astype(jnp.bfloat16)
    score_scale = 1.0 / math.sqrt(HEAD_SIZE)
    total = jnp.zeros((SPAN_ROWS, HEAD_SIZE), jnp.float32)
    for pair in range(GROUP_WIDTH // 2):
        heads = jnp.concatenate([stacked(query_ref, pair), unit], axis=1)
        scores = lax.dot_general(keys, heads, NT, preferred_element_type=jnp.float32)
        top = jnp.max(scores, axis=0, keepdims=True)
        weights = jnp.exp((scores - top) * score_scale)
        weights = weights * (1.0 / jnp.sum(weights, axis=0, keepdims=True))
        low = weights.astype(jnp.bfloat16)
        weights_ref[0, :, pair * PAIR : (pair + 1) * PAIR] = low
        total += jnp.dot(low, stacked(grad_ref, pair), preferred_element_type=jnp.float32)
    for block, out_ref in enumerate(out_refs):
        out_ref[...] = total[block * BLOCK : (block + 1) * BLOCK].astype(out_ref.dtype)


def scores_kernel(core_ref, weights_ref, query_ref, grad_ref, *refs):
    value_refs, out_refs = refs[:5], refs[5:]
    values = span_rows(core_ref, *value_refs)
    total = jnp.zeros((SPAN_ROWS, HEAD_SIZE), jnp.float32)
    for pair in range(GROUP_WIDTH // 2):
        prob_grad = lax.dot_general(
            values, stacked(grad_ref, pair), NT, preferred_element_type=jnp.float32
        )
        weights = weights_ref[0, :, pair * PAIR : (pair + 1) * PAIR].astype(jnp.float32)
        row_delta = jnp.sum(weights * prob_grad, axis=0, keepdims=True)
        low = (weights * (prob_grad - row_delta)).astype(jnp.bfloat16)
        total += jnp.dot(low, stacked(query_ref, pair), preferred_element_type=jnp.float32)
    total = total * (1.0 / math.sqrt(HEAD_SIZE))
    for block, out_ref in enumerate(out_refs):
        out_ref[...] = total[block * BLOCK : (block + 1) * BLOCK].astype(out_ref.dtype)


in_smem = pl.BlockSpec(memory_space=pltpu.SMEM)
in_vmem = pl.BlockSpec(memory_space=pltpu.VMEM)
wide = pl.BlockSpec((BLOCK, GROUP_COLUMNS), lambda g: (0, g))
narrow = pl.BlockSpec((BLOCK, HEAD_SIZE), lambda g: (0, g))
held = pl.BlockSpec((1, SPAN_ROWS, GROUP_COLUMNS), lambda g: (g, 0, 0))
gradients = [
    jax.ShapeDtypeStruct((BLOCK, KEY_HEADS * HEAD_SIZE), kind)
    for kind in (jnp.bfloat16, jnp.bfloat16, jnp.bfloat16, jnp.float32)
]
KERNEL_FLOPS = 2 * 2 * SPAN_ROWS * BLOCK * KEY_HEADS * GROUP_COLUMNS
params = pltpu.CompilerParams(vmem_limit_bytes=16 * 1024 * 1024)


def in_hbm(array):
    return pltpu.with_memory_space_constraint(array, pltpu.HBM)


def attention_weights(core, position, queries, grads, keys):
    return pl.pallas_call(
        weights_kernel,
        grid=(KEY_HEADS,),
        in_specs=[in_smem, pl.BlockSpec((1, BLOCK), lambda g: (0, 0)), wide, wide] + [narrow] * 5,
        out_specs=[held] + [narrow] * 4,
        out_shape=[pltpu.HBM((KEY_HEADS, SPAN_ROWS, GROUP_COLUMNS), jnp.bfloat16)] + gradients,
        compiler_params=params,
        cost_estimate=pl.CostEstimate(
            flops=2 * KERNEL_FLOPS, bytes_accessed=8 << 20, transcendentals=SPAN_ROWS * BLOCK * 32
        ),
        name="attention_weights",
    )(core, position, in_hbm(queries), in_hbm(grads), *keys)


def key_gradient(core, weights, queries, grads, values):
    return pl.pallas_call(
        scores_kernel,
        grid=(KEY_HEADS,),
        in_specs=[in_smem, held, wide, wide] + [narrow] * 5,
        out_specs=[narrow] * 4,
        out_shape=gradients,
        compiler_params=params,
        cost_estimate=pl.CostEstimate(
            flops=2 * KERNEL_FLOPS, bytes_accessed=8 << 20, transcendentals=0
        ),
        name="key_gradient",
    )(core, in_hbm(weights), in_hbm(queries), in_hbm(grads), *values)


def quarters_kernel(rows_ref, out_ref):
    for x in range(4):
        for shard in range(8):
            start = shard * SHARD + x * BLOCK
            out_ref[x * BLOCK : (x + 1) * BLOCK, shard * BLOCK : (shard + 1) * BLOCK] = rows_ref[
                :, start : start + BLOCK
            ]


def partial_values_kernel(core_ref, near_ref, far_ref, weight_ref, out_ref):
    for rows_ref, core in ((near_ref, core_ref[0]), (far_ref, 1 - core_ref[0])):
        values = jnp.dot(rows_ref[...], weight_ref[...], preferred_element_type=jnp.float32)
        values = values.astype(jnp.bfloat16)
        for x in range(4):
            rows = pl.ds(pl.multiple_of((2 * x + core) * BLOCK, BLOCK), BLOCK)
            out_ref[rows, :] = values[x * BLOCK : (x + 1) * BLOCK]


def pack_kernel(core_ref, own_ref, two_ref, across_ref, three_ref, values_ref, out_ref):
    last = jnp.where(core_ref[0] == 0, across_ref[...], three_ref[...])
    total = own_ref[...] + two_ref[...].astype(jnp.float32) + last.astype(jnp.float32)
    low = total.astype(jnp.bfloat16)
    for device in range(8):
        core = device % 2
        rows = slice(device * BLOCK, (device + 1) * BLOCK)
        out_ref[rows, :HALF] = low[:, core * HALF : (core + 1) * HALF]
        out_ref[rows, HALF:] = values_ref[rows, :]


def product_kernel(core_ref, near_ref, far_ref, grads_ref, out_ref):
    total = None
    for rows_ref, core in ((near_ref, core_ref[0]), (far_ref, 1 - core_ref[0])):
        grads = [
            grads_ref[pl.ds(pl.multiple_of((2 * x + core) * BLOCK, BLOCK), BLOCK), :HALF]
            for x in range(4)
        ]
        part = lax.dot_general(
            jnp.concatenate(grads, axis=0),
            rows_ref[...],
            (((0,), (0,)), ((), ())),
            preferred_element_type=jnp.float32,
        )
        total = part if total is None else total + part
    out_ref[...] = total.T.astype(jnp.bfloat16)


def exchange_rows(rows):
    quarters = pl.pallas_call(
        quarters_kernel,
        in_specs=[in_vmem],
        out_specs=in_vmem,
        out_shape=jax.ShapeDtypeStruct((4 * BLOCK, QUARTER), jnp.bfloat16),
        compiler_params=params,
        name="quarters",
    )(rows)
    return lax.all_to_all(quarters, "x", 0, 0, tiled=True)


def projection_part(w_value):
    start = (lax.axis_index("x") * BLOCK, lax.axis_index("c") * HALF)
    return lax.dynamic_slice(w_value, start, (BLOCK, HALF))


def gathered_over_y(piece):
    copies = jnp.broadcast_to(piece[None], (8, BLOCK, HALF)).reshape(8 * BLOCK, HALF)
    return lax.all_to_all(copies, "y", 0, 0, tiled=True)


def partial_values(core, near, far, weight):
    return pl.pallas_call(
        partial_values_kernel,
        in_specs=[in_smem, in_vmem, in_vmem, in_vmem],
        out_specs=in_vmem,
        out_shape=jax.ShapeDtypeStruct((8 * BLOCK, HALF), jnp.bfloat16),
        compiler_params=params,
        name="partial_values",
    )(core, near, far, weight)


def exchange_packed(core, own, received, values):
    packed = pl.pallas_call(
        pack_kernel,
        in_specs=[in_smem] + [in_vmem] * 5,
        out_specs=in_vmem,
        out_shape=jax.ShapeDtypeStruct((8 * BLOCK, 2 * HALF), jnp.bfloat16),
        compiler_params=params,
        name="pack",
    )(core, own, *received, values)
    return lax.all_to_all(packed, ("x", "c"), 0, 0, tiled=True)


def group_product(core, near, far, packed):
    rows = pl.BlockSpec((4 * BLOCK, HALF), lambda part: (0, part))
    return pl.pallas_call(
        product_kernel,
        grid=(QUARTER // HALF,),
        in_specs=[in_smem, rows, rows, pl.BlockSpec((8 * BLOCK, 2 * HALF), lambda part: (0, 0))],
        out_specs=pl.BlockSpec((HALF, HALF), lambda part: (part, 0)),
        out_shape=jax.ShapeDtypeStruct((QUARTER, HALF), jnp.bfloat16),
        compiler_params=params,
        name="group_product",
    )(core, near, far, packed)


def whole_shard(piece):
    rows, columns = piece.shape
    copies = jnp.broadcast_to(piece[None], (32, rows, columns)).reshape(32 * rows, columns)
    half = lax.all_to_all(copies, ("x", "z"), 0, 0, tiled=True)
    other = swap(half)
    first = lax.axis_index("c") == 0
    return jnp.concatenate(
        [jnp.where(first, half, other), jnp.where(first, other, half)], axis=1
    )


def per_device(queries, key_rows, out_grad, inputs, w_value, doc_pos):
    queries, keys, grads, rows = queries[0], key_rows[0], out_grad[0], inputs[0]
    core = lax.axis_index("c").astype(jnp.int32).reshape(1)
    even = core[0] == 0
    key_blocks = from_earlier(keys)
    near = exchange_rows(rows)
    piece = projection_part(w_value)
    weights, *value_parts = attention_weights(core, doc_pos, queries, grads, (keys,) + key_blocks)
    near, piece, value_parts = lax.optimization_barrier((near, piece, value_parts))

    received = to_earlier(value_parts, even)
    far = swap(near)
    values = partial_values(core, near, far, gathered_over_y(piece))
    packed = exchange_packed(core, value_parts[SPAN], received, values)
    product = group_product(core, near, far, packed)
    pieces = lax.all_to_all(product, ("y", "z"), 0, 0, tiled=True)

    parts = packed.reshape(4, 2, BLOCK, 2 * HALF)[..., HALF:].astype(jnp.float32)
    values = jnp.sum(parts, axis=0).astype(jnp.bfloat16)
    values = jnp.concatenate([values[0], values[1]], axis=1)
    value_blocks = from_earlier(values)
    pieces, value_blocks = lax.optimization_barrier((pieces, value_blocks))
    key_parts = key_gradient(core, weights, queries, grads, (values,) + value_blocks)

    pieces = pieces.reshape(64, -1, HALF).astype(jnp.float32)
    token_total = lax.axis_size(("x", "z", "c", "y")) * BLOCK
    piece = (jnp.sum(pieces, axis=0) * (1.0 / math.sqrt(token_total))).astype(jnp.bfloat16)
    weight_grad = whole_shard(piece)
    two, across, three = to_earlier(key_parts, even)
    key_grad = key_parts[SPAN] + two.astype(jnp.float32)
    key_grad = key_grad + jnp.where(even, across, three).astype(jnp.float32)
    return (key_grad.astype(jnp.bfloat16)[None], weight_grad)


def solution(mesh):
    mesh = Mesh(mesh.devices.reshape(4, 8, 2, 8), ("x", "z", "c", "y"))
    tokens = P("y", DP, None)
    return jax.shard_map(
        per_device,
        mesh=mesh,
        in_specs=(tokens, tokens, tokens, tokens, P("y", None), P("y", DP)),
        out_specs=(tokens, P("y", None)),
        check_vma=False,
    )
```

```python
import math

import jax
import jax.numpy as jnp
from jax import lax
from jax.experimental import pallas as pl
from jax.experimental.pallas import tpu as pltpu
from jax.sharding import Mesh, PartitionSpec as P

KEY_HEADS = 4
GROUP_WIDTH = 8
HEAD_SIZE = 128
SPAN = 3
BLOCK = 128
PAIR = 2 * HEAD_SIZE
GROUP_COLUMNS = GROUP_WIDTH * HEAD_SIZE
SPAN_ROWS = (SPAN + 1) * BLOCK

DP = ("x", "z", "c")
OTHER_CORE = [(0, 1), (1, 0)]
QUARTER = 1024
SHARD = 512
HALF = 256
masked_value = -1e30
NT = (((1,), (1,)), ((), ()))


def shift(block, distance, parities=(0, 1)):
    devices = range(lax.axis_size(DP))
    route = [(i, i + distance) for i in devices if i + distance in devices and i % 2 in parities]
    return lax.ppermute(block, DP, route)


def swap(block):
    return lax.ppermute(block, "c", OTHER_CORE)


def from_earlier(block):
    two = shift(block, 2)
    three = shift(block, 3, (1,))
    one = shift(block, 1, (0,))
    return one, two, three, swap(two)


def to_earlier(parts, even):
    third, second, first, _ = parts
    from_three = shift(third, -3, (0,))
    across = swap(first)
    across_third = shift(third, -1, (1,))
    joined = second.astype(jnp.float32) + jnp.where(even, across_third, across).astype(jnp.float32)
    from_two = shift(joined.astype(jnp.bfloat16), -2)
    return from_two, across, from_three


def span_rows(core_ref, own_ref, one_ref, two_ref, three_ref, swapped_ref):
    even = core_ref[0] == 0
    third = jnp.where(even, three_ref[...], swapped_ref[...])
    first = jnp.where(even, swapped_ref[...], one_ref[...])
    return jnp.concatenate([third, two_ref[...], first, own_ref[...]], axis=0)


def stacked(ref, pair):
    first = ref[:, pair * PAIR : pair * PAIR + HEAD_SIZE]
    second = ref[:, pair * PAIR + HEAD_SIZE : (pair + 1) * PAIR]
    return jnp.concatenate([first, second], axis=0)


def weights_kernel(core_ref, position_ref, query_ref, grad_ref, *refs):
    keys_down = lax.broadcasted_iota(jnp.int32, (SPAN_ROWS, BLOCK), 0)
    queries_across = lax.broadcasted_iota(jnp.int32, (SPAN_ROWS, BLOCK), 1)
    offset = SPAN * BLOCK + queries_across - keys_down
    allowed = (offset >= 0) & (offset <= position_ref[...])
    mask = jnp.where(allowed, 0.0, masked_value).astype(jnp.bfloat16)
    key_refs, weights_ref, out_refs = refs[:5], refs[5], refs[6:]
    keys = jnp.concatenate([span_rows(core_ref, *key_refs), mask], axis=1)
    unit = (
        lax.broadcasted_iota(jnp.int32, (PAIR, BLOCK), 0) % BLOCK
        == lax.broadcasted_iota(jnp.int32, (PAIR, BLOCK), 1)
    )
    unit = jnp.where(unit, 1.0, 0.0).astype(jnp.bfloat16)
    score_scale = math.log2(math.e) / math.sqrt(HEAD_SIZE)
    total = jnp.zeros((SPAN_ROWS, HEAD_SIZE), jnp.float32)
    for pair in range(GROUP_WIDTH // 2):
        heads = jnp.concatenate([stacked(query_ref, pair), unit], axis=1)
        scores = lax.dot_general(keys, heads, NT, preferred_element_type=jnp.float32)
        top = jnp.max(scores, axis=0, keepdims=True)
        weights = jnp.exp2((scores - top) * score_scale)
        weights = weights * (1.0 / jnp.sum(weights, axis=0, keepdims=True))
        low = weights.astype(jnp.bfloat16)
        weights_ref[0, :, pair * PAIR : (pair + 1) * PAIR] = low
        total += jnp.dot(low, stacked(grad_ref, pair), preferred_element_type=jnp.float32)
    for block, out_ref in enumerate(out_refs):
        out_ref[...] = total[block * BLOCK : (block + 1) * BLOCK].astype(out_ref.dtype)


def scores_kernel(core_ref, weights_ref, query_ref, grad_ref, *refs):
    value_refs, out_refs = refs[:5], refs[5:]
    values = span_rows(core_ref, *value_refs)
    total = jnp.zeros((SPAN_ROWS, HEAD_SIZE), jnp.float32)
    for pair in range(GROUP_WIDTH // 2):
        prob_grad = lax.dot_general(
            values, stacked(grad_ref, pair), NT, preferred_element_type=jnp.float32
        )
        weights = weights_ref[0, :, pair * PAIR : (pair + 1) * PAIR].astype(jnp.float32)
        row_delta = jnp.sum(weights * prob_grad, axis=0, keepdims=True)
        low = (weights * (prob_grad - row_delta)).astype(jnp.bfloat16)
        total += jnp.dot(low, stacked(query_ref, pair), preferred_element_type=jnp.float32)
    total = total * (1.0 / math.sqrt(HEAD_SIZE))
    for block, out_ref in enumerate(out_refs):
        out_ref[...] = total[block * BLOCK : (block + 1) * BLOCK].astype(out_ref.dtype)


in_smem = pl.BlockSpec(memory_space=pltpu.SMEM)
in_vmem = pl.BlockSpec(memory_space=pltpu.VMEM)
wide = pl.BlockSpec((BLOCK, GROUP_COLUMNS), lambda g: (0, g))
narrow = pl.BlockSpec((BLOCK, HEAD_SIZE), lambda g: (0, g))
held = pl.BlockSpec((1, SPAN_ROWS, GROUP_COLUMNS), lambda g: (g, 0, 0))
gradients = [
    jax.ShapeDtypeStruct((BLOCK, KEY_HEADS * HEAD_SIZE), kind)
    for kind in (jnp.bfloat16, jnp.bfloat16, jnp.bfloat16, jnp.float32)
]
KERNEL_FLOPS = 2 * 2 * SPAN_ROWS * BLOCK * KEY_HEADS * GROUP_COLUMNS
params = pltpu.CompilerParams(vmem_limit_bytes=16 * 1024 * 1024)


def in_hbm(array):
    return pltpu.with_memory_space_constraint(array, pltpu.HBM)


def attention_weights(core, position, queries, grads, keys):
    return pl.pallas_call(
        weights_kernel,
        grid=(KEY_HEADS,),
        in_specs=[in_smem, pl.BlockSpec((1, BLOCK), lambda g: (0, 0)), wide, wide] + [narrow] * 5,
        out_specs=[held] + [narrow] * 4,
        out_shape=[pltpu.HBM((KEY_HEADS, SPAN_ROWS, GROUP_COLUMNS), jnp.bfloat16)] + gradients,
        compiler_params=params,
        cost_estimate=pl.CostEstimate(
            flops=2 * KERNEL_FLOPS, bytes_accessed=8 << 20, transcendentals=SPAN_ROWS * BLOCK * 32
        ),
        name="attention_weights",
    )(core, position, in_hbm(queries), in_hbm(grads), *keys)


def key_gradient(core, weights, queries, grads, values):
    return pl.pallas_call(
        scores_kernel,
        grid=(KEY_HEADS,),
        in_specs=[in_smem, held, wide, wide] + [narrow] * 5,
        out_specs=[narrow] * 4,
        out_shape=gradients,
        compiler_params=params,
        cost_estimate=pl.CostEstimate(
            flops=2 * KERNEL_FLOPS, bytes_accessed=8 << 20, transcendentals=0
        ),
        name="key_gradient",
    )(core, in_hbm(weights), in_hbm(queries), in_hbm(grads), *values)


def quarters_kernel(rows_ref, out_ref):
    for x in range(4):
        for shard in range(8):
            start = shard * SHARD + x * BLOCK
            out_ref[x * BLOCK : (x + 1) * BLOCK, shard * BLOCK : (shard + 1) * BLOCK] = rows_ref[
                :, start : start + BLOCK
            ]


def partial_values_kernel(core_ref, near_ref, far_ref, weight_ref, out_ref):
    for rows_ref, core in ((near_ref, core_ref[0]), (far_ref, 1 - core_ref[0])):
        values = jnp.dot(rows_ref[...], weight_ref[...], preferred_element_type=jnp.float32)
        values = values.astype(jnp.bfloat16)
        for x in range(4):
            rows = pl.ds(pl.multiple_of((2 * x + core) * BLOCK, BLOCK), BLOCK)
            out_ref[rows, :] = values[x * BLOCK : (x + 1) * BLOCK]


def pack_kernel(core_ref, own_ref, two_ref, across_ref, three_ref, values_ref, out_ref):
    last = jnp.where(core_ref[0] == 0, across_ref[...], three_ref[...])
    total = own_ref[...] + two_ref[...].astype(jnp.float32) + last.astype(jnp.float32)
    low = total.astype(jnp.bfloat16)
    for device in range(8):
        core = device % 2
        rows = slice(device * BLOCK, (device + 1) * BLOCK)
        out_ref[rows, :HALF] = low[:, core * HALF : (core + 1) * HALF]
        out_ref[rows, HALF:] = values_ref[rows, :]


def product_kernel(core_ref, near_ref, far_ref, grads_ref, out_ref):
    total = None
    for rows_ref, core in ((near_ref, core_ref[0]), (far_ref, 1 - core_ref[0])):
        grads = [
            grads_ref[pl.ds(pl.multiple_of((2 * x + core) * BLOCK, BLOCK), BLOCK), :HALF]
            for x in range(4)
        ]
        part = lax.dot_general(
            jnp.concatenate(grads, axis=0),
            rows_ref[...],
            (((0,), (0,)), ((), ())),
            preferred_element_type=jnp.float32,
        )
        total = part if total is None else total + part
    out_ref[...] = total.T.astype(jnp.bfloat16)


def exchange_rows(rows):
    quarters = pl.pallas_call(
        quarters_kernel,
        in_specs=[in_vmem],
        out_specs=in_vmem,
        out_shape=jax.ShapeDtypeStruct((4 * BLOCK, QUARTER), jnp.bfloat16),
        compiler_params=params,
        name="quarters",
    )(rows)
    return lax.all_to_all(quarters, "x", 0, 0, tiled=True)


def projection_part(w_value):
    start = (lax.axis_index("x") * BLOCK, lax.axis_index("c") * HALF)
    piece = lax.dynamic_slice(w_value, start, (BLOCK, HALF))
    return jnp.broadcast_to(piece[None], (8, BLOCK, HALF)).reshape(8 * BLOCK, HALF)


def partial_values(core, near, far, weight):
    return pl.pallas_call(
        partial_values_kernel,
        in_specs=[in_smem, in_vmem, in_vmem, in_vmem],
        out_specs=in_vmem,
        out_shape=jax.ShapeDtypeStruct((8 * BLOCK, HALF), jnp.bfloat16),
        compiler_params=params,
        name="partial_values",
    )(core, near, far, weight)


def exchange_packed(core, own, received, values):
    packed = pl.pallas_call(
        pack_kernel,
        in_specs=[in_smem] + [in_vmem] * 5,
        out_specs=in_vmem,
        out_shape=jax.ShapeDtypeStruct((8 * BLOCK, 2 * HALF), jnp.bfloat16),
        compiler_params=params,
        name="pack",
    )(core, own, *received, values)
    return lax.all_to_all(packed, ("x", "c"), 0, 0, tiled=True)


def group_product(core, near, far, packed):
    rows = pl.BlockSpec((4 * BLOCK, HALF), lambda part: (0, part))
    return pl.pallas_call(
        product_kernel,
        grid=(QUARTER // HALF,),
        in_specs=[in_smem, rows, rows, pl.BlockSpec((8 * BLOCK, 2 * HALF), lambda part: (0, 0))],
        out_specs=pl.BlockSpec((HALF, HALF), lambda part: (part, 0)),
        out_shape=pltpu.HBM((QUARTER, HALF), jnp.bfloat16),
        compiler_params=params,
        name="group_product",
    )(core, near, far, packed)


def whole_shard(piece):
    rows, columns = piece.shape
    copies = jnp.broadcast_to(piece[None], (32, rows, columns)).reshape(32 * rows, columns)
    half = lax.all_to_all(copies, ("x", "z"), 0, 0, tiled=True)
    other = swap(half)
    first = lax.axis_index("c") == 0
    return jnp.concatenate(
        [jnp.where(first, half, other), jnp.where(first, other, half)], axis=1
    )


def per_device(queries, key_rows, out_grad, inputs, w_value, doc_pos):
    queries, keys, grads, rows = queries[0], key_rows[0], out_grad[0], inputs[0]
    core = lax.axis_index("c").astype(jnp.int32).reshape(1)
    even = core[0] == 0
    key_blocks = from_earlier(keys)
    near = exchange_rows(rows)
    near, piece, key_blocks = lax.optimization_barrier((near, projection_part(w_value), key_blocks))
    part = lax.all_to_all(piece, "y", 0, 0, tiled=True)
    weights, *value_parts = attention_weights(core, doc_pos, queries, grads, (keys,) + key_blocks)

    received = to_earlier(value_parts, even)
    far = swap(near)
    values = partial_values(core, near, far, part)
    packed = exchange_packed(core, value_parts[SPAN], received, values)
    product = group_product(core, near, far, packed)
    pieces = lax.all_to_all(product, ("y", "z"), 0, 0, tiled=True)

    parts = packed.reshape(4, 2, BLOCK, 2 * HALF)[..., HALF:].astype(jnp.float32)
    values = jnp.sum(parts, axis=0).astype(jnp.bfloat16)
    values = jnp.concatenate([values[0], values[1]], axis=1)
    value_blocks = from_earlier(values)
    pieces, value_blocks = lax.optimization_barrier((pieces, value_blocks))
    key_parts = key_gradient(core, weights, queries, grads, (values,) + value_blocks)

    pieces = pieces.reshape(64, -1, HALF).astype(jnp.float32)
    token_total = lax.axis_size(("x", "z", "c", "y")) * BLOCK
    piece = (jnp.sum(pieces, axis=0) * (1.0 / math.sqrt(token_total))).astype(jnp.bfloat16)
    weight_grad = whole_shard(piece)
    two, across, three = to_earlier(key_parts, even)
    key_grad = key_parts[SPAN] + two.astype(jnp.float32)
    key_grad = key_grad + jnp.where(even, across, three).astype(jnp.float32)
    return (key_grad.astype(jnp.bfloat16)[None], weight_grad)


def solution(mesh):
    mesh = Mesh(mesh.devices.reshape(4, 8, 2, 8), ("x", "z", "c", "y"))
    tokens = P("y", DP, None)
    return jax.shard_map(
        per_device,
        mesh=mesh,
        in_specs=(tokens, tokens, tokens, tokens, P("y", None), P("y", DP)),
        out_specs=(tokens, P("y", None)),
        check_vma=False,
    )
```

```python
import math

import jax
import jax.numpy as jnp
from jax import lax
from jax.experimental import pallas as pl
from jax.experimental.pallas import tpu as pltpu
from jax.sharding import Mesh, PartitionSpec as P

KEY_HEADS = 4
GROUP_WIDTH = 8
HEAD_SIZE = 128
SPAN = 3
BLOCK = 128
PAIR = 2 * HEAD_SIZE
GROUP_COLUMNS = GROUP_WIDTH * HEAD_SIZE
SPAN_ROWS = (SPAN + 1) * BLOCK

DP = ("x", "z", "c")
OTHER_CORE = [(0, 1), (1, 0)]
QUARTER = 1024
SHARD = 512
HALF = 256
masked_value = -1e30
NT = (((1,), (1,)), ((), ()))


def shift(block, distance, parities=(0, 1)):
    devices = range(lax.axis_size(DP))
    route = [(i, i + distance) for i in devices if i + distance in devices and i % 2 in parities]
    return lax.ppermute(block, DP, route)


def swap(block):
    return lax.ppermute(block, "c", OTHER_CORE)


def from_earlier(block):
    two = shift(block, 2)
    three = shift(block, 3, (1,))
    one = shift(block, 1, (0,))
    return one, two, three, swap(two)


def to_earlier(parts, even):
    third, second, first, _ = parts
    from_three = shift(third, -3, (0,))
    across = swap(first)
    across_third = shift(third, -1, (1,))
    joined = second.astype(jnp.float32) + jnp.where(even, across_third, across).astype(jnp.float32)
    from_two = shift(joined.astype(jnp.bfloat16), -2)
    return from_two, across, from_three


def span_rows(core_ref, own_ref, one_ref, two_ref, three_ref, swapped_ref):
    even = core_ref[0] == 0
    third = jnp.where(even, three_ref[...], swapped_ref[...])
    first = jnp.where(even, swapped_ref[...], one_ref[...])
    return jnp.concatenate([third, two_ref[...], first, own_ref[...]], axis=0)


def stacked(ref, pair):
    first = ref[:, pair * PAIR : pair * PAIR + HEAD_SIZE]
    second = ref[:, pair * PAIR + HEAD_SIZE : (pair + 1) * PAIR]
    return jnp.concatenate([first, second], axis=0)


def weights_kernel(core_ref, position_ref, query_ref, grad_ref, *refs):
    keys_down = lax.broadcasted_iota(jnp.int32, (SPAN_ROWS, BLOCK), 0)
    queries_across = lax.broadcasted_iota(jnp.int32, (SPAN_ROWS, BLOCK), 1)
    offset = SPAN * BLOCK + queries_across - keys_down
    allowed = (offset >= 0) & (offset <= position_ref[...])
    mask = jnp.where(allowed, 0.0, masked_value).astype(jnp.bfloat16)
    key_refs, weights_ref, out_refs = refs[:5], refs[5], refs[6:]
    keys = jnp.concatenate([span_rows(core_ref, *key_refs), mask], axis=1)
    unit = (
        lax.broadcasted_iota(jnp.int32, (PAIR, BLOCK), 0) % BLOCK
        == lax.broadcasted_iota(jnp.int32, (PAIR, BLOCK), 1)
    )
    unit = jnp.where(unit, 1.0, 0.0).astype(jnp.bfloat16)
    score_scale = math.log2(math.e) / math.sqrt(HEAD_SIZE)
    total = jnp.zeros((SPAN_ROWS, HEAD_SIZE), jnp.float32)
    heads = jnp.concatenate([stacked(query_ref, pair) for pair in range(GROUP_WIDTH // 2)], axis=0)
    heads = jnp.concatenate([heads, jnp.concatenate([unit] * (GROUP_WIDTH // 2), axis=0)], axis=1)
    scores = lax.dot_general(keys, heads, NT, preferred_element_type=jnp.float32)
    top = jnp.max(scores, axis=0, keepdims=True)
    weights = jnp.exp2((scores - top) * score_scale)
    weights = weights * (1.0 / jnp.sum(weights, axis=0, keepdims=True))
    low = weights.astype(jnp.bfloat16)
    weights_ref[0] = low
    grads = jnp.concatenate([stacked(grad_ref, pair) for pair in range(GROUP_WIDTH // 2)], axis=0)
    total = jnp.dot(low, grads, preferred_element_type=jnp.float32)
    for block, out_ref in enumerate(out_refs):
        out_ref[...] = total[block * BLOCK : (block + 1) * BLOCK].astype(out_ref.dtype)


def scores_kernel(core_ref, weights_ref, query_ref, grad_ref, *refs):
    value_refs, out_refs = refs[:5], refs[5:]
    values = span_rows(core_ref, *value_refs)
    total = jnp.zeros((SPAN_ROWS, HEAD_SIZE), jnp.float32)
    pairs = range(GROUP_WIDTH // 2)
    grads = jnp.concatenate([stacked(grad_ref, pair) for pair in pairs], axis=0)
    prob_grad = lax.dot_general(values, grads, NT, preferred_element_type=jnp.float32)
    weights = weights_ref[0].astype(jnp.float32)
    row_delta = jnp.sum(weights * prob_grad, axis=0, keepdims=True)
    low = (weights * (prob_grad - row_delta)).astype(jnp.bfloat16)
    queries = jnp.concatenate([stacked(query_ref, pair) for pair in pairs], axis=0)
    total = jnp.dot(low, queries, preferred_element_type=jnp.float32)
    total = total * (1.0 / math.sqrt(HEAD_SIZE))
    for block, out_ref in enumerate(out_refs):
        out_ref[...] = total[block * BLOCK : (block + 1) * BLOCK].astype(out_ref.dtype)


in_smem = pl.BlockSpec(memory_space=pltpu.SMEM)
in_vmem = pl.BlockSpec(memory_space=pltpu.VMEM)
wide = pl.BlockSpec((BLOCK, GROUP_COLUMNS), lambda g: (0, g))
narrow = pl.BlockSpec((BLOCK, HEAD_SIZE), lambda g: (0, g))
held = pl.BlockSpec((1, SPAN_ROWS, GROUP_COLUMNS), lambda g: (g, 0, 0))
gradients = [
    jax.ShapeDtypeStruct((BLOCK, KEY_HEADS * HEAD_SIZE), kind)
    for kind in (jnp.bfloat16, jnp.bfloat16, jnp.bfloat16, jnp.float32)
]
KERNEL_FLOPS = 2 * 2 * SPAN_ROWS * BLOCK * KEY_HEADS * GROUP_COLUMNS
params = pltpu.CompilerParams(vmem_limit_bytes=16 * 1024 * 1024)


def in_hbm(array):
    return pltpu.with_memory_space_constraint(array, pltpu.HBM)


def attention_weights(core, position, queries, grads, keys):
    return pl.pallas_call(
        weights_kernel,
        grid=(KEY_HEADS,),
        in_specs=[in_smem, pl.BlockSpec((1, BLOCK), lambda g: (0, 0)), wide, wide] + [narrow] * 5,
        out_specs=[held] + [narrow] * 4,
        out_shape=[pltpu.HBM((KEY_HEADS, SPAN_ROWS, GROUP_COLUMNS), jnp.bfloat16)] + gradients,
        compiler_params=params,
        cost_estimate=pl.CostEstimate(
            flops=2 * KERNEL_FLOPS, bytes_accessed=8 << 20, transcendentals=SPAN_ROWS * BLOCK * 32
        ),
        name="attention_weights",
    )(core, position, in_hbm(queries), in_hbm(grads), *keys)


def key_gradient(core, weights, queries, grads, values):
    return pl.pallas_call(
        scores_kernel,
        grid=(KEY_HEADS,),
        in_specs=[in_smem, held, wide, wide] + [narrow] * 5,
        out_specs=[narrow] * 4,
        out_shape=gradients,
        compiler_params=params,
        cost_estimate=pl.CostEstimate(
            flops=2 * KERNEL_FLOPS, bytes_accessed=8 << 20, transcendentals=0
        ),
        name="key_gradient",
    )(core, in_hbm(weights), in_hbm(queries), in_hbm(grads), *values)


def quarters_kernel(rows_ref, out_ref):
    for x in range(4):
        for shard in range(8):
            start = shard * SHARD + x * BLOCK
            out_ref[x * BLOCK : (x + 1) * BLOCK, shard * BLOCK : (shard + 1) * BLOCK] = rows_ref[
                :, start : start + BLOCK
            ]


def partial_values_kernel(core_ref, near_ref, far_ref, weight_ref, out_ref):
    for rows_ref, core in ((near_ref, core_ref[0]), (far_ref, 1 - core_ref[0])):
        values = jnp.dot(rows_ref[...], weight_ref[...], preferred_element_type=jnp.float32)
        values = values.astype(jnp.bfloat16)
        for x in range(4):
            rows = pl.ds(pl.multiple_of((2 * x + core) * BLOCK, BLOCK), BLOCK)
            out_ref[rows, :] = values[x * BLOCK : (x + 1) * BLOCK]


def pack_kernel(core_ref, own_ref, two_ref, across_ref, three_ref, out_ref):
    last = jnp.where(core_ref[0] == 0, across_ref[...], three_ref[...])
    total = own_ref[...] + two_ref[...].astype(jnp.float32) + last.astype(jnp.float32)
    low = total.astype(jnp.bfloat16)
    for device in range(8):
        core = device % 2
        rows = slice(device * BLOCK, (device + 1) * BLOCK)
        out_ref[rows, :] = low[:, core * HALF : (core + 1) * HALF]


def product_kernel(core_ref, near_ref, far_ref, grads_ref, out_ref):
    total = None
    for rows_ref, core in ((near_ref, core_ref[0]), (far_ref, 1 - core_ref[0])):
        grads = [
            grads_ref[pl.ds(pl.multiple_of((2 * x + core) * BLOCK, BLOCK), BLOCK), :]
            for x in range(4)
        ]
        part = lax.dot_general(
            jnp.concatenate(grads, axis=0),
            rows_ref[...],
            (((0,), (0,)), ((), ())),
            preferred_element_type=jnp.float32,
        )
        total = part if total is None else total + part
    out_ref[...] = total.T.astype(jnp.bfloat16)


def exchange_rows(rows):
    quarters = pl.pallas_call(
        quarters_kernel,
        in_specs=[in_vmem],
        out_specs=in_vmem,
        out_shape=jax.ShapeDtypeStruct((4 * BLOCK, QUARTER), jnp.bfloat16),
        compiler_params=params,
        name="quarters",
    )(rows)
    return lax.all_to_all(quarters, "x", 0, 0, tiled=True)


def projection_part(w_value):
    start = (lax.axis_index("x") * BLOCK, lax.axis_index("c") * HALF)
    piece = lax.dynamic_slice(w_value, start, (BLOCK, HALF))
    return jnp.broadcast_to(piece[None], (8, BLOCK, HALF)).reshape(8 * BLOCK, HALF)


def partial_values(core, near, far, weight):
    return pl.pallas_call(
        partial_values_kernel,
        in_specs=[in_smem, in_vmem, in_vmem, in_vmem],
        out_specs=in_vmem,
        out_shape=jax.ShapeDtypeStruct((8 * BLOCK, HALF), jnp.bfloat16),
        compiler_params=params,
        name="partial_values",
    )(core, near, far, weight)


def exchange_value_grad(core, own, received):
    packed = pl.pallas_call(
        pack_kernel,
        in_specs=[in_smem] + [in_vmem] * 4,
        out_specs=in_vmem,
        out_shape=jax.ShapeDtypeStruct((8 * BLOCK, HALF), jnp.bfloat16),
        compiler_params=params,
        name="pack",
    )(core, own, *received)
    return lax.all_to_all(packed, ("x", "c"), 0, 0, tiled=True)


def exchange_values(values):
    parts = lax.all_to_all(values, ("x", "c"), 0, 0, tiled=True)
    parts = parts.reshape(4, 2, BLOCK, HALF).astype(jnp.float32)
    values = jnp.sum(parts, axis=0).astype(jnp.bfloat16)
    return jnp.concatenate([values[0], values[1]], axis=1)


def group_product(core, near, far, value_grads):
    rows = pl.BlockSpec((4 * BLOCK, HALF), lambda part: (0, part))
    return pl.pallas_call(
        product_kernel,
        grid=(QUARTER // HALF,),
        in_specs=[in_smem, rows, rows, pl.BlockSpec((8 * BLOCK, HALF), lambda part: (0, 0))],
        out_specs=pl.BlockSpec((HALF, HALF), lambda part: (part, 0)),
        out_shape=jax.ShapeDtypeStruct((QUARTER, HALF), jnp.bfloat16),
        compiler_params=params,
        name="group_product",
    )(core, near, far, value_grads)


def whole_shard(piece):
    rows, columns = piece.shape
    copies = jnp.broadcast_to(piece[None], (32, rows, columns)).reshape(32 * rows, columns)
    half = lax.all_to_all(copies, ("x", "z"), 0, 0, tiled=True)
    other = swap(half)
    first = lax.axis_index("c") == 0
    return jnp.concatenate(
        [jnp.where(first, half, other), jnp.where(first, other, half)], axis=1
    )


def per_device(queries, key_rows, out_grad, inputs, w_value, doc_pos):
    queries, keys, grads, rows = queries[0], key_rows[0], out_grad[0], inputs[0]
    core = lax.axis_index("c").astype(jnp.int32).reshape(1)
    even = core[0] == 0
    key_blocks = from_earlier(keys)
    near = exchange_rows(rows)
    near, piece, key_blocks = lax.optimization_barrier((near, projection_part(w_value), key_blocks))
    part = lax.all_to_all(piece, "y", 0, 0, tiled=True)
    weights, *value_parts = attention_weights(core, doc_pos, queries, grads, (keys,) + key_blocks)

    two, across, three = to_earlier(value_parts, even)
    part, across = lax.optimization_barrier((part, across))
    far = swap(near)
    values = exchange_values(partial_values(core, near, far, part))
    values, two, across, three = lax.optimization_barrier((values, two, across, three))
    value_grads = exchange_value_grad(core, value_parts[SPAN], (two, across, three))
    value_blocks = from_earlier(values)
    value_grads, value_blocks = lax.optimization_barrier((value_grads, value_blocks))
    product = group_product(core, near, far, value_grads)
    pieces = lax.all_to_all(product, ("y", "z"), 0, 0, tiled=True)

    key_parts = key_gradient(core, weights, queries, grads, (values,) + value_blocks)
    two, across, three = to_earlier(key_parts, even)
    pieces, two, across, three = lax.optimization_barrier((pieces, two, across, three))

    pieces = pieces.reshape(64, -1, HALF).astype(jnp.float32)
    token_total = lax.axis_size(("x", "z", "c", "y")) * BLOCK
    piece = (jnp.sum(pieces, axis=0) * (1.0 / math.sqrt(token_total))).astype(jnp.bfloat16)
    weight_grad = whole_shard(piece)
    key_grad = key_parts[SPAN] + two.astype(jnp.float32)
    key_grad = key_grad + jnp.where(even, across, three).astype(jnp.float32)
    return (key_grad.astype(jnp.bfloat16)[None], weight_grad)


def solution(mesh):
    mesh = Mesh(mesh.devices.reshape(4, 8, 2, 8), ("x", "z", "c", "y"))
    tokens = P("y", DP, None)
    return jax.shard_map(
        per_device,
        mesh=mesh,
        in_specs=(tokens, tokens, tokens, tokens, P("y", None), P("y", DP)),
        out_specs=(tokens, P("y", None)),
        check_vma=False,
    )
```

```python
import math

import jax
import jax.numpy as jnp
from jax import lax
from jax.experimental import pallas as pl
from jax.experimental.pallas import tpu as pltpu
from jax.sharding import Mesh, PartitionSpec as P

KEY_HEADS = 4
GROUP_WIDTH = 8
HEAD_SIZE = 128
SPAN = 3
BLOCK = 128
PAIR = 2 * HEAD_SIZE
GROUP_COLUMNS = GROUP_WIDTH * HEAD_SIZE
SPAN_ROWS = (SPAN + 1) * BLOCK

DP = ("x", "z", "c")
OTHER_CORE = [(0, 1), (1, 0)]
QUARTER = 1024
SHARD = 512
HALF = 256
masked_value = -1e30
NT = (((1,), (1,)), ((), ()))


def shift(block, distance, parities=(0, 1)):
    devices = range(lax.axis_size(DP))
    route = [(i, i + distance) for i in devices if i + distance in devices and i % 2 in parities]
    return lax.ppermute(block, DP, route)


def swap(block):
    return lax.ppermute(block, "c", OTHER_CORE)


def from_earlier(block):
    two = shift(block, 2)
    three = shift(block, 3, (1,))
    one = shift(block, 1, (0,))
    return one, two, three, swap(two)


def to_earlier(parts, even):
    third, second, first, _ = parts
    from_three = shift(third, -3, (0,))
    across = swap(first)
    across_third = shift(third, -1, (1,))
    joined = second.astype(jnp.float32) + jnp.where(even, across_third, across).astype(jnp.float32)
    from_two = shift(joined.astype(jnp.bfloat16), -2)
    return from_two, across, from_three


def span_rows(core_ref, own_ref, one_ref, two_ref, three_ref, swapped_ref):
    even = core_ref[0] == 0
    third = jnp.where(even, three_ref[...], swapped_ref[...])
    first = jnp.where(even, swapped_ref[...], one_ref[...])
    return jnp.concatenate([third, two_ref[...], first, own_ref[...]], axis=0)


def stacked(ref, pair):
    first = ref[:, pair * PAIR : pair * PAIR + HEAD_SIZE]
    second = ref[:, pair * PAIR + HEAD_SIZE : (pair + 1) * PAIR]
    return jnp.concatenate([first, second], axis=0)


def weights_kernel(core_ref, position_ref, query_ref, grad_ref, *refs):
    keys_down = lax.broadcasted_iota(jnp.int32, (SPAN_ROWS, BLOCK), 0)
    queries_across = lax.broadcasted_iota(jnp.int32, (SPAN_ROWS, BLOCK), 1)
    offset = SPAN * BLOCK + queries_across - keys_down
    allowed = (offset >= 0) & (offset <= position_ref[...])
    mask = jnp.where(allowed, 0.0, masked_value).astype(jnp.bfloat16)
    key_refs, weights_ref, out_refs = refs[:5], refs[5], refs[6:]
    keys = jnp.concatenate([span_rows(core_ref, *key_refs), mask], axis=1)
    unit = (
        lax.broadcasted_iota(jnp.int32, (PAIR, BLOCK), 0) % BLOCK
        == lax.broadcasted_iota(jnp.int32, (PAIR, BLOCK), 1)
    )
    unit = jnp.where(unit, 1.0, 0.0).astype(jnp.bfloat16)
    score_scale = math.log2(math.e) / math.sqrt(HEAD_SIZE)
    total = jnp.zeros((SPAN_ROWS, HEAD_SIZE), jnp.float32)
    heads = jnp.concatenate([stacked(query_ref, pair) for pair in range(GROUP_WIDTH // 2)], axis=0)
    heads = jnp.concatenate([heads, jnp.concatenate([unit] * (GROUP_WIDTH // 2), axis=0)], axis=1)
    scores = lax.dot_general(keys, heads, NT, preferred_element_type=jnp.float32)
    top = jnp.max(scores, axis=0, keepdims=True)
    weights = jnp.exp2((scores - top) * score_scale)
    weights = weights * (1.0 / jnp.sum(weights, axis=0, keepdims=True))
    low = weights.astype(jnp.bfloat16)
    weights_ref[0] = low
    grads = jnp.concatenate([stacked(grad_ref, pair) for pair in range(GROUP_WIDTH // 2)], axis=0)
    total = jnp.dot(low, grads, preferred_element_type=jnp.float32)
    for block, out_ref in enumerate(out_refs):
        out_ref[...] = total[block * BLOCK : (block + 1) * BLOCK].astype(out_ref.dtype)


def scores_kernel(core_ref, weights_ref, query_ref, grad_ref, *refs):
    value_refs, out_refs = refs[:5], refs[5:]
    values = span_rows(core_ref, *value_refs)
    total = jnp.zeros((SPAN_ROWS, HEAD_SIZE), jnp.float32)
    pairs = range(GROUP_WIDTH // 2)
    grads = jnp.concatenate([stacked(grad_ref, pair) for pair in pairs], axis=0)
    prob_grad = lax.dot_general(values, grads, NT, preferred_element_type=jnp.float32)
    weights = weights_ref[0].astype(jnp.float32)
    row_delta = jnp.sum(weights * prob_grad, axis=0, keepdims=True)
    low = (weights * (prob_grad - row_delta)).astype(jnp.bfloat16)
    queries = jnp.concatenate([stacked(query_ref, pair) for pair in pairs], axis=0)
    total = jnp.dot(low, queries, preferred_element_type=jnp.float32)
    total = total * (1.0 / math.sqrt(HEAD_SIZE))
    for block, out_ref in enumerate(out_refs):
        out_ref[...] = total[block * BLOCK : (block + 1) * BLOCK].astype(out_ref.dtype)


in_smem = pl.BlockSpec(memory_space=pltpu.SMEM)
in_vmem = pl.BlockSpec(memory_space=pltpu.VMEM)
wide = pl.BlockSpec((BLOCK, GROUP_COLUMNS), lambda g: (0, g))
narrow = pl.BlockSpec((BLOCK, HEAD_SIZE), lambda g: (0, g))
held = pl.BlockSpec((1, SPAN_ROWS, GROUP_COLUMNS), lambda g: (g, 0, 0))
gradients = [
    jax.ShapeDtypeStruct((BLOCK, KEY_HEADS * HEAD_SIZE), kind)
    for kind in (jnp.bfloat16, jnp.bfloat16, jnp.bfloat16, jnp.float32)
]
KERNEL_FLOPS = 2 * 2 * SPAN_ROWS * BLOCK * KEY_HEADS * GROUP_COLUMNS
params = pltpu.CompilerParams(vmem_limit_bytes=16 * 1024 * 1024)


def in_hbm(array):
    return pltpu.with_memory_space_constraint(array, pltpu.HBM)


def attention_weights(core, position, queries, grads, keys):
    return pl.pallas_call(
        weights_kernel,
        grid=(KEY_HEADS,),
        in_specs=[in_smem, pl.BlockSpec((1, BLOCK), lambda g: (0, 0)), wide, wide] + [narrow] * 5,
        out_specs=[held] + [narrow] * 4,
        out_shape=[pltpu.HBM((KEY_HEADS, SPAN_ROWS, GROUP_COLUMNS), jnp.bfloat16)] + gradients,
        compiler_params=params,
        cost_estimate=pl.CostEstimate(
            flops=2 * KERNEL_FLOPS, bytes_accessed=8 << 20, transcendentals=SPAN_ROWS * BLOCK * 32
        ),
        name="attention_weights",
    )(core, position, in_hbm(queries), in_hbm(grads), *keys)


def key_gradient(core, weights, queries, grads, values):
    return pl.pallas_call(
        scores_kernel,
        grid=(KEY_HEADS,),
        in_specs=[in_smem, held, wide, wide] + [narrow] * 5,
        out_specs=[narrow] * 4,
        out_shape=gradients,
        compiler_params=params,
        cost_estimate=pl.CostEstimate(
            flops=2 * KERNEL_FLOPS, bytes_accessed=8 << 20, transcendentals=0
        ),
        name="key_gradient",
    )(core, in_hbm(weights), in_hbm(queries), in_hbm(grads), *values)


def quarters_kernel(rows_ref, out_ref):
    for x in range(4):
        for shard in range(8):
            start = shard * SHARD + x * BLOCK
            out_ref[x * BLOCK : (x + 1) * BLOCK, shard * BLOCK : (shard + 1) * BLOCK] = rows_ref[
                :, start : start + BLOCK
            ]


def partial_values_kernel(core_ref, near_ref, far_ref, weight_ref, out_ref):
    for rows_ref, core in ((near_ref, core_ref[0]), (far_ref, 1 - core_ref[0])):
        values = jnp.dot(rows_ref[...], weight_ref[...], preferred_element_type=jnp.float32)
        values = values.astype(jnp.bfloat16)
        for x in range(4):
            rows = pl.ds(pl.multiple_of((2 * x + core) * BLOCK, BLOCK), BLOCK)
            out_ref[rows, :] = values[x * BLOCK : (x + 1) * BLOCK]


def pack_kernel(core_ref, own_ref, two_ref, across_ref, three_ref, values_ref, out_ref):
    last = jnp.where(core_ref[0] == 0, across_ref[...], three_ref[...])
    total = own_ref[...] + two_ref[...].astype(jnp.float32) + last.astype(jnp.float32)
    low = total.astype(jnp.bfloat16)
    for device in range(8):
        core = device % 2
        rows = slice(device * BLOCK, (device + 1) * BLOCK)
        out_ref[rows, :HALF] = low[:, core * HALF : (core + 1) * HALF]
        out_ref[rows, HALF:] = values_ref[rows, :]


def product_kernel(core_ref, near_ref, far_ref, grads_ref, out_ref):
    total = None
    for rows_ref, core in ((near_ref, core_ref[0]), (far_ref, 1 - core_ref[0])):
        grads = [
            grads_ref[pl.ds(pl.multiple_of((2 * x + core) * BLOCK, BLOCK), BLOCK), :HALF]
            for x in range(4)
        ]
        part = lax.dot_general(
            jnp.concatenate(grads, axis=0),
            rows_ref[...],
            (((0,), (0,)), ((), ())),
            preferred_element_type=jnp.float32,
        )
        total = part if total is None else total + part
    out_ref[...] = total.T.astype(jnp.bfloat16)


def exchange_rows(rows):
    quarters = pl.pallas_call(
        quarters_kernel,
        in_specs=[in_vmem],
        out_specs=in_vmem,
        out_shape=jax.ShapeDtypeStruct((4 * BLOCK, QUARTER), jnp.bfloat16),
        compiler_params=params,
        name="quarters",
    )(rows)
    return lax.all_to_all(quarters, "x", 0, 0, tiled=True)


def projection_part(w_value):
    start = (lax.axis_index("x") * BLOCK, lax.axis_index("c") * HALF)
    piece = lax.dynamic_slice(w_value, start, (BLOCK, HALF))
    return jnp.broadcast_to(piece[None], (8, BLOCK, HALF)).reshape(8 * BLOCK, HALF)


def partial_values(core, near, far, weight):
    return pl.pallas_call(
        partial_values_kernel,
        in_specs=[in_smem, in_vmem, in_vmem, in_vmem],
        out_specs=in_vmem,
        out_shape=jax.ShapeDtypeStruct((8 * BLOCK, HALF), jnp.bfloat16),
        compiler_params=params,
        name="partial_values",
    )(core, near, far, weight)


def exchange_packed(core, own, received, values):
    packed = pl.pallas_call(
        pack_kernel,
        in_specs=[in_smem] + [in_vmem] * 5,
        out_specs=in_vmem,
        out_shape=jax.ShapeDtypeStruct((8 * BLOCK, 2 * HALF), jnp.bfloat16),
        compiler_params=params,
        name="pack",
    )(core, own, *received, values)
    return lax.all_to_all(packed, ("x", "c"), 0, 0, tiled=True)


def group_product(core, near, far, packed):
    rows = pl.BlockSpec((4 * BLOCK, HALF), lambda part: (0, part))
    return pl.pallas_call(
        product_kernel,
        grid=(QUARTER // HALF,),
        in_specs=[in_smem, rows, rows, pl.BlockSpec((8 * BLOCK, 2 * HALF), lambda part: (0, 0))],
        out_specs=pl.BlockSpec((HALF, HALF), lambda part: (part, 0)),
        out_shape=jax.ShapeDtypeStruct((QUARTER, HALF), jnp.bfloat16),
        compiler_params=params,
        name="group_product",
    )(core, near, far, packed)


def whole_shard(piece):
    rows, columns = piece.shape
    copies = jnp.broadcast_to(piece[None], (32, rows, columns)).reshape(32 * rows, columns)
    half = lax.all_to_all(copies, ("x", "z"), 0, 0, tiled=True)
    other = swap(half)
    first = lax.axis_index("c") == 0
    return jnp.concatenate(
        [jnp.where(first, half, other), jnp.where(first, other, half)], axis=1
    )


def per_device(queries, key_rows, out_grad, inputs, w_value, doc_pos):
    queries, keys, grads, rows = queries[0], key_rows[0], out_grad[0], inputs[0]
    core = lax.axis_index("c").astype(jnp.int32).reshape(1)
    even = core[0] == 0
    key_blocks = from_earlier(keys)
    near = exchange_rows(rows)
    near, piece, key_blocks = lax.optimization_barrier((near, projection_part(w_value), key_blocks))
    part = lax.all_to_all(piece, "y", 0, 0, tiled=True)
    weights, *value_parts = attention_weights(core, doc_pos, queries, grads, (keys,) + key_blocks)

    two, across, three = to_earlier(value_parts, even)
    near, part, across = lax.optimization_barrier((near, part, across))
    far = swap(near)
    values = partial_values(core, near, far, part)
    packed = exchange_packed(core, value_parts[SPAN], (two, across, three), values)
    product = group_product(core, near, far, packed)
    pieces = lax.all_to_all(product, ("y", "z"), 0, 0, tiled=True)

    parts = packed.reshape(4, 2, BLOCK, 2 * HALF)[..., HALF:].astype(jnp.float32)
    values = jnp.sum(parts, axis=0).astype(jnp.bfloat16)
    values = jnp.concatenate([values[0], values[1]], axis=1)
    value_blocks = from_earlier(values)
    pieces, value_blocks = lax.optimization_barrier((pieces, value_blocks))
    key_parts = key_gradient(core, weights, queries, grads, (values,) + value_blocks)

    pieces = pieces.reshape(64, -1, HALF).astype(jnp.float32)
    token_total = lax.axis_size(("x", "z", "c", "y")) * BLOCK
    piece = (jnp.sum(pieces, axis=0) * (1.0 / math.sqrt(token_total))).astype(jnp.bfloat16)
    weight_grad = whole_shard(piece)
    two, across, three = to_earlier(key_parts, even)
    key_grad = key_parts[SPAN] + two.astype(jnp.float32)
    key_grad = key_grad + jnp.where(even, across, three).astype(jnp.float32)
    return (key_grad.astype(jnp.bfloat16)[None], weight_grad)


def solution(mesh):
    mesh = Mesh(mesh.devices.reshape(4, 8, 2, 8), ("x", "z", "c", "y"))
    tokens = P("y", DP, None)
    return jax.shard_map(
        per_device,
        mesh=mesh,
        in_specs=(tokens, tokens, tokens, tokens, P("y", None), P("y", DP)),
        out_specs=(tokens, P("y", None)),
        check_vma=False,
    )
```

```python
import math

import jax
import jax.numpy as jnp
from jax import lax
from jax.experimental import pallas as pl
from jax.experimental.pallas import tpu as pltpu
from jax.sharding import Mesh, PartitionSpec as P

KEY_HEADS = 4
GROUP_WIDTH = 8
HEAD_SIZE = 128
SPAN = 3
BLOCK = 128
PAIR = 2 * HEAD_SIZE
GROUP_COLUMNS = GROUP_WIDTH * HEAD_SIZE
SPAN_ROWS = (SPAN + 1) * BLOCK

DP = ("x", "z", "c")
OTHER_CORE = [(0, 1), (1, 0)]
QUARTER = 1024
SHARD = 512
HALF = 256
masked_value = -1e30
NT = (((1,), (1,)), ((), ()))


def shift(block, distance, parities=(0, 1)):
    devices = range(lax.axis_size(DP))
    route = [(i, i + distance) for i in devices if i + distance in devices and i % 2 in parities]
    return lax.ppermute(block, DP, route)


def swap(block):
    return lax.ppermute(block, "c", OTHER_CORE)


def from_earlier(block):
    two = shift(block, 2)
    three = shift(block, 3, (1,))
    one = shift(block, 1, (0,))
    return one, two, three, swap(two)


def to_earlier(parts, even):
    third, second, first, _ = parts
    from_three = shift(third, -3, (0,))
    across = swap(first)
    across_third = shift(third, -1, (1,))
    joined = second.astype(jnp.float32) + jnp.where(even, across_third, across).astype(jnp.float32)
    from_two = shift(joined.astype(jnp.bfloat16), -2)
    return from_two, across, from_three


def span_rows(core_ref, own_ref, one_ref, two_ref, three_ref, swapped_ref):
    even = core_ref[0] == 0
    third = jnp.where(even, three_ref[...], swapped_ref[...])
    first = jnp.where(even, swapped_ref[...], one_ref[...])
    return jnp.concatenate([third, two_ref[...], first, own_ref[...]], axis=0)


def stacked(ref, pair):
    first = ref[:, pair * PAIR : pair * PAIR + HEAD_SIZE]
    second = ref[:, pair * PAIR + HEAD_SIZE : (pair + 1) * PAIR]
    return jnp.concatenate([first, second], axis=0)


def weights_kernel(core_ref, position_ref, query_ref, grad_ref, *refs):
    keys_down = lax.broadcasted_iota(jnp.int32, (SPAN_ROWS, BLOCK), 0)
    queries_across = lax.broadcasted_iota(jnp.int32, (SPAN_ROWS, BLOCK), 1)
    offset = SPAN * BLOCK + queries_across - keys_down
    allowed = (offset >= 0) & (offset <= position_ref[...])
    mask = jnp.where(allowed, 0.0, masked_value).astype(jnp.bfloat16)
    key_refs, weights_ref, out_refs = refs[:5], refs[5], refs[6:]
    keys = jnp.concatenate([span_rows(core_ref, *key_refs), mask], axis=1)
    unit = (
        lax.broadcasted_iota(jnp.int32, (PAIR, BLOCK), 0) % BLOCK
        == lax.broadcasted_iota(jnp.int32, (PAIR, BLOCK), 1)
    )
    unit = jnp.where(unit, 1.0, 0.0).astype(jnp.bfloat16)
    score_scale = math.log2(math.e) / math.sqrt(HEAD_SIZE)
    total = jnp.zeros((SPAN_ROWS, HEAD_SIZE), jnp.float32)
    heads = jnp.concatenate([stacked(query_ref, pair) for pair in range(GROUP_WIDTH // 2)], axis=0)
    heads = jnp.concatenate([heads, jnp.concatenate([unit] * (GROUP_WIDTH // 2), axis=0)], axis=1)
    scores = lax.dot_general(keys, heads, NT, preferred_element_type=jnp.float32)
    top = jnp.max(scores, axis=0, keepdims=True)
    weights = jnp.exp2((scores - top) * score_scale)
    weights = weights * (1.0 / jnp.sum(weights, axis=0, keepdims=True))
    low = weights.astype(jnp.bfloat16)
    weights_ref[0] = low
    grads = jnp.concatenate([stacked(grad_ref, pair) for pair in range(GROUP_WIDTH // 2)], axis=0)
    total = jnp.dot(low, grads, preferred_element_type=jnp.float32)
    for block, out_ref in enumerate(out_refs):
        out_ref[...] = total[block * BLOCK : (block + 1) * BLOCK].astype(out_ref.dtype)


def scores_kernel(core_ref, weights_ref, query_ref, grad_ref, *refs):
    value_refs, out_refs = refs[:5], refs[5:]
    values = span_rows(core_ref, *value_refs)
    total = jnp.zeros((SPAN_ROWS, HEAD_SIZE), jnp.float32)
    pairs = range(GROUP_WIDTH // 2)
    grads = jnp.concatenate([stacked(grad_ref, pair) for pair in pairs], axis=0)
    prob_grad = lax.dot_general(values, grads, NT, preferred_element_type=jnp.float32)
    weights = weights_ref[0].astype(jnp.float32)
    row_delta = jnp.sum(weights * prob_grad, axis=0, keepdims=True)
    low = (weights * (prob_grad - row_delta)).astype(jnp.bfloat16)
    queries = jnp.concatenate([stacked(query_ref, pair) for pair in pairs], axis=0)
    total = jnp.dot(low, queries, preferred_element_type=jnp.float32)
    total = total * (1.0 / math.sqrt(HEAD_SIZE))
    for block, out_ref in enumerate(out_refs):
        out_ref[...] = total[block * BLOCK : (block + 1) * BLOCK].astype(out_ref.dtype)


in_smem = pl.BlockSpec(memory_space=pltpu.SMEM)
in_vmem = pl.BlockSpec(memory_space=pltpu.VMEM)
wide = pl.BlockSpec((BLOCK, GROUP_COLUMNS), lambda g: (0, g))
narrow = pl.BlockSpec((BLOCK, HEAD_SIZE), lambda g: (0, g))
held = pl.BlockSpec((1, SPAN_ROWS, GROUP_COLUMNS), lambda g: (g, 0, 0))
gradients = [
    jax.ShapeDtypeStruct((BLOCK, KEY_HEADS * HEAD_SIZE), kind)
    for kind in (jnp.bfloat16, jnp.bfloat16, jnp.bfloat16, jnp.float32)
]
KERNEL_FLOPS = 2 * 2 * SPAN_ROWS * BLOCK * KEY_HEADS * GROUP_COLUMNS
params = pltpu.CompilerParams(vmem_limit_bytes=16 * 1024 * 1024)


def in_hbm(array):
    return pltpu.with_memory_space_constraint(array, pltpu.HBM)


def attention_weights(core, position, queries, grads, keys):
    return pl.pallas_call(
        weights_kernel,
        grid=(KEY_HEADS,),
        in_specs=[in_smem, pl.BlockSpec((1, BLOCK), lambda g: (0, 0)), wide, wide] + [narrow] * 5,
        out_specs=[held] + [narrow] * 4,
        out_shape=[pltpu.HBM((KEY_HEADS, SPAN_ROWS, GROUP_COLUMNS), jnp.bfloat16)] + gradients,
        compiler_params=params,
        cost_estimate=pl.CostEstimate(
            flops=2 * KERNEL_FLOPS, bytes_accessed=8 << 20, transcendentals=SPAN_ROWS * BLOCK * 32
        ),
        name="attention_weights",
    )(core, position, in_hbm(queries), in_hbm(grads), *keys)


def key_gradient(core, weights, queries, grads, values):
    return pl.pallas_call(
        scores_kernel,
        grid=(KEY_HEADS,),
        in_specs=[in_smem, held, wide, wide] + [narrow] * 5,
        out_specs=[narrow] * 4,
        out_shape=gradients,
        compiler_params=params,
        cost_estimate=pl.CostEstimate(
            flops=2 * KERNEL_FLOPS, bytes_accessed=8 << 20, transcendentals=0
        ),
        name="key_gradient",
    )(core, in_hbm(weights), in_hbm(queries), in_hbm(grads), *values)


def quarters_kernel(rows_ref, out_ref):
    for x in range(4):
        for shard in range(8):
            start = shard * SHARD + x * BLOCK
            out_ref[x * BLOCK : (x + 1) * BLOCK, shard * BLOCK : (shard + 1) * BLOCK] = rows_ref[
                :, start : start + BLOCK
            ]


def partial_values_kernel(core_ref, near_ref, far_ref, weight_ref, out_ref):
    for rows_ref, core in ((near_ref, core_ref[0]), (far_ref, 1 - core_ref[0])):
        values = jnp.dot(rows_ref[...], weight_ref[...], preferred_element_type=jnp.float32)
        values = values.astype(jnp.bfloat16)
        for x in range(4):
            rows = pl.ds(pl.multiple_of((2 * x + core) * BLOCK, BLOCK), BLOCK)
            out_ref[rows, :] = values[x * BLOCK : (x + 1) * BLOCK]


def pack_kernel(core_ref, own_ref, two_ref, across_ref, three_ref, values_ref, out_ref):
    last = jnp.where(core_ref[0] == 0, across_ref[...], three_ref[...])
    total = own_ref[...] + two_ref[...].astype(jnp.float32) + last.astype(jnp.float32)
    low = total.astype(jnp.bfloat16)
    for device in range(8):
        core = device % 2
        rows = slice(device * BLOCK, (device + 1) * BLOCK)
        out_ref[rows, :HALF] = low[:, core * HALF : (core + 1) * HALF]
        out_ref[rows, HALF:] = values_ref[rows, :]


def product_kernel(core_ref, near_ref, far_ref, grads_ref, out_ref):
    total = None
    for rows_ref, core in ((near_ref, core_ref[0]), (far_ref, 1 - core_ref[0])):
        grads = [
            grads_ref[pl.ds(pl.multiple_of((2 * x + core) * BLOCK, BLOCK), BLOCK), :HALF]
            for x in range(4)
        ]
        part = lax.dot_general(
            jnp.concatenate(grads, axis=0),
            rows_ref[...],
            (((0,), (0,)), ((), ())),
            preferred_element_type=jnp.float32,
        )
        total = part if total is None else total + part
    out_ref[...] = total.T.astype(jnp.bfloat16)


def exchange_rows(rows):
    quarters = pl.pallas_call(
        quarters_kernel,
        in_specs=[in_vmem],
        out_specs=in_vmem,
        out_shape=jax.ShapeDtypeStruct((4 * BLOCK, QUARTER), jnp.bfloat16),
        compiler_params=params,
        name="quarters",
    )(rows)
    return lax.all_to_all(quarters, "x", 0, 0, tiled=True)


def projection_part(w_value):
    start = (lax.axis_index("x") * BLOCK, lax.axis_index("c") * HALF)
    piece = lax.dynamic_slice(w_value, start, (BLOCK, HALF))
    return jnp.broadcast_to(piece[None], (8, BLOCK, HALF)).reshape(8 * BLOCK, HALF)


def partial_values(core, near, far, weight):
    return pl.pallas_call(
        partial_values_kernel,
        in_specs=[in_smem, in_vmem, in_vmem, in_vmem],
        out_specs=in_vmem,
        out_shape=jax.ShapeDtypeStruct((8 * BLOCK, HALF), jnp.bfloat16),
        compiler_params=params,
        name="partial_values",
    )(core, near, far, weight)


def exchange_packed(core, own, received, values):
    packed = pl.pallas_call(
        pack_kernel,
        in_specs=[in_smem] + [in_vmem] * 5,
        out_specs=in_vmem,
        out_shape=jax.ShapeDtypeStruct((8 * BLOCK, 2 * HALF), jnp.bfloat16),
        compiler_params=params,
        name="pack",
    )(core, own, *received, values)
    return lax.all_to_all(packed, ("x", "c"), 0, 0, tiled=True)


def group_product(core, near, far, packed):
    rows = pl.BlockSpec((4 * BLOCK, HALF), lambda part: (0, part))
    return pl.pallas_call(
        product_kernel,
        grid=(QUARTER // HALF,),
        in_specs=[in_smem, rows, rows, pl.BlockSpec((8 * BLOCK, 2 * HALF), lambda part: (0, 0))],
        out_specs=pl.BlockSpec((HALF, HALF), lambda part: (part, 0)),
        out_shape=jax.ShapeDtypeStruct((QUARTER, HALF), jnp.bfloat16),
        compiler_params=params,
        name="group_product",
    )(core, near, far, packed)


def whole_shard(piece):
    rows, columns = piece.shape
    copies = jnp.broadcast_to(piece[None], (32, rows, columns)).reshape(32 * rows, columns)
    half = lax.all_to_all(copies, ("x", "z"), 0, 0, tiled=True)
    other = swap(half)
    first = lax.axis_index("c") == 0
    return jnp.concatenate(
        [jnp.where(first, half, other), jnp.where(first, other, half)], axis=1
    )


def per_device(queries, key_rows, out_grad, inputs, w_value, doc_pos):
    queries, keys, grads, rows = queries[0], key_rows[0], out_grad[0], inputs[0]
    core = lax.axis_index("c").astype(jnp.int32).reshape(1)
    even = core[0] == 0
    key_blocks = from_earlier(keys)
    near = exchange_rows(rows)
    near, piece, key_blocks = lax.optimization_barrier((near, projection_part(w_value), key_blocks))
    part = lax.all_to_all(piece, "y", 0, 0, tiled=True)
    weights, *value_parts = attention_weights(core, doc_pos, queries, grads, (keys,) + key_blocks)

    received = to_earlier(value_parts, even)
    far = swap(near)
    values = partial_values(core, near, far, part)
    packed = exchange_packed(core, value_parts[SPAN], received, values)
    product = group_product(core, near, far, packed)
    pieces = lax.all_to_all(product, ("y", "z"), 0, 0, tiled=True)

    parts = packed.reshape(4, 2, BLOCK, 2 * HALF)[..., HALF:].astype(jnp.float32)
    values = jnp.sum(parts, axis=0).astype(jnp.bfloat16)
    values = jnp.concatenate([values[0], values[1]], axis=1)
    value_blocks = from_earlier(values)
    pieces, value_blocks = lax.optimization_barrier((pieces, value_blocks))
    key_parts = key_gradient(core, weights, queries, grads, (values,) + value_blocks)

    pieces = pieces.reshape(64, -1, HALF).astype(jnp.float32)
    token_total = lax.axis_size(("x", "z", "c", "y")) * BLOCK
    piece = (jnp.sum(pieces, axis=0) * (1.0 / math.sqrt(token_total))).astype(jnp.bfloat16)
    weight_grad = whole_shard(piece)
    two, across, three = to_earlier(key_parts, even)
    key_grad = key_parts[SPAN] + two.astype(jnp.float32)
    key_grad = key_grad + jnp.where(even, across, three).astype(jnp.float32)
    return (key_grad.astype(jnp.bfloat16)[None], weight_grad)


def solution(mesh):
    mesh = Mesh(mesh.devices.reshape(4, 8, 2, 8), ("x", "z", "c", "y"))
    tokens = P("y", DP, None)
    return jax.shard_map(
        per_device,
        mesh=mesh,
        in_specs=(tokens, tokens, tokens, tokens, P("y", None), P("y", DP)),
        out_specs=(tokens, P("y", None)),
        check_vma=False,
    )
```
